32 devices in a mesh: seq: 8 (over z, core), chan: 4 (over y, x).
Axes of the slice: x: 2, y: 2, z: 4, core: 2. Of those that a mesh axis runs over, the one named last changes fastest.
Arguments:
- layer_source: bfloat16 [8192, 4096], P('seq', 'chan'), may hold values from -6 to 6
- entering_mixer_sections: bfloat16 [2, 8192, 1024], P(None, 'chan'), may hold values from -0.125 to 0.125
- sigmoid_switch_matrix: bfloat16 [4096, 1024], P('chan'), may hold values from -0.1875 to 0.1875
- leaving_mixer_sections: bfloat16 [2, 8192, 1024], P(None, 'chan'), may hold values from -0.125 to 0.125
- channel_persistence: float32 [4096], P('chan'), may hold values from 0.96 to 1, as said below
- position_boosts: float32 [8192], P('seq'), may hold values from 0.5 to 1, as said below
- result_cotangent: bfloat16 [8192, 4096], P('seq', 'chan'), may hold values from -6 to 6
Outputs:
- layer_out: bfloat16 [8192, 4096], P('seq', 'chan')
- token_grads: bfloat16 [8192, 4096], P('seq', 'chan')
- in_grads: float32 [2, 8192, 1024], P(None, ('chan', 'seq'))
- out_grads: float32 [2, 8192, 1024], P(None, ('chan', 'seq'))
- gate_grads: float32 [4096, 1024], P(('chan', 'seq'))
The draws below stay inside these ranges and needn't reach their ends.
Inputs may be any that keep to these rules, and one draw needn't show every extreme that they name: `channel_persistence`: each entry is positive and below one. `position_boosts`: each entry is positive and at most one.
All inputs are finite; a program needn't handle non-finite values.
Results may differ from the reference program's by a relative error of at most 0.027.
Values may be sent and summed in bfloat16 or wider, within the bound.
A program may use at most 192 MiB of HBM per device.

```python
import jax
import jax.numpy as jnp
from jax import lax

D = 4096
LENGTH = 8192
BLOCK = 1024
SECTIONS = 2
N_CHAN = 4


def draw_channel_persistence(key, part):
    coin_key, slow_key, fast_key = jax.random.split(jax.random.fold_in(key, 11), 3)
    slow_share = 0.5
    slow = jax.random.uniform(coin_key, (D,), jnp.float32) < slow_share
    slow_rate = jnp.exp(jax.random.uniform(slow_key, (D,), jnp.float32, jnp.log(0.1 / LENGTH), jnp.log(2.0 / LENGTH)))
    fast_rate = jnp.exp(jax.random.uniform(fast_key, (D,), jnp.float32, jnp.log(1.0 / 512.0), jnp.log(1.0 / 30.0)))
    rates = jnp.where(slow, slow_rate, fast_rate)
    return jnp.exp(-rates).astype(jnp.float32)


def draw_position_boosts(key, part):
    place_key, depth_key = jax.random.split(jax.random.fold_in(key, 23), 2)
    hits = jax.random.uniform(place_key, (LENGTH,), jnp.float32) < 8.0 / LENGTH
    depth = jax.random.uniform(depth_key, (LENGTH,), jnp.float32, 0.5, 0.8)
    return jnp.where(hits, depth, 1.0).astype(jnp.float32)


def steps_of(stream_key, shape, shards, smallest, largest):
    level, own = 1.0, jax.random.fold_in(stream_key, 6)
    for dim, parts in shards:
        steps = jnp.exp(jax.random.uniform(jax.random.fold_in(own, dim), (parts,), jnp.float32, smallest / len(shards), largest / len(shards)))
        level = level * jnp.repeat(steps, shape[dim] // parts).reshape([-1 if axis == dim else 1 for axis in range(len(shape))])
    return level


def scatter_about(rng, extent, scale, limit, shards=(), dtype=jnp.bfloat16):
    values = scale * jax.random.normal(rng, extent, jnp.float32)
    if shards:
        values = values * steps_of(rng, extent, shards, -0.22, 0.18)
    return jnp.clip(values, -limit, limit).astype(dtype)


def setup_inputs(seed: int = 0) -> dict:
    splits = jax.random.split(jax.random.key(seed), 8)
    layer_source = scatter_about(splits[0], (LENGTH, D), 1.0, 6.0, ((0, 8), (1, 4)))
    entering_mixer_sections = scatter_about(splits[1], (SECTIONS, 2 * D, BLOCK), (2 * BLOCK) ** -0.5, 0.125, ((1, 4),))
    sigmoid_switch_matrix = scatter_about(splits[2], (D, BLOCK), BLOCK ** -0.5, 0.1875, ((0, 4),))
    leaving_mixer_sections = scatter_about(splits[3], (SECTIONS, 2 * D, BLOCK), (2 * BLOCK) ** -0.5, 0.125, ((1, 4),))
    channel_persistence = draw_channel_persistence(jax.random.fold_in(splits[7], 71), 0)
    position_boosts = draw_position_boosts(jax.random.fold_in(splits[7], 71), 0)
    result_cotangent = scatter_about(splits[6], (LENGTH, D), 1.0, 6.0, ((0, 8), (1, 4)))
    return {"layer_source": layer_source, "entering_mixer_sections": entering_mixer_sections, "sigmoid_switch_matrix": sigmoid_switch_matrix, "leaving_mixer_sections": leaving_mixer_sections, "channel_persistence": channel_persistence, "position_boosts": position_boosts, "result_cotangent": result_cotangent}


def link(earlier, following):
    return (earlier[0] * following[0], following[0] * earlier[1] + following[1])

def dot_rows(left, right):
    return lax.dot_general(left, right, (((0,), (0,)), ((), ())), preferred_element_type=jnp.float32)

def dot_trans(left, right):
    return lax.dot_general(left, right, (((1,), (1,)), ((), ())), preferred_element_type=jnp.float32)

def forward_map(blocks, weights, round_last):
    width = BLOCK
    stored = []
    for level in range(SECTIONS):
        stored.append(blocks)
        result = []
        for owner in range(N_CHAN):
            partner = owner ^ 1 << level
            local_w = weights[level, owner * 2 * width:(owner + 1) * 2 * width]
            summed = jnp.dot(blocks[owner], local_w[:width], preferred_element_type=jnp.float32)
            summed = summed + jnp.dot(blocks[partner], local_w[width:], preferred_element_type=jnp.float32)
            if round_last or level + 1 < SECTIONS:
                summed = summed.astype(jnp.bfloat16)
            result.append(summed)
        blocks = result
    return (blocks, stored)

def backward_map(cotans, weights, stored, round_last):
    width = BLOCK
    grads = [None] * SECTIONS
    for level in reversed(range(SECTIONS)):
        inputs = stored[level]
        shares = []
        for owner in range(N_CHAN):
            local_w = weights[level, owner * 2 * width:(owner + 1) * 2 * width]
            shares.append(dot_trans(cotans[owner], local_w[width:]).astype(jnp.bfloat16))
        result = []
        pieces = []
        for owner in range(N_CHAN):
            partner = owner ^ 1 << level
            local_w = weights[level, owner * 2 * width:(owner + 1) * 2 * width]
            own_grad = dot_rows(inputs[owner], cotans[owner])
            mate_grad = dot_rows(inputs[partner], cotans[owner])
            pieces.append(jnp.concatenate([own_grad, mate_grad], axis=0))
            summed = dot_trans(cotans[owner], local_w[:width]) + shares[partner].astype(jnp.float32)
            if round_last or level > 0:
                summed = summed.astype(jnp.bfloat16)
            result.append(summed)
        grads[level] = jnp.concatenate(pieces, axis=0)
        cotans = result
    return (cotans, jnp.stack(grads))

def reference(layer_source, entering_mixer_sections, sigmoid_switch_matrix, leaving_mixer_sections, channel_persistence, position_boosts, result_cotangent):
    width = BLOCK
    token_blocks = [layer_source[:, owner * width:(owner + 1) * width] for owner in range(N_CHAN)]
    grad_blocks = [result_cotangent[:, owner * width:(owner + 1) * width] for owner in range(N_CHAN)]
    drives, in_stored = forward_map(token_blocks, entering_mixer_sections, True)
    mixed_blocks = []
    saved = []
    for owner in range(N_CHAN):
        local_gate = sigmoid_switch_matrix[owner * width:(owner + 1) * width]
        gate = jax.nn.sigmoid(jnp.dot(token_blocks[owner], local_gate, preferred_element_type=jnp.float32))
        segment_shrink_multiplier = channel_persistence[owner * width:(owner + 1) * width]
        surviving_portion = segment_shrink_multiplier[None, :] * position_boosts[:, None]
        input_scale = jnp.sqrt(1.0 - segment_shrink_multiplier * segment_shrink_multiplier)
        drive = input_scale[None, :] * drives[owner].astype(jnp.float32)
        products, hidden = lax.associative_scan(link, (surviving_portion, drive))
        mixed_blocks.append((hidden * gate).astype(jnp.bfloat16))
        saved.append((gate, surviving_portion, input_scale, hidden))
    branches, out_stored = forward_map(mixed_blocks, leaving_mixer_sections, False)
    layer_out = jnp.concatenate([(token_blocks[owner].astype(jnp.float32) + branches[owner]).astype(jnp.bfloat16) for owner in range(N_CHAN)], axis=1)
    out_cots, out_sums = backward_map(grad_blocks, leaving_mixer_sections, out_stored, False)
    drive_grads = []
    gate_pres = []
    for owner in range(N_CHAN):
        gate, surviving_portion, input_scale, hidden = saved[owner]
        out_cot = out_cots[owner]
        hidden_grad = out_cot * gate
        gate_pre_grad = (out_cot * hidden * gate * (1.0 - gate)).astype(jnp.bfloat16)
        rev_prod, carried = lax.associative_scan(link, (surviving_portion, surviving_portion * hidden_grad), reverse=True)
        after = jnp.concatenate([carried[1:], jnp.zeros((1, width), jnp.float32)], axis=0)
        state_grad = hidden_grad + after
        drive_grads.append((input_scale[None, :] * state_grad).astype(jnp.bfloat16))
        gate_pres.append(gate_pre_grad)
    input_sides, in_sums = backward_map(drive_grads, entering_mixer_sections, in_stored, False)
    grad_scale = LENGTH ** (-0.5)
    token_parts = []
    gate_parts = []
    for owner in range(N_CHAN):
        local_gate = sigmoid_switch_matrix[owner * width:(owner + 1) * width]
        summed = grad_blocks[owner].astype(jnp.float32) + input_sides[owner] + dot_trans(gate_pres[owner], local_gate)
        token_parts.append(summed.astype(jnp.bfloat16))
        gate_parts.append(dot_rows(token_blocks[owner], gate_pres[owner]))
    token_grads = jnp.concatenate(token_parts, axis=1)
    gate_grads = jnp.concatenate(gate_parts, axis=0) * grad_scale
    return (layer_out, token_grads, in_sums * grad_scale, out_sums * grad_scale, gate_grads)
```

```python
import functools

import jax
import jax.numpy as jnp
from jax import lax
from jax.experimental import pallas as pl
from jax.experimental.pallas import tpu as pltpu
from jax.sharding import PartitionSpec as P

SEGMENTS = 32
LANES = 128
MESH = pl.DeviceIdType.MESH
F32, BF16 = jnp.float32, jnp.bfloat16


def from_partner(block, axis, distance):
    count = lax.axis_size(axis)
    route = []
    for low in range(count):
        high = low | 1 << distance
        if high != low and high < count:
            route += [(low, high), (high, low)]
    return lax.ppermute(block, axis, route)


def dot(left, right):
    return jnp.dot(left, right, preferred_element_type=jnp.float32)


def dot_rows(left, right):
    return lax.dot_general(
        left, right, (((0,), (0,)), ((), ())), preferred_element_type=jnp.float32
    )


def dot_trans(left, right):
    return lax.dot_general(
        left, right, (((1,), (1,)), ((), ())), preferred_element_type=jnp.float32
    )


def every(ref, step):
    return ref[pl.ds(step, SEGMENTS, stride=ref.shape[0] // SEGMENTS), :]


def ends_kernel(drive, out_cot, gate, keep, boosts, seg_ref, tot_ref, x_ref, g_ref):
    lam = keep[...]
    scale = jnp.sqrt(1.0 - lam * lam)
    x_ref[...] = scale * drive[...].astype(jnp.float32)
    g_ref[...] = out_cot[...] * gate[...]
    steps = x_ref.shape[0] // SEGMENTS
    shape = (SEGMENTS, LANES)
    lam = jnp.broadcast_to(lam, shape)
    state = jnp.zeros(shape, jnp.float32)
    prod = jnp.ones(shape, jnp.float32)
    for i in range(steps):
        a = every(boosts, i) * lam
        state = a * state + every(x_ref, i)
        prod = a * prod
    back = jnp.zeros(shape, jnp.float32)
    for i in reversed(range(steps)):
        a = every(boosts, i) * lam
        back = a * (every(g_ref, i) + back)
    seg_ref[0] = prod
    seg_ref[1] = state
    seg_ref[2] = back
    p = jnp.ones((1, LANES), jnp.float32)
    h = jnp.zeros((1, LANES), jnp.float32)
    c = jnp.zeros((1, LANES), jnp.float32)
    for s in range(SEGMENTS):
        here = prod[s : s + 1]
        h = here * h + state[s : s + 1]
        p = here * p
        r = SEGMENTS - 1 - s
        c = prod[r : r + 1] * c + back[r : r + 1]
    tot_ref[0] = p
    tot_ref[1] = h
    tot_ref[2] = c


def run_kernel(
    devices, drive, out_cot, gate, keep, boosts, seg, tots, place,
    mixed, gate_pre, drive_grad, x_ref, g_ref, start_ref, stop_ref,
):
    lam = keep[...]
    scale = jnp.sqrt(1.0 - lam * lam)
    x_ref[...] = scale * drive[...].astype(jnp.float32)
    g_ref[...] = out_cot[...] * gate[...]
    steps = x_ref.shape[0] // SEGMENTS
    shape = (SEGMENTS, LANES)
    here = place[...]
    h = jnp.zeros((1, LANES), jnp.float32)
    c = jnp.zeros((1, LANES), jnp.float32)
    for k in range(devices):
        h = jnp.where(k < here, tots[k, 0] * h + tots[k, 1], h)
        r = devices - 1 - k
        c = jnp.where(r > here, tots[r, 0] * c + tots[r, 2], c)
    for s in range(SEGMENTS):
        start_ref[s : s + 1] = h
        h = seg[0, s : s + 1] * h + seg[1, s : s + 1]
        r = SEGMENTS - 1 - s
        stop_ref[r : r + 1] = c
        c = seg[0, r : r + 1] * c + seg[2, r : r + 1]
    lam = jnp.broadcast_to(lam, shape)
    state = start_ref[...]
    back = stop_ref[...]
    for i in range(steps):
        state = every(boosts, i) * lam * state + every(x_ref, i)
        x_ref[pl.ds(i, SEGMENTS, stride=steps), :] = state
        r = steps - 1 - i
        total = every(g_ref, r) + back
        g_ref[pl.ds(r, SEGMENTS, stride=steps), :] = total
        back = every(boosts, r) * lam * total
    sig = gate[...]
    product = x_ref[...] * sig
    mixed[...] = product.astype(jnp.bfloat16)
    gate_pre[...] = (out_cot[...] * product * (1.0 - sig)).astype(jnp.bfloat16)
    drive_grad[...] = (scale * g_ref[...]).astype(jnp.bfloat16)


def recurrences(drive, out_cot, gate, keep, boosts):
    tokens, width = drive.shape
    devices = lax.axis_size("seq")
    keep = keep[None, :]
    boosts = jnp.broadcast_to(boosts[:, None], (tokens, LANES))
    big = pl.BlockSpec((tokens, LANES), lambda j: (0, j))
    row = pl.BlockSpec((1, LANES), lambda j: (0, j))
    same = pl.BlockSpec((tokens, LANES), lambda j: (0, 0))
    seg_spec = pl.BlockSpec((3, SEGMENTS, LANES), lambda j: (0, 0, j))
    scratch = pltpu.VMEM((tokens, LANES), jnp.float32)
    small = pltpu.VMEM((SEGMENTS, LANES), jnp.float32)
    area = tokens * width
    seg, totals = pl.pallas_call(
        ends_kernel,
        grid=(width // LANES,),
        in_specs=[big, big, big, row, same],
        out_specs=[seg_spec, pl.BlockSpec((3, 1, LANES), lambda j: (0, 0, j))],
        out_shape=[
            jax.ShapeDtypeStruct((3, SEGMENTS, width), jnp.float32),
            jax.ShapeDtypeStruct((3, 1, width), jnp.float32),
        ],
        scratch_shapes=[scratch, scratch],
        compiler_params=pltpu.CompilerParams(vmem_limit_bytes=24 << 20),
        cost_estimate=pl.CostEstimate(flops=10 * area, bytes_accessed=10 * area, transcendentals=0),
        name="ends",
    )(drive, out_cot, gate, keep, boosts)
    totals = lax.all_gather(totals, "seq")
    place = jnp.full((1, LANES), lax.axis_index("seq"), jnp.int32)
    return pl.pallas_call(
        functools.partial(run_kernel, devices),
        grid=(width // LANES,),
        in_specs=[
            big, big, big, row, same, seg_spec,
            pl.BlockSpec((devices, 3, 1, LANES), lambda j: (0, 0, 0, j)),
            pl.BlockSpec((1, LANES), lambda j: (0, 0)),
        ],
        out_specs=[big, big, big],
        out_shape=[jax.ShapeDtypeStruct((tokens, width), jnp.bfloat16)] * 3,
        scratch_shapes=[scratch, scratch, small, small],
        compiler_params=pltpu.CompilerParams(vmem_limit_bytes=24 << 20),
        cost_estimate=pl.CostEstimate(flops=20 * area, bytes_accessed=16 * area, transcendentals=0),
        name="recurrences",
    )(drive, out_cot, gate, keep, boosts, seg, totals, place)


SLOTS = 4
FLIGHT = 2


def after_kernel(levels, chips, scale, *refs):
    it = iter(refs)
    z = [next(it) for _ in range(levels)]
    zm = [next(it) for _ in range(levels)]
    e = [None] + [next(it) for _ in range(levels)]
    mixed, gate_pre, drive_grad, entering, leaving, switch = (next(it) for _ in range(6))
    layer_out, token_grads, in_grads, out_grads, gate_grads = (next(it) for _ in range(5))
    stage, part, sums, gate_sums, right, left, gate_right, gate_left = (next(it) for _ in range(8))
    mates, shares, outs, cots, sent, final = (next(it) for _ in range(6))
    load_sem, sib_send, sib_recv, right_send, right_recv, left_send, left_recv = (
        next(it) for _ in range(7)
    )
    swap_send, swap_recv, final_sem, store_sem = (next(it) for _ in range(4))

    tokens, width = mixed.shape
    half = width // 2
    seq, chan = lax.axis_index("seq"), lax.axis_index("chan")
    zi, core = lax.div(seq, 2), lax.rem(seq, 2)
    zo = chips - 1 - zi
    sibling = {"seq": seq + 1 - 2 * core}
    upper, lower = {"seq": seq + 2}, {"seq": seq - 2}

    def partner(level):
        d = 1 << level
        bit = lax.rem(lax.div(chan, d), 2)
        return {"chan": chan + d * (1 - 2 * bit)}

    barrier = pltpu.get_barrier_semaphore()

    def greet(device):
        pl.semaphore_signal(barrier, inc=1, device_id=device, device_id_type=MESH)

    for level in range(levels):
        greet(partner(level))
    greet(sibling)

    for device in (lax.rem(seq + 2, 2 * chips), lax.rem(seq + 2 * chips - 2, 2 * chips)):
        greet({"seq": device})
    pl.semaphore_wait(barrier, levels + 3)

    def remote(source, target, send, recv, device):
        return pltpu.make_async_remote_copy(
            src_ref=source, dst_ref=target, send_sem=send, recv_sem=recv,
            device_id=device, device_id_type=MESH,
        )

    def swap_out(step, source):
        return remote(source, mates.at[step], swap_send.at[step], swap_recv.at[step], partner(step))

    def swap_back(step):
        n = levels + step
        return remote(
            sent, shares.at[step], swap_send.at[n], swap_recv.at[n], partner(levels - 1 - step)
        )

    groups = [(gate_grads, gate_sums, gate_right, gate_left)]
    for step in range(levels):
        for out in (in_grads.at[levels - 1 - step], out_grads.at[step]):
            n = len(groups) - 1
            groups.append((out, sums.at[n], right.at[n], left.at[n]))

    def hop(g, k, h, way):
        _, total, up, down = groups[g]
        rows = up.shape[1]
        cols = pl.ds(h * half, half)
        into = (up, down)[way]
        at = (0 if way else chips - k) if k > 0 else 0
        if way:
            first = total.at[pl.ds((k - 1) * rows, rows), cols]
            send, recv, device = left_send, left_recv, lower
        else:
            first = total.at[pl.ds((chips - k) * rows, rows), cols]
            send, recv, device = right_send, right_recv, upper
        n = (g * (chips - 1) + k - 1) * 2 + h

        def copy(source):
            return remote(source, into.at[k - 1, :, cols], send.at[n], recv.at[n], device)

        later = into.at[k - 2, :, cols] if k > 1 else None
        return copy, first, later

    issued = []

    def finish_send(key):
        g, k, h = key
        for way, place in ((0, zi), (1, zo)):
            @pl.when(place <= k - 1)
            def _(way=way):
                copy, first, _ = hop(g, k, h, way)
                copy(first).wait_send()

    def send(g, k, h):
        if len(issued) >= FLIGHT:
            finish_send(issued[-FLIGHT])
        issued.append((g, k, h))
        for way, place in ((0, zi), (1, zo)):
            copy, first, later = hop(g, k, h, way)

            @pl.when(place == 0)
            def _(copy=copy, first=first):
                copy(first).start()

            if k > 1:
                @pl.when((place >= 1) & (place <= k - 1))
                def _(copy=copy, later=later):
                    copy(later).start()

    def event(g, k, h):
        out, total, up, down = groups[g]
        rows = up.shape[1]
        cols = pl.ds(h * half, half)
        for way, place in ((0, zi), (1, zo)):
            copy, first, _ = hop(g, k, h, way)

            @pl.when((place >= 1) & (place <= k))
            def _(way=way, copy=copy, first=first):
                copy(first).wait_recv()
                if k < chips - 1:
                    shard = zi - 1 + chips - k
                    if way:
                        shard = chips - 1 - (zo - 1 + chips - k)
                    at = pl.ds(pl.multiple_of(shard * rows, rows), rows)
                    into = (up, down)[way]
                    into[k - 1, :, cols] = (
                        into[k - 1, :, cols].astype(F32) + total[at, cols].astype(F32)
                    ).astype(BF16)

        if k < chips - 1:
            send(g, k + 1, h)
            return
        slot = g % 2
        if h == 0 and g >= 2:
            final_copy(g - 2).wait()
        at = pl.ds(pl.multiple_of(zi * rows, rows), rows)
        final[slot, :rows, cols] = total[at, cols].astype(F32) * scale

        @pl.when(zi > 0)
        def _():
            final[slot, :rows, cols] += up[chips - 2, :, cols].astype(F32) * scale

        @pl.when(zo > 0)
        def _():
            final[slot, :rows, cols] += down[chips - 2, :, cols].astype(F32) * scale

        if h == 1:
            final_copy(g).start()

    def final_copy(g):
        out, _, up, _ = groups[g]
        rows = up.shape[1]
        return pltpu.make_async_copy(final.at[g % 2, :rows], out, final_sem.at[g % 2])

    blocks = []

    def sibling_copy(b):
        g, offset, slot = blocks[b]
        total = groups[g][1]
        return remote(
            part.at[slot, 1 - core], total.at[pl.ds(offset, half)],
            sib_send.at[b], sib_recv.at[b], sibling,
        )

    def grad(g, offset, left_ref, right_ref):
        b = len(blocks)
        blocks.append((g, offset, b % 2))
        slot = b % 2
        if b >= 2:
            sibling_copy(b - 2).wait_send()
        rows = groups[g][2].shape[1]
        tile = min(256, width)

        @pl.loop(0, width // tile)
        def _(i):
            cols = pl.ds(pl.multiple_of(i * tile, tile), tile)
            result = dot_rows(left_ref[:, cols], right_ref[...]).astype(BF16)
            pieces = tile // rows
            if pieces <= 1:
                per = rows // tile
                shard = lax.div(i, per)
                at = lax.div(shard, 2) * rows + lax.rem(i, per) * tile
                part[slot, lax.rem(shard, 2), pl.ds(pl.multiple_of(at, tile), tile), :] = result
            else:
                for q in range(pieces):
                    at = i * (tile // 2) + q // 2 * rows
                    part[slot, q % 2, pl.ds(pl.multiple_of(at, rows), rows), :] = (
                        result[q * rows : (q + 1) * rows]
                    )

        sibling_copy(b).start()
        return b

    def chip_sum(b):
        g, offset, slot = blocks[b]
        total = groups[g][1]
        sibling_copy(b).wait_recv()
        tile = min(128, half)

        @pl.loop(0, half // tile)
        def _(i):
            at = pl.multiple_of(i * tile, tile)
            there = pl.ds(offset + at, tile)
            total[there, :] = (
                total[there, :].astype(F32) + part[slot, core, pl.ds(at, tile), :].astype(F32)
            ).astype(BF16)

    work = []
    tall = min(256, tokens)

    def tiles(store):
        @pl.loop(0, tokens // tall)
        def _(i):
            store(pl.ds(pl.multiple_of(i * tall, tall), tall))

    def task(loads, run):
        work.append((loads, run))

    def top(weights, level):
        return weights.at[level, pl.ds(0, width)]

    def bot(weights, level):
        return weights.at[level, pl.ds(width, width)]

    queue = []
    pending = []

    def settle():
        while pending:
            b, group_done = pending.pop(0)
            chip_sum(b)
            if group_done:
                g = blocks[b][0]
                for k in range(1, chips):
                    for h in range(2):
                        queue.append((g, k, h))

    started = set()

    def begin():
        for g, k, h in list(queue):
            if k == 1 and (g, h) not in started:
                ahead = queue.index((g, k, h))
                if ahead <= 1:
                    started.add((g, h))
                    send(g, 1, h)

    def pump(count):
        begin()
        for _ in range(count):
            if not queue:
                return
            event(*queue.pop(0))
            begin()

    def drain(keep):
        pump(max(len(queue) - keep, 0))

    def grad_task(g, offset, left_ref, right_ref, last):
        fixed = [r for r in (left_ref, right_ref) if isinstance(r, tuple)]
        loads = [r[0] for r in fixed]

        def run(bufs):
            bufs = list(bufs)
            lhs = bufs.pop(0) if isinstance(left_ref, tuple) else left_ref
            rhs = bufs.pop(0) if isinstance(right_ref, tuple) else right_ref
            settle()
            pending.append((grad(g, offset, lhs, rhs), last))
            pump(1)

        task(loads, run)

    def hbm(ref):
        return (ref,)

    def share_task(step):
        down = levels - 1 - step
        loads = [bot(entering, down)]
        if step == 0:
            loads = [drive_grad] + loads

        def run(bufs):
            cot = bufs[0] if step == 0 else cots.at[step - 1]
            weight = bufs[-1]
            if step > 0:
                swap_back(step - 1).wait_send()

            def store(at):
                sent[at, :] = dot_trans(cot[at, :], weight[...]).astype(BF16)

            tiles(store)
            swap_back(step).start()
            settle()
            pump(1)

        task(loads, run)

    def wait_task(fn, keep):
        def run(bufs):
            settle()
            drain(keep)
            fn()

        task([], run)

    def out_task(step):
        loads = [top(leaving, step), bot(leaving, step)]
        last = step == levels - 1
        if step == 0:
            loads.append(mixed)
        if last:
            loads.append(z[0])

        def run(bufs):
            held = bufs[2] if step == 0 else outs.at[step - 1]
            mate = mates.at[step]

            def store(at):
                total = dot(held[at, :], bufs[0][...]) + dot(mate[at, :], bufs[1][...])
                if last:
                    mates[0, at, :] = (bufs[-1][at, :].astype(F32) + total).astype(BF16)
                else:
                    outs[step, at, :] = total.astype(BF16)

            tiles(store)
            if last:
                pltpu.make_async_copy(mates.at[0], layer_out, store_sem.at[0]).start()
            else:
                swap_out(step + 1, outs.at[step]).start()
            settle()
            pump(1)

        task(loads, run)

    def back_task(step):
        down = levels - 1 - step
        last = step == levels - 1
        loads = [top(entering, down)]
        if step == 0:
            loads.append(drive_grad)
        if last:
            loads += [gate_pre, switch, e[levels]]

        def run(bufs):
            cot = bufs[1] if step == 0 else cots.at[step - 1]

            def store(at):
                total = dot_trans(cot[at, :], bufs[0][...]) + shares[step, at, :].astype(F32)
                if last:
                    total = total + dot_trans(bufs[-3][at, :], bufs[-2][...])
                    total = total + bufs[-1][at, :].astype(F32)
                    shares[0, at, :] = total.astype(BF16)
                else:
                    cots[step, at, :] = total.astype(BF16)

            tiles(store)
            if last:
                pltpu.make_async_copy(shares.at[0], token_grads, store_sem.at[1]).start()
            settle()
            pump(1)

        task(loads, run)

    swap_out(0, mixed).start()
    share_task(0)
    grad_task(0, 0, hbm(z[0]), hbm(gate_pre), True)
    for step in range(levels):
        down = levels - 1 - step
        g = 1 + 2 * step
        cot = hbm(drive_grad) if step == 0 else cots.at[step - 1]
        held = hbm(mixed) if step == 0 else outs.at[step - 1]
        grad_task(g, 0, hbm(z[down]), cot, False)
        grad_task(g, half, hbm(zm[down]), cot, True)
        grad_task(g + 1, 0, held, hbm(e[step + 1]), False)
        wait_task(lambda step=step: swap_out(step, mixed).wait_recv(), 3)
        grad_task(g + 1, half, mates.at[step], hbm(e[step + 1]), True)
        out_task(step)
        wait_task(lambda step=step: swap_back(step).wait_recv(), 1 << 20)
        back_task(step)
        if step < levels - 1:
            share_task(step + 1)

    spans, count = [], 0
    for loads, _ in work:
        spans.append((count, count + len(loads)))
        count += len(loads)
    flat = [ref for loads, _ in work for ref in loads]
    owner = [t for t, (loads, _) in enumerate(work) for _ in loads]

    def load(n):
        rows = flat[n].shape[0]
        return pltpu.make_async_copy(
            flat[n], stage.at[n % SLOTS, pl.ds(0, rows)], load_sem.at[n % SLOTS]
        )

    ahead = 0
    for t, (loads, run) in enumerate(work):
        while ahead < count and (ahead < SLOTS or owner[ahead - SLOTS] < t):
            load(ahead).start()
            ahead += 1
        first, last = spans[t]
        for n in range(first, last):
            load(n).wait()
        run([stage.at[n % SLOTS, pl.ds(0, flat[n].shape[0])] for n in range(first, last)])
    settle()
    drain(0)
    for key in issued[-FLIGHT:]:
        finish_send(key)
    for b in (len(blocks) - 2, len(blocks) - 1):
        sibling_copy(b).wait_send()
    for g in (len(groups) - 2, len(groups) - 1):
        final_copy(g).wait()
    for step in range(levels):
        swap_out(step, mixed).wait_send()
    swap_back(levels - 1).wait_send()
    pltpu.make_async_copy(mates.at[0], layer_out, store_sem.at[0]).wait()
    pltpu.make_async_copy(shares.at[0], token_grads, store_sem.at[1]).wait()


def after_scan(z, z_mates, e, mixed, gate_pre, drive_grad, entering, leaving, switch, scale):
    levels = len(z)
    tokens, width = mixed.shape
    seq = lax.axis_size("seq")
    chips = seq // 2
    groups, blocks = 1 + 2 * levels, 1 + 4 * levels
    rows = 2 * width // seq
    hops = groups * (chips - 1) * 2
    hbm = pl.BlockSpec(memory_space=pl.ANY)
    dma = pltpu.SemaphoreType.DMA
    args = [*z, *z_mates, *e, mixed, gate_pre, drive_grad, entering, leaving, switch]
    square = width * width
    count = 2 * tokens * square * (4 * levels + 1 + 4 * levels + 1)
    return pl.pallas_call(
        functools.partial(after_kernel, levels, chips, scale),
        in_specs=[hbm] * len(args),
        out_specs=[hbm] * 5,
        out_shape=[
            jax.ShapeDtypeStruct((tokens, width), BF16),
            jax.ShapeDtypeStruct((tokens, width), BF16),
            jax.ShapeDtypeStruct((levels, rows, width), F32),
            jax.ShapeDtypeStruct((levels, rows, width), F32),
            jax.ShapeDtypeStruct((rows // 2, width), F32),
        ],
        scratch_shapes=[
            pltpu.VMEM((SLOTS, max(tokens, width), width), BF16),
            pltpu.VMEM((2, 2, width // 2, width), BF16),
            pltpu.VMEM((2 * levels, width, width), BF16),
            pltpu.VMEM((width // 2, width), BF16),
            pltpu.VMEM((2 * levels, chips - 1, rows, width), BF16),
            pltpu.VMEM((2 * levels, chips - 1, rows, width), BF16),
            pltpu.VMEM((chips - 1, rows // 2, width), BF16),
            pltpu.VMEM((chips - 1, rows // 2, width), BF16),
            pltpu.VMEM((levels, tokens, width), BF16),
            pltpu.VMEM((levels, tokens, width), BF16),
            pltpu.VMEM((levels - 1, tokens, width), BF16),
            pltpu.VMEM((levels - 1, tokens, width), BF16),
            pltpu.VMEM((tokens, width), BF16),
            pltpu.VMEM((2, rows, width), F32),
            dma((SLOTS,)), dma((blocks,)), dma((blocks,)),
            dma((hops,)), dma((hops,)), dma((hops,)), dma((hops,)),
            dma((2 * levels,)), dma((2 * levels,)), dma((2,)), dma((2,)),
        ],
        compiler_params=pltpu.CompilerParams(
            collective_id=0, has_side_effects=True, vmem_limit_bytes=60 << 20
        ),
        cost_estimate=pl.CostEstimate(
            flops=count, bytes_accessed=60 * tokens * width, transcendentals=0
        ),
        name="after_scan",
    )(*args)


def share_of(cotangent, weight):
    return dot_trans(cotangent, weight[cotangent.shape[1] :]).astype(jnp.bfloat16)


def transposed_step(cotangent, weight, received):
    width = cotangent.shape[1]
    return dot_trans(cotangent, weight[:width]) + received.astype(jnp.float32)


def shards(
    layer_source,
    entering,
    switch,
    leaving,
    channel_persistence,
    position_boosts,
    result_cotangent,
):
    levels = entering.shape[0]
    width = layer_source.shape[1]
    scale = float(layer_source.shape[0] * lax.axis_size("seq")) ** (-0.5)

    z, z_mates = [layer_source], []
    e = [None] * levels + [result_cotangent]
    for step in range(levels):
        z_mates.append(from_partner(z[step], "chan", step))
        down = levels - 1 - step
        share = from_partner(share_of(e[down + 1], leaving[down]), "chan", down)
        e[down] = transposed_step(e[down + 1], leaving[down], share)
        if down > 0:
            e[down] = e[down].astype(jnp.bfloat16)
        summed = dot(z[step], entering[step, :width]) + dot(z_mates[step], entering[step, width:])
        z.append(summed.astype(jnp.bfloat16))
    gate = jax.nn.sigmoid(dot(layer_source, switch))

    mixed, gate_pre_grad, drive_grad = recurrences(
        z[levels], e[0], gate, channel_persistence, position_boosts
    )
    return after_scan(
        z[:levels], z_mates, e[1:], mixed, gate_pre_grad, drive_grad,
        entering, leaving, switch, scale,
    )


def solution(mesh):
    placed = (
        P("seq", "chan"),
        P(None, "chan", None),
        P("chan", None),
        P(None, "chan", None),
        P("chan"),
        P("seq"),
        P("seq", "chan"),
    )
    return jax.shard_map(
        shards,
        mesh=mesh,
        in_specs=placed,
        out_specs=(
            P("seq", "chan"),
            P("seq", "chan"),
            P(None, ("chan", "seq"), None),
            P(None, ("chan", "seq"), None),
            P(("chan", "seq"), None),
        ),
        check_vma=False,
    )
```

```python
import functools

import jax
import jax.numpy as jnp
from jax import lax
from jax.experimental import pallas as pl
from jax.experimental.pallas import tpu as pltpu
from jax.sharding import PartitionSpec as P

LANES = 128
MESH = pl.DeviceIdType.MESH
F32, BF16 = jnp.float32, jnp.bfloat16


def dot(left, right):
    return jnp.dot(left, right, preferred_element_type=jnp.float32)


def dot_rows(left, right):
    return lax.dot_general(
        left, right, (((0,), (0,)), ((), ())), preferred_element_type=jnp.float32
    )


def dot_trans(left, right):
    return lax.dot_general(
        left, right, (((1,), (1,)), ((), ())), preferred_element_type=jnp.float32
    )


SEGMENT = 16
CHUNK = SEGMENT * SEGMENT


def swapped():
    row = lax.broadcasted_iota(jnp.int32, (CHUNK, CHUNK), 0)
    col = lax.broadcasted_iota(jnp.int32, (CHUNK, CHUNK), 1)
    return (lax.rem(row, SEGMENT) * SEGMENT + lax.div(row, SEGMENT) == col).astype(BF16)


def before_kernel(levels, devices, *refs):
    it = iter(refs)
    source, cotangent, entering, leaving, switch, keep, boosts = (next(it) for _ in range(7))
    z_out = [next(it) for _ in range(levels)]
    m_out = [next(it) for _ in range(levels)]
    e_out = [next(it) for _ in range(levels)]
    mixed_out, gate_out, drive_out = (next(it) for _ in range(3))
    w_in, w_out, w_gate, zs, ms, es, shares, sent = (next(it) for _ in range(8))
    drive, out_cot, gate, mixed, gate_pre, drive_grad = (next(it) for _ in range(6))
    totals, prod, ends, backs, carry, order = (next(it) for _ in range(6))
    load_sem, chunk_sem, z_send, z_recv, s_send, s_recv, t_send, t_recv, store_sem = (
        next(it) for _ in range(9)
    )
    tokens, width = drive.shape
    chunks = tokens // CHUNK
    seq, chan = lax.axis_index("seq"), lax.axis_index("chan")

    def partner(level):
        d = 1 << level
        bit = lax.rem(lax.div(chan, d), 2)
        return {"chan": chan + d * (1 - 2 * bit)}

    def rows(c):
        return pl.ds(c * CHUNK, CHUNK)

    def load(n, source, target):
        return pltpu.make_async_copy(source, target, load_sem.at[n])

    def weight(weights, into, level, part, n):
        at = pl.ds(part * width, width)
        return load(n, weights.at[level, at], into.at[level, at])

    def load_z(c):
        return pltpu.make_async_copy(source.at[rows(c)], zs.at[0, rows(c)], chunk_sem.at[c])

    def load_e(c):
        return pltpu.make_async_copy(
            cotangent.at[rows(c)], es.at[levels - 1, rows(c)], chunk_sem.at[chunks + c]
        )

    load_w = {}
    wanted = []
    for step in range(levels):
        down = levels - 1 - step
        wanted += [("out", down, 1), ("in", step, 0), ("in", step, 1), ("out", down, 0)]
    for n, (which, level, part) in enumerate(wanted):
        load_w[which, level, part] = weight(
            *((entering, w_in) if which == "in" else (leaving, w_out)), level, part, n
        )
    load_gate = load(4 * levels, switch, w_gate)
    arrived = set()

    def need(*key):
        if key not in arrived:
            arrived.add(key)
            load_w[key].wait()

    for c in reversed(range(chunks)):
        load_e(c).start()
        if c == chunks - 1:
            load_w[wanted[0]].start()
    for c in range(chunks):
        load_z(c).start()
    load_gate.start()
    for key in wanted[1:]:
        load_w[key].start()

    barrier = pltpu.get_barrier_semaphore()
    for level in range(levels):
        pl.semaphore_signal(barrier, inc=1, device_id=partner(level), device_id_type=MESH)
    for k in range(1, devices):
        pl.semaphore_signal(
            barrier, inc=1, device_id={"seq": lax.rem(seq + k, devices)}, device_id_type=MESH
        )
    pl.semaphore_wait(barrier, levels + devices - 1)

    def remote(source, target, send, recv, device):
        return pltpu.make_async_remote_copy(
            src_ref=source, dst_ref=target, send_sem=send, recv_sem=recv,
            device_id=device, device_id_type=MESH,
        )

    def send_z(level, c):
        n = level * chunks + c
        block = source.at[rows(c)] if level == 0 else zs.at[level, rows(c)]
        return remote(block, ms.at[level, rows(c)], z_send.at[n], z_recv.at[n], partner(level))

    def send_share(level, c):
        n = level * chunks + c
        return remote(
            sent.at[level, rows(c)], shares.at[level, rows(c)],
            s_send.at[n], s_recv.at[n], partner(level),
        )

    def send_totals(k):
        return remote(
            totals.at[seq], totals.at[seq], t_send.at[k - 1], t_recv.at[k - 1],
            {"seq": lax.rem(seq + k, devices)},
        )

    def wait_totals(k):
        there = totals.at[lax.rem(seq + devices - k, devices)]
        remote(
            there, there, t_send.at[k - 1], t_recv.at[k - 1],
            {"seq": lax.rem(seq + k, devices)},
        ).wait_recv()

    for c in range(chunks):
        send_z(0, c).start()
    order[...] = swapped()

    def in_order(ref, level, c):
        ref[level, rows(c), :] = dot(order[...], ref[level, rows(c), :]).astype(BF16)

    def share(level, c):
        need("out", level, 1)
        sent[level, rows(c), :] = dot_trans(
            es[level, rows(c), :], w_out[level, pl.ds(width, width), :]
        ).astype(BF16)
        send_share(level, c).start()

    for c in reversed(range(chunks)):
        load_e(c).wait()
        in_order(es, levels - 1, c)
        share(levels - 1, c)
    load_gate.wait()
    for c in range(chunks):
        load_z(c).wait()
        in_order(zs, 0, c)
        gate[rows(c), :] = jax.nn.sigmoid(dot(zs[0, rows(c), :], w_gate[...]))

    piece = min(256, width)

    def tile(c, i, lane):
        return pl.ds(c * CHUNK + i * SEGMENT, SEGMENT), pl.ds(lane, LANES)

    def for_lanes(run):
        @pl.loop(0, width // piece)
        def _(n):
            run([pl.multiple_of(n * piece, piece) + q for q in range(0, piece, LANES)])

    def lane_row(lane):
        lam = keep[:, pl.ds(lane, LANES)]
        return lam, jnp.sqrt(1.0 - lam * lam)

    def wide(row):
        return jnp.broadcast_to(row, (SEGMENT, LANES))

    def ends_forward(c):
        @for_lanes
        def _(lanes):
            for lane in lanes:
                at = pl.ds(lane, LANES)
                lam, scale = (wide(v) for v in lane_row(lane))
                state = jnp.zeros((SEGMENT, LANES), F32)
                p = jnp.ones((SEGMENT, LANES), F32)
                for i in range(SEGMENT):
                    r, at = tile(c, i, lane)
                    a = boosts[r, :] * lam
                    state = a * state + scale * drive[r, at].astype(F32)
                    p = a * p
                span = pl.ds(c * SEGMENT, SEGMENT)
                prod[span, at] = p
                run = carry[0:1, at]
                grown = carry[1:2, at]
                starts, growths = [], []
                for s in range(SEGMENT):
                    starts.append(run)
                    growths.append(grown)
                    run = p[s : s + 1] * run + state[s : s + 1]
                    grown = p[s : s + 1] * grown
                ends[0, span, at] = jnp.concatenate(starts, axis=0)
                ends[1, span, at] = jnp.concatenate(growths, axis=0)
                carry[0:1, at] = run
                carry[1:2, at] = grown

    def ends_backward(c):
        @for_lanes
        def _(lanes):
            for lane in lanes:
                at = pl.ds(lane, LANES)
                lam = wide(lane_row(lane)[0])
                back = jnp.zeros((SEGMENT, LANES), F32)
                p = jnp.ones((SEGMENT, LANES), F32)
                for i in reversed(range(SEGMENT)):
                    r, at = tile(c, i, lane)
                    a = boosts[r, :] * lam
                    back = a * (out_cot[r, at] * gate[r, at] + back)
                    p = a * p
                span = pl.ds(c * SEGMENT, SEGMENT)
                run = carry[2:3, at]
                grown = carry[3:4, at]
                starts, growths = [None] * SEGMENT, [None] * SEGMENT
                for s in reversed(range(SEGMENT)):
                    starts[s] = run
                    growths[s] = grown
                    run = p[s : s + 1] * run + back[s : s + 1]
                    grown = p[s : s + 1] * grown
                backs[0, span, at] = jnp.concatenate(starts, axis=0)
                backs[1, span, at] = jnp.concatenate(growths, axis=0)
                carry[2:3, at] = run
                carry[3:4, at] = grown

    carry[...] = jnp.zeros_like(carry)
    carry[1:2, :] = jnp.ones((1, width), F32)
    carry[3:4, :] = jnp.ones((1, width), F32)

    stores = []

    def store(ref, out):
        copy = pltpu.make_async_copy(ref, out, store_sem.at[len(stores)])
        copy.start()
        stores.append(copy)

    top, bot = pl.ds(0, width), pl.ds(width, width)
    store(zs.at[0], z_out[0])
    store(es.at[levels - 1], e_out[levels - 1])
    for step in range(levels):
        down = levels - 1 - step
        for n in range(chunks):
            c = n
            send_z(step, c).wait_recv()
            if step == 0:
                in_order(ms, 0, c)
            need("in", step, 0)
            need("in", step, 1)
            summed = (
                dot(zs[step, rows(c), :], w_in[step, top, :])
                + dot(ms[step, rows(c), :], w_in[step, bot, :])
            ).astype(BF16)
            if step + 1 < levels:
                zs[step + 1, rows(c), :] = summed
                send_z(step + 1, c).start()
            else:
                drive[rows(c), :] = summed
                ends_forward(c)
            c = chunks - 1 - n
            send_share(down, c).wait_recv()
            need("out", down, 0)
            total = dot_trans(es[down, rows(c), :], w_out[down, top, :])
            total = total + shares[down, rows(c), :].astype(F32)
            if down > 0:
                es[down - 1, rows(c), :] = total.astype(BF16)
                share(down - 1, c)
            else:
                out_cot[rows(c), :] = total
                ends_backward(c)
        store(ms.at[step], m_out[step])
        if step + 1 < levels:
            store(zs.at[step + 1], z_out[step + 1])
            store(es.at[down - 1], e_out[down - 1])

    totals[seq, 0:1, :] = carry[1:2, :]
    totals[seq, 1:2, :] = carry[0:1, :]
    totals[seq, 2:3, :] = carry[2:3, :]
    for k in range(1, devices):
        send_totals(k).start()
    for k in range(1, devices):
        wait_totals(k)
    h = jnp.zeros((1, width), F32)
    b = jnp.zeros((1, width), F32)
    for k in range(devices):
        h = jnp.where(k < seq, totals[k, 0:1] * h + totals[k, 1:2], h)
        r = devices - 1 - k
        b = jnp.where(r > seq, totals[r, 0:1] * b + totals[r, 2:3], b)
    carry[0:1, :] = h
    carry[2:3, :] = b

    for c in range(chunks):
        span = pl.ds(c * SEGMENT, SEGMENT)

        @for_lanes
        def _(lanes):
            for lane in lanes:
                at = pl.ds(lane, LANES)
                lam, scale = (wide(v) for v in lane_row(lane))
                state = ends[0, span, at] + ends[1, span, at] * wide(carry[0:1, at])
                back = backs[0, span, at] + backs[1, span, at] * wide(carry[2:3, at])
                for i in range(SEGMENT):
                    r, at = tile(c, i, lane)
                    state = boosts[r, :] * lam * state + scale * drive[r, at].astype(F32)
                    sig = gate[r, at]
                    product = state * sig
                    mixed[r, at] = product.astype(BF16)
                    gate_pre[r, at] = (out_cot[r, at] * product * (1.0 - sig)).astype(BF16)
                for i in reversed(range(SEGMENT)):
                    r, at = tile(c, i, lane)
                    total = out_cot[r, at] * gate[r, at] + back
                    drive_grad[r, at] = (scale * total).astype(BF16)
                    back = boosts[r, :] * lam * total

    store(mixed, mixed_out)
    store(gate_pre, gate_out)
    store(drive_grad, drive_out)
    for copy in stores:
        copy.wait()
    for level in range(levels):
        for c in range(chunks):
            send_z(level, c).wait_send()
            send_share(level, c).wait_send()
    for k in range(1, devices):
        send_totals(k).wait_send()


def before_scan(source, cotangent, entering, leaving, switch, keep, boosts):
    levels = entering.shape[0]
    tokens, width = source.shape
    devices = lax.axis_size("seq")
    chunks = tokens // CHUNK
    boosts = boosts.reshape(chunks, SEGMENT, SEGMENT).swapaxes(1, 2).reshape(tokens, 1)
    boosts = jnp.broadcast_to(boosts, (tokens, LANES))
    hbm = pl.BlockSpec(memory_space=pl.ANY)
    vmem = pl.BlockSpec(memory_space=pltpu.VMEM)
    dma = pltpu.SemaphoreType.DMA
    block = jax.ShapeDtypeStruct((tokens, width), BF16)
    count = 3 * levels + 3
    segments = tokens // SEGMENT
    result = pl.pallas_call(
        functools.partial(before_kernel, levels, devices),
        in_specs=[hbm] * 5 + [vmem] * 2,
        out_specs=[hbm] * count,
        out_shape=[block] * count,
        scratch_shapes=[
            pltpu.VMEM((levels, 2 * width, width), BF16),
            pltpu.VMEM((levels, 2 * width, width), BF16),
            pltpu.VMEM((width, width), BF16),
            *[pltpu.VMEM((levels, tokens, width), BF16)] * 5,
            pltpu.VMEM((tokens, width), BF16),
            pltpu.VMEM((tokens, width), F32),
            pltpu.VMEM((tokens, width), F32),
            *[pltpu.VMEM((tokens, width), BF16)] * 3,
            pltpu.VMEM((devices, 8, width), F32),
            pltpu.VMEM((segments, width), F32),
            pltpu.VMEM((2, segments, width), F32),
            pltpu.VMEM((2, segments, width), F32),
            pltpu.VMEM((8, width), F32),
            pltpu.VMEM((CHUNK, CHUNK), BF16),
            dma((4 * levels + 1,)), dma((2 * chunks,)),
            *[dma((levels * chunks,))] * 4,
            *[dma((devices - 1,))] * 2,
            dma((count,)),
        ],
        compiler_params=pltpu.CompilerParams(
            collective_id=1, has_side_effects=True, vmem_limit_bytes=60 << 20
        ),
        cost_estimate=pl.CostEstimate(
            flops=2 * tokens * width * width * (4 * levels + 1),
            bytes_accessed=60 * tokens * width, transcendentals=tokens * width,
        ),
        name="before_scan",
    )(source, cotangent, entering, leaving, switch, keep[None, :], boosts)
    return (
        result[:levels], result[levels : 2 * levels], result[2 * levels : 3 * levels],
        *result[3 * levels :],
    )


SLOTS = 4
FLIGHT = 2


def after_kernel(levels, chips, scale, *refs):
    it = iter(refs)
    z = [next(it) for _ in range(levels)]
    zm = [next(it) for _ in range(levels)]
    e = [None] + [next(it) for _ in range(levels)]
    mixed, gate_pre, drive_grad, entering, leaving, switch = (next(it) for _ in range(6))
    layer_out, token_grads, in_grads, out_grads, gate_grads = (next(it) for _ in range(5))
    stage, part, sums, gate_sums, right, left, gate_right, gate_left = (next(it) for _ in range(8))
    mates, shares, outs, cots, sent, final, order = (next(it) for _ in range(7))
    load_sem, sib_send, sib_recv, right_send, right_recv, left_send, left_recv = (
        next(it) for _ in range(7)
    )
    swap_send, swap_recv, final_sem, store_sem = (next(it) for _ in range(4))

    tokens, width = mixed.shape
    half = width // 2
    seq, chan = lax.axis_index("seq"), lax.axis_index("chan")
    zi, core = lax.div(seq, 2), lax.rem(seq, 2)
    zo = chips - 1 - zi
    sibling = {"seq": seq + 1 - 2 * core}
    upper, lower = {"seq": seq + 2}, {"seq": seq - 2}

    def partner(level):
        d = 1 << level
        bit = lax.rem(lax.div(chan, d), 2)
        return {"chan": chan + d * (1 - 2 * bit)}

    barrier = pltpu.get_barrier_semaphore()

    def greet(device):
        pl.semaphore_signal(barrier, inc=1, device_id=device, device_id_type=MESH)

    for level in range(levels):
        greet(partner(level))
    greet(sibling)

    for device in (lax.rem(seq + 2, 2 * chips), lax.rem(seq + 2 * chips - 2, 2 * chips)):
        greet({"seq": device})
    pl.semaphore_wait(barrier, levels + 3)

    def remote(source, target, send, recv, device):
        return pltpu.make_async_remote_copy(
            src_ref=source, dst_ref=target, send_sem=send, recv_sem=recv,
            device_id=device, device_id_type=MESH,
        )

    def swap_out(step, source):
        return remote(source, mates.at[step], swap_send.at[step], swap_recv.at[step], partner(step))

    def swap_back(step):
        n = levels + step
        return remote(
            sent, shares.at[step], swap_send.at[n], swap_recv.at[n], partner(levels - 1 - step)
        )

    groups = [(gate_grads, gate_sums, gate_right, gate_left)]
    for step in range(levels):
        for out in (in_grads.at[levels - 1 - step], out_grads.at[step]):
            n = len(groups) - 1
            groups.append((out, sums.at[n], right.at[n], left.at[n]))

    def hop(g, k, h, way):
        _, total, up, down = groups[g]
        rows = up.shape[1]
        cols = pl.ds(h * half, half)
        into = (up, down)[way]
        at = (0 if way else chips - k) if k > 0 else 0
        if way:
            first = total.at[pl.ds((k - 1) * rows, rows), cols]
            send, recv, device = left_send, left_recv, lower
        else:
            first = total.at[pl.ds((chips - k) * rows, rows), cols]
            send, recv, device = right_send, right_recv, upper
        n = (g * (chips - 1) + k - 1) * 2 + h

        def copy(source):
            return remote(source, into.at[k - 1, :, cols], send.at[n], recv.at[n], device)

        later = into.at[k - 2, :, cols] if k > 1 else None
        return copy, first, later

    issued = []

    def finish_send(key):
        g, k, h = key
        for way, place in ((0, zi), (1, zo)):
            @pl.when(place <= k - 1)
            def _(way=way):
                copy, first, _ = hop(g, k, h, way)
                copy(first).wait_send()

    def send(g, k, h):
        if len(issued) >= FLIGHT:
            finish_send(issued[-FLIGHT])
        issued.append((g, k, h))
        for way, place in ((0, zi), (1, zo)):
            copy, first, later = hop(g, k, h, way)

            @pl.when(place == 0)
            def _(copy=copy, first=first):
                copy(first).start()

            if k > 1:
                @pl.when((place >= 1) & (place <= k - 1))
                def _(copy=copy, later=later):
                    copy(later).start()

    def event(g, k, h):
        out, total, up, down = groups[g]
        rows = up.shape[1]
        cols = pl.ds(h * half, half)
        for way, place in ((0, zi), (1, zo)):
            copy, first, _ = hop(g, k, h, way)

            @pl.when((place >= 1) & (place <= k))
            def _(way=way, copy=copy, first=first):
                copy(first).wait_recv()
                if k < chips - 1:
                    shard = zi - 1 + chips - k
                    if way:
                        shard = chips - 1 - (zo - 1 + chips - k)
                    at = pl.ds(pl.multiple_of(shard * rows, rows), rows)
                    into = (up, down)[way]
                    into[k - 1, :, cols] = (
                        into[k - 1, :, cols].astype(F32) + total[at, cols].astype(F32)
                    ).astype(BF16)

        if k < chips - 1:
            send(g, k + 1, h)
            return
        slot = g % 2
        if h == 0 and g >= 2:
            final_copy(g - 2).wait()
        at = pl.ds(pl.multiple_of(zi * rows, rows), rows)
        final[slot, :rows, cols] = total[at, cols].astype(F32) * scale

        @pl.when(zi > 0)
        def _():
            final[slot, :rows, cols] += up[chips - 2, :, cols].astype(F32) * scale

        @pl.when(zo > 0)
        def _():
            final[slot, :rows, cols] += down[chips - 2, :, cols].astype(F32) * scale

        if h == 1:
            final_copy(g).start()

    def final_copy(g):
        out, _, up, _ = groups[g]
        rows = up.shape[1]
        return pltpu.make_async_copy(final.at[g % 2, :rows], out, final_sem.at[g % 2])

    blocks = []

    def sibling_copy(b):
        g, offset, slot = blocks[b]
        total = groups[g][1]
        return remote(
            part.at[slot, 1 - core], total.at[pl.ds(offset, half)],
            sib_send.at[b], sib_recv.at[b], sibling,
        )

    def grad(g, offset, left_ref, right_ref):
        b = len(blocks)
        blocks.append((g, offset, b % 2))
        slot = b % 2
        if b >= 2:
            sibling_copy(b - 2).wait_send()
        rows = groups[g][2].shape[1]
        tile = min(256, width)

        @pl.loop(0, width // tile)
        def _(i):
            cols = pl.ds(pl.multiple_of(i * tile, tile), tile)
            result = dot_rows(left_ref[:, cols], right_ref[...]).astype(BF16)
            pieces = tile // rows
            if pieces <= 1:
                per = rows // tile
                shard = lax.div(i, per)
                at = lax.div(shard, 2) * rows + lax.rem(i, per) * tile
                part[slot, lax.rem(shard, 2), pl.ds(pl.multiple_of(at, tile), tile), :] = result
            else:
                for q in range(pieces):
                    at = i * (tile // 2) + q // 2 * rows
                    part[slot, q % 2, pl.ds(pl.multiple_of(at, rows), rows), :] = (
                        result[q * rows : (q + 1) * rows]
                    )

        sibling_copy(b).start()
        return b

    def chip_sum(b):
        g, offset, slot = blocks[b]
        total = groups[g][1]
        sibling_copy(b).wait_recv()
        tile = min(128, half)

        @pl.loop(0, half // tile)
        def _(i):
            at = pl.multiple_of(i * tile, tile)
            there = pl.ds(offset + at, tile)
            total[there, :] = (
                total[there, :].astype(F32) + part[slot, core, pl.ds(at, tile), :].astype(F32)
            ).astype(BF16)

    work = []
    tall = CHUNK

    def tiles(store):
        @pl.loop(0, tokens // tall)
        def _(i):
            store(pl.ds(pl.multiple_of(i * tall, tall), tall))

    def task(loads, run):
        work.append((loads, run))

    def top(weights, level):
        return weights.at[level, pl.ds(0, width)]

    def bot(weights, level):
        return weights.at[level, pl.ds(width, width)]

    queue = []
    pending = []

    def settle():
        while pending:
            b, group_done = pending.pop(0)
            chip_sum(b)
            if group_done:
                g = blocks[b][0]
                for k in range(1, chips):
                    for h in range(2):
                        queue.append((g, k, h))

    started = set()

    def begin():
        for g, k, h in list(queue):
            if k == 1 and (g, h) not in started:
                ahead = queue.index((g, k, h))
                if ahead <= 1:
                    started.add((g, h))
                    send(g, 1, h)

    def pump(count):
        begin()
        for _ in range(count):
            if not queue:
                return
            event(*queue.pop(0))
            begin()

    def drain(keep):
        pump(max(len(queue) - keep, 0))

    def grad_task(g, offset, left_ref, right_ref, last):
        fixed = [r for r in (left_ref, right_ref) if isinstance(r, tuple)]
        loads = [r[0] for r in fixed]

        def run(bufs):
            bufs = list(bufs)
            lhs = bufs.pop(0) if isinstance(left_ref, tuple) else left_ref
            rhs = bufs.pop(0) if isinstance(right_ref, tuple) else right_ref
            settle()
            pending.append((grad(g, offset, lhs, rhs), last))
            pump(1)

        task(loads, run)

    def hbm(ref):
        return (ref,)

    def share_task(step):
        down = levels - 1 - step
        loads = [bot(entering, down)]
        if step == 0:
            loads = [drive_grad] + loads

        def run(bufs):
            cot = bufs[0] if step == 0 else cots.at[step - 1]
            weight = bufs[-1]
            if step > 0:
                swap_back(step - 1).wait_send()

            def store(at):
                sent[at, :] = dot_trans(cot[at, :], weight[...]).astype(BF16)

            tiles(store)
            swap_back(step).start()
            settle()
            pump(1)

        task(loads, run)

    def wait_task(fn, keep):
        def run(bufs):
            settle()
            drain(keep)
            fn()

        task([], run)

    def out_task(step):
        loads = [top(leaving, step), bot(leaving, step)]
        last = step == levels - 1
        if step == 0:
            loads.append(mixed)
        if last:
            loads.append(z[0])

        def run(bufs):
            held = bufs[2] if step == 0 else outs.at[step - 1]
            mate = mates.at[step]

            def store(at):
                total = dot(held[at, :], bufs[0][...]) + dot(mate[at, :], bufs[1][...])
                if last:
                    total = (bufs[-1][at, :].astype(F32) + total).astype(BF16)
                    mates[0, at, :] = dot(order[...], total).astype(BF16)
                else:
                    outs[step, at, :] = total.astype(BF16)

            tiles(store)
            if last:
                pltpu.make_async_copy(mates.at[0], layer_out, store_sem.at[0]).start()
            else:
                swap_out(step + 1, outs.at[step]).start()
            settle()
            pump(1)

        task(loads, run)

    def back_task(step):
        down = levels - 1 - step
        last = step == levels - 1
        loads = [top(entering, down)]
        if step == 0:
            loads.append(drive_grad)
        if last:
            loads += [gate_pre, switch, e[levels]]

        def run(bufs):
            cot = bufs[1] if step == 0 else cots.at[step - 1]

            def store(at):
                total = dot_trans(cot[at, :], bufs[0][...]) + shares[step, at, :].astype(F32)
                if last:
                    total = total + dot_trans(bufs[-3][at, :], bufs[-2][...])
                    total = total + bufs[-1][at, :].astype(F32)
                    shares[0, at, :] = dot(order[...], total.astype(BF16)).astype(BF16)
                else:
                    cots[step, at, :] = total.astype(BF16)

            tiles(store)
            if last:
                pltpu.make_async_copy(shares.at[0], token_grads, store_sem.at[1]).start()
            settle()
            pump(1)

        task(loads, run)

    swap_out(0, mixed).start()
    order[...] = swapped()
    share_task(0)
    grad_task(0, 0, hbm(z[0]), hbm(gate_pre), True)
    for step in range(levels):
        down = levels - 1 - step
        g = 1 + 2 * step
        cot = hbm(drive_grad) if step == 0 else cots.at[step - 1]
        held = hbm(mixed) if step == 0 else outs.at[step - 1]
        grad_task(g, 0, hbm(z[down]), cot, False)
        grad_task(g, half, hbm(zm[down]), cot, True)
        grad_task(g + 1, 0, held, hbm(e[step + 1]), False)
        wait_task(lambda step=step: swap_out(step, mixed).wait_recv(), 3)
        grad_task(g + 1, half, mates.at[step], hbm(e[step + 1]), True)
        out_task(step)
        wait_task(lambda step=step: swap_back(step).wait_recv(), 1 << 20)
        back_task(step)
        if step < levels - 1:
            share_task(step + 1)

    spans, count = [], 0
    for loads, _ in work:
        spans.append((count, count + len(loads)))
        count += len(loads)
    flat = [ref for loads, _ in work for ref in loads]
    owner = [t for t, (loads, _) in enumerate(work) for _ in loads]

    def load(n):
        rows = flat[n].shape[0]
        return pltpu.make_async_copy(
            flat[n], stage.at[n % SLOTS, pl.ds(0, rows)], load_sem.at[n % SLOTS]
        )

    ahead = 0
    for t, (loads, run) in enumerate(work):
        while ahead < count and (ahead < SLOTS or owner[ahead - SLOTS] < t):
            load(ahead).start()
            ahead += 1
        first, last = spans[t]
        for n in range(first, last):
            load(n).wait()
        run([stage.at[n % SLOTS, pl.ds(0, flat[n].shape[0])] for n in range(first, last)])
    settle()
    drain(0)
    for key in issued[-FLIGHT:]:
        finish_send(key)
    for b in (len(blocks) - 2, len(blocks) - 1):
        sibling_copy(b).wait_send()
    for g in (len(groups) - 2, len(groups) - 1):
        final_copy(g).wait()
    for step in range(levels):
        swap_out(step, mixed).wait_send()
    swap_back(levels - 1).wait_send()
    pltpu.make_async_copy(mates.at[0], layer_out, store_sem.at[0]).wait()
    pltpu.make_async_copy(shares.at[0], token_grads, store_sem.at[1]).wait()


def after_scan(z, z_mates, e, mixed, gate_pre, drive_grad, entering, leaving, switch, scale):
    levels = len(z)
    tokens, width = mixed.shape
    seq = lax.axis_size("seq")
    chips = seq // 2
    groups, blocks = 1 + 2 * levels, 1 + 4 * levels
    rows = 2 * width // seq
    hops = groups * (chips - 1) * 2
    hbm = pl.BlockSpec(memory_space=pl.ANY)
    dma = pltpu.SemaphoreType.DMA
    args = [*z, *z_mates, *e, mixed, gate_pre, drive_grad, entering, leaving, switch]
    square = width * width
    count = 2 * tokens * square * (4 * levels + 1 + 4 * levels + 1)
    return pl.pallas_call(
        functools.partial(after_kernel, levels, chips, scale),
        in_specs=[hbm] * len(args),
        out_specs=[hbm] * 5,
        out_shape=[
            jax.ShapeDtypeStruct((tokens, width), BF16),
            jax.ShapeDtypeStruct((tokens, width), BF16),
            jax.ShapeDtypeStruct((levels, rows, width), F32),
            jax.ShapeDtypeStruct((levels, rows, width), F32),
            jax.ShapeDtypeStruct((rows // 2, width), F32),
        ],
        scratch_shapes=[
            pltpu.VMEM((SLOTS, max(tokens, width), width), BF16),
            pltpu.VMEM((2, 2, width // 2, width), BF16),
            pltpu.VMEM((2 * levels, width, width), BF16),
            pltpu.VMEM((width // 2, width), BF16),
            pltpu.VMEM((2 * levels, chips - 1, rows, width), BF16),
            pltpu.VMEM((2 * levels, chips - 1, rows, width), BF16),
            pltpu.VMEM((chips - 1, rows // 2, width), BF16),
            pltpu.VMEM((chips - 1, rows // 2, width), BF16),
            pltpu.VMEM((levels, tokens, width), BF16),
            pltpu.VMEM((levels, tokens, width), BF16),
            pltpu.VMEM((levels - 1, tokens, width), BF16),
            pltpu.VMEM((levels - 1, tokens, width), BF16),
            pltpu.VMEM((tokens, width), BF16),
            pltpu.VMEM((2, rows, width), F32),
            pltpu.VMEM((CHUNK, CHUNK), BF16),
            dma((SLOTS,)), dma((blocks,)), dma((blocks,)),
            dma((hops,)), dma((hops,)), dma((hops,)), dma((hops,)),
            dma((2 * levels,)), dma((2 * levels,)), dma((2,)), dma((2,)),
        ],
        compiler_params=pltpu.CompilerParams(
            collective_id=0, has_side_effects=True, vmem_limit_bytes=60 << 20
        ),
        cost_estimate=pl.CostEstimate(
            flops=count, bytes_accessed=60 * tokens * width, transcendentals=0
        ),
        name="after_scan",
    )(*args)


def shards(
    layer_source,
    entering,
    switch,
    leaving,
    channel_persistence,
    position_boosts,
    result_cotangent,
):
    scale = float(layer_source.shape[0] * lax.axis_size("seq")) ** (-0.5)
    z, z_mates, e, mixed, gate_pre_grad, drive_grad = before_scan(
        layer_source, result_cotangent, entering, leaving, switch,
        channel_persistence, position_boosts,
    )
    return after_scan(
        z, z_mates, e, mixed, gate_pre_grad, drive_grad, entering, leaving, switch, scale
    )


def solution(mesh):
    placed = (
        P("seq", "chan"),
        P(None, "chan", None),
        P("chan", None),
        P(None, "chan", None),
        P("chan"),
        P("seq"),
        P("seq", "chan"),
    )
    return jax.shard_map(
        shards,
        mesh=mesh,
        in_specs=placed,
        out_specs=(
            P("seq", "chan"),
            P("seq", "chan"),
            P(None, ("chan", "seq"), None),
            P(None, ("chan", "seq"), None),
            P(("chan", "seq"), None),
        ),
        check_vma=False,
    )
```

```python
import functools

import jax
import jax.numpy as jnp
from jax import lax
from jax.experimental import pallas as pl
from jax.experimental.pallas import tpu as pltpu
from jax.sharding import PartitionSpec as P

LANES = 128
MESH = pl.DeviceIdType.MESH
F32, BF16 = jnp.float32, jnp.bfloat16


def dot(left, right):
    return jnp.dot(left, right, preferred_element_type=jnp.float32)


def dot_rows(left, right):
    return lax.dot_general(
        left, right, (((0,), (0,)), ((), ())), preferred_element_type=jnp.float32
    )


def dot_trans(left, right):
    return lax.dot_general(
        left, right, (((1,), (1,)), ((), ())), preferred_element_type=jnp.float32
    )


SEGMENT = 16
CHUNK = SEGMENT * SEGMENT


def swapped():
    row = lax.broadcasted_iota(jnp.int32, (CHUNK, CHUNK), 0)
    col = lax.broadcasted_iota(jnp.int32, (CHUNK, CHUNK), 1)
    return (lax.rem(row, SEGMENT) * SEGMENT + lax.div(row, SEGMENT) == col).astype(BF16)


def before_kernel(levels, devices, *refs):
    it = iter(refs)
    source, cotangent, entering, leaving, switch, keep, position = (next(it) for _ in range(7))
    z_out = [next(it) for _ in range(levels)]
    m_out = [next(it) for _ in range(levels)]
    e_out = [next(it) for _ in range(levels)]
    mixed_out, gate_out, drive_out = (next(it) for _ in range(3))
    w_in, w_out, w_gate, zs, ms, es, shares, sent = (next(it) for _ in range(8))
    drive, out_cot, gate, mixed, gate_pre, drive_grad = (next(it) for _ in range(6))
    totals, ends, backs, carry, order, boosts = (next(it) for _ in range(6))
    load_sem, chunk_sem, z_send, z_recv, s_send, s_recv, t_send, t_recv, store_sem = (
        next(it) for _ in range(9)
    )
    tokens, width = drive.shape
    chunks = tokens // CHUNK
    seq, chan = lax.axis_index("seq"), lax.axis_index("chan")

    def partner(level):
        d = 1 << level
        bit = lax.rem(lax.div(chan, d), 2)
        return {"chan": chan + d * (1 - 2 * bit)}

    def rows(c):
        return pl.ds(c * CHUNK, CHUNK)

    def load(n, source, target):
        return pltpu.make_async_copy(source, target, load_sem.at[n])

    def weight(weights, into, level, part, n):
        at = pl.ds(part * width, width)
        return load(n, weights.at[level, at], into.at[level, at])

    def load_z(c):
        return pltpu.make_async_copy(source.at[rows(c)], zs.at[0, rows(c)], chunk_sem.at[c])

    def load_e(c):
        return pltpu.make_async_copy(
            cotangent.at[rows(c)], es.at[levels - 1, rows(c)], chunk_sem.at[chunks + c]
        )

    load_w = {}
    wanted = []
    for step in range(levels):
        down = levels - 1 - step
        wanted += [("out", down, 1), ("in", step, 0), ("in", step, 1), ("out", down, 0)]
    for n, (which, level, part) in enumerate(wanted):
        load_w[which, level, part] = weight(
            *((entering, w_in) if which == "in" else (leaving, w_out)), level, part, n
        )
    load_gate = load(4 * levels, switch, w_gate)
    arrived = set()

    def need(*key):
        if key not in arrived:
            arrived.add(key)
            load_w[key].wait()

    for c in reversed(range(chunks)):
        load_e(c).start()
        if c == chunks - 1:
            load_w[wanted[0]].start()
    for c in range(chunks):
        load_z(c).start()
    load_gate.start()
    for key in wanted[1:]:
        load_w[key].start()

    barrier = pltpu.get_barrier_semaphore()
    for level in range(levels):
        pl.semaphore_signal(barrier, inc=1, device_id=partner(level), device_id_type=MESH)
    for k in range(1, devices):
        pl.semaphore_signal(
            barrier, inc=1, device_id={"seq": lax.rem(seq + k, devices)}, device_id_type=MESH
        )
    pl.semaphore_wait(barrier, levels + devices - 1)

    def remote(source, target, send, recv, device):
        return pltpu.make_async_remote_copy(
            src_ref=source, dst_ref=target, send_sem=send, recv_sem=recv,
            device_id=device, device_id_type=MESH,
        )

    def send_z(level, c):
        n = level * chunks + c
        block = source.at[rows(c)] if level == 0 else zs.at[level, rows(c)]
        return remote(block, ms.at[level, rows(c)], z_send.at[n], z_recv.at[n], partner(level))

    def send_share(level, c):
        n = level * chunks + c
        return remote(
            sent.at[level, rows(c)], shares.at[level, rows(c)],
            s_send.at[n], s_recv.at[n], partner(level),
        )

    def send_totals(k):
        return remote(
            totals.at[seq], totals.at[seq], t_send.at[k - 1], t_recv.at[k - 1],
            {"seq": lax.rem(seq + k, devices)},
        )

    def wait_totals(k):
        there = totals.at[lax.rem(seq + devices - k, devices)]
        remote(
            there, there, t_send.at[k - 1], t_recv.at[k - 1],
            {"seq": lax.rem(seq + k, devices)},
        ).wait_recv()

    for c in range(chunks):
        send_z(0, c).start()
    order[...] = swapped()
    for c in range(chunks):
        here = position[c * SEGMENT : (c + 1) * SEGMENT, :]
        for i in range(SEGMENT):
            boosts[pl.ds(c * CHUNK + i * SEGMENT, SEGMENT), :] = jnp.broadcast_to(
                here[:, i : i + 1], (SEGMENT, LANES)
            )

    def in_order(ref, level, c):
        ref[level, rows(c), :] = dot(order[...], ref[level, rows(c), :]).astype(BF16)

    def share(level, c):
        need("out", level, 1)
        sent[level, rows(c), :] = dot_trans(
            es[level, rows(c), :], w_out[level, pl.ds(width, width), :]
        ).astype(BF16)
        send_share(level, c).start()

    for c in reversed(range(chunks)):
        load_e(c).wait()
        in_order(es, levels - 1, c)
        share(levels - 1, c)
    load_gate.wait()
    for c in range(chunks):
        load_z(c).wait()
        in_order(zs, 0, c)
        gate[rows(c), :] = jax.nn.sigmoid(dot(zs[0, rows(c), :], w_gate[...]))

    piece = min(256, width)

    def tile(c, i, lane):
        return pl.ds(c * CHUNK + i * SEGMENT, SEGMENT), pl.ds(lane, LANES)

    def for_lanes(run):
        @pl.loop(0, width // piece)
        def _(n):
            run([pl.multiple_of(n * piece, piece) + q for q in range(0, piece, LANES)])

    def lane_row(lane):
        lam = keep[:, pl.ds(lane, LANES)]
        return lam, jnp.sqrt(1.0 - lam * lam)

    def wide(row):
        return jnp.broadcast_to(row, (SEGMENT, LANES))

    def ends_forward(c):
        @for_lanes
        def _(lanes):
            for lane in lanes:
                at = pl.ds(lane, LANES)
                lam, scale = (wide(v) for v in lane_row(lane))
                state = jnp.zeros((SEGMENT, LANES), F32)
                p = jnp.ones((SEGMENT, LANES), F32)
                for i in range(SEGMENT):
                    r, at = tile(c, i, lane)
                    a = boosts[r, :] * lam
                    state = a * state + scale * drive[r, at].astype(F32)
                    p = a * p
                span = pl.ds(c * SEGMENT, SEGMENT)
                run = carry[0:1, at]
                grown = carry[1:2, at]
                starts, growths = [], []
                for s in range(SEGMENT):
                    starts.append(run)
                    growths.append(grown)
                    run = p[s : s + 1] * run + state[s : s + 1]
                    grown = p[s : s + 1] * grown
                ends[0, span, at] = jnp.concatenate(starts, axis=0)
                ends[1, span, at] = jnp.concatenate(growths, axis=0)
                carry[0:1, at] = run
                carry[1:2, at] = grown

    def ends_backward(c):
        @for_lanes
        def _(lanes):
            for lane in lanes:
                at = pl.ds(lane, LANES)
                lam = wide(lane_row(lane)[0])
                back = jnp.zeros((SEGMENT, LANES), F32)
                p = jnp.ones((SEGMENT, LANES), F32)
                for i in reversed(range(SEGMENT)):
                    r, at = tile(c, i, lane)
                    a = boosts[r, :] * lam
                    back = a * (out_cot[r, at] * gate[r, at] + back)
                    p = a * p
                span = pl.ds(c * SEGMENT, SEGMENT)
                run = carry[2:3, at]
                grown = carry[3:4, at]
                starts, growths = [None] * SEGMENT, [None] * SEGMENT
                for s in reversed(range(SEGMENT)):
                    starts[s] = run
                    growths[s] = grown
                    run = p[s : s + 1] * run + back[s : s + 1]
                    grown = p[s : s + 1] * grown
                backs[0, span, at] = jnp.concatenate(starts, axis=0)
                backs[1, span, at] = jnp.concatenate(growths, axis=0)
                carry[2:3, at] = run
                carry[3:4, at] = grown

    carry[...] = jnp.zeros_like(carry)
    carry[1:2, :] = jnp.ones((1, width), F32)
    carry[3:4, :] = jnp.ones((1, width), F32)

    stores = []

    def store(ref, out):
        copy = pltpu.make_async_copy(ref, out, store_sem.at[len(stores)])
        copy.start()
        stores.append(copy)

    top, bot = pl.ds(0, width), pl.ds(width, width)
    store(zs.at[0], z_out[0])
    store(es.at[levels - 1], e_out[levels - 1])
    for step in range(levels):
        down = levels - 1 - step
        for n in range(chunks):
            c = n
            send_z(step, c).wait_recv()
            if step == 0:
                in_order(ms, 0, c)
            need("in", step, 0)
            need("in", step, 1)
            summed = (
                dot(zs[step, rows(c), :], w_in[step, top, :])
                + dot(ms[step, rows(c), :], w_in[step, bot, :])
            ).astype(BF16)
            if step + 1 < levels:
                zs[step + 1, rows(c), :] = summed
                send_z(step + 1, c).start()
            else:
                drive[rows(c), :] = summed
                ends_forward(c)
            c = chunks - 1 - n
            send_share(down, c).wait_recv()
            need("out", down, 0)
            total = dot_trans(es[down, rows(c), :], w_out[down, top, :])
            total = total + shares[down, rows(c), :].astype(F32)
            if down > 0:
                es[down - 1, rows(c), :] = total.astype(BF16)
                share(down - 1, c)
            else:
                out_cot[rows(c), :] = total
                ends_backward(c)
        store(ms.at[step], m_out[step])
        if step + 1 < levels:
            store(zs.at[step + 1], z_out[step + 1])
            store(es.at[down - 1], e_out[down - 1])

    totals[seq, 0:1, :] = carry[1:2, :]
    totals[seq, 1:2, :] = carry[0:1, :]
    totals[seq, 2:3, :] = carry[2:3, :]
    for k in range(1, devices):
        send_totals(k).start()
    for k in range(1, devices):
        wait_totals(k)
    h = jnp.zeros((1, width), F32)
    b = jnp.zeros((1, width), F32)
    for k in range(devices):
        h = jnp.where(k < seq, totals[k, 0:1] * h + totals[k, 1:2], h)
        r = devices - 1 - k
        b = jnp.where(r > seq, totals[r, 0:1] * b + totals[r, 2:3], b)
    carry[0:1, :] = h
    carry[2:3, :] = b

    for c in range(chunks):
        span = pl.ds(c * SEGMENT, SEGMENT)

        @for_lanes
        def _(lanes):
            for lane in lanes:
                at = pl.ds(lane, LANES)
                lam, scale = (wide(v) for v in lane_row(lane))
                state = ends[0, span, at] + ends[1, span, at] * wide(carry[0:1, at])
                back = backs[0, span, at] + backs[1, span, at] * wide(carry[2:3, at])
                for i in range(SEGMENT):
                    r, at = tile(c, i, lane)
                    state = boosts[r, :] * lam * state + scale * drive[r, at].astype(F32)
                    sig = gate[r, at]
                    product = state * sig
                    mixed[r, at] = product.astype(BF16)
                    gate_pre[r, at] = (out_cot[r, at] * product * (1.0 - sig)).astype(BF16)
                for i in reversed(range(SEGMENT)):
                    r, at = tile(c, i, lane)
                    total = out_cot[r, at] * gate[r, at] + back
                    drive_grad[r, at] = (scale * total).astype(BF16)
                    back = boosts[r, :] * lam * total

        for ref, out in ((mixed, mixed_out), (gate_pre, gate_out), (drive_grad, drive_out)):
            store(ref.at[rows(c)], out.at[rows(c)])

    for copy in stores:
        copy.wait()
    for level in range(levels):
        for c in range(chunks):
            send_z(level, c).wait_send()
            send_share(level, c).wait_send()
    for k in range(1, devices):
        send_totals(k).wait_send()


def before_scan(source, cotangent, entering, leaving, switch, keep, boosts):
    levels = entering.shape[0]
    tokens, width = source.shape
    devices = lax.axis_size("seq")
    chunks = tokens // CHUNK
    boosts = boosts.reshape(tokens // SEGMENT, SEGMENT)
    hbm = pl.BlockSpec(memory_space=pl.ANY)
    vmem = pl.BlockSpec(memory_space=pltpu.VMEM)
    dma = pltpu.SemaphoreType.DMA
    block = jax.ShapeDtypeStruct((tokens, width), BF16)
    count = 3 * levels + 3
    segments = tokens // SEGMENT
    result = pl.pallas_call(
        functools.partial(before_kernel, levels, devices),
        in_specs=[hbm] * 5 + [vmem] * 2,
        out_specs=[hbm] * count,
        out_shape=[block] * count,
        scratch_shapes=[
            pltpu.VMEM((levels, 2 * width, width), BF16),
            pltpu.VMEM((levels, 2 * width, width), BF16),
            pltpu.VMEM((width, width), BF16),
            *[pltpu.VMEM((levels, tokens, width), BF16)] * 5,
            pltpu.VMEM((tokens, width), BF16),
            pltpu.VMEM((tokens, width), F32),
            pltpu.VMEM((tokens, width), F32),
            *[pltpu.VMEM((tokens, width), BF16)] * 3,
            pltpu.VMEM((devices, 8, width), F32),
            pltpu.VMEM((2, segments, width), F32),
            pltpu.VMEM((2, segments, width), F32),
            pltpu.VMEM((8, width), F32),
            pltpu.VMEM((CHUNK, CHUNK), BF16),
            pltpu.VMEM((tokens, LANES), F32),
            dma((4 * levels + 1,)), dma((2 * chunks,)),
            *[dma((levels * chunks,))] * 4,
            *[dma((devices - 1,))] * 2,
            dma((3 * levels + 3 * chunks,)),
        ],
        compiler_params=pltpu.CompilerParams(
            collective_id=1, has_side_effects=True, vmem_limit_bytes=60 << 20
        ),
        cost_estimate=pl.CostEstimate(
            flops=2 * tokens * width * width * (4 * levels + 1),
            bytes_accessed=60 * tokens * width, transcendentals=tokens * width,
        ),
        name="before_scan",
    )(source, cotangent, entering, leaving, switch, keep[None, :], boosts)
    return (
        result[:levels], result[levels : 2 * levels], result[2 * levels : 3 * levels],
        *result[3 * levels :],
    )


SLOTS = 4


def after_kernel(levels, chips, scale, *refs):
    it = iter(refs)
    z = [next(it) for _ in range(levels)]
    zm = [next(it) for _ in range(levels)]
    e = [None] + [next(it) for _ in range(levels)]
    mixed, gate_pre, drive_grad, entering, leaving, switch = (next(it) for _ in range(6))
    layer_out, token_grads, in_grads, out_grads, gate_grads = (next(it) for _ in range(5))
    stage, part, sums, gate_sums, right, left, gate_right, gate_left = (next(it) for _ in range(8))
    mates, shares, outs, cots, sent, order = (next(it) for _ in range(6))
    load_sem, sib_send, sib_recv, right_send, right_recv, left_send, left_recv = (
        next(it) for _ in range(7)
    )
    swap_send, swap_recv = (next(it) for _ in range(2))

    tokens, width = mixed.shape
    half = width // 2
    seq, chan = lax.axis_index("seq"), lax.axis_index("chan")
    zi, core = lax.div(seq, 2), lax.rem(seq, 2)
    zo = chips - 1 - zi
    sibling = {"seq": seq + 1 - 2 * core}
    upper, lower = {"seq": seq + 2}, {"seq": seq - 2}

    def partner(level):
        d = 1 << level
        bit = lax.rem(lax.div(chan, d), 2)
        return {"chan": chan + d * (1 - 2 * bit)}

    def remote(source, target, send, recv, device):
        return pltpu.make_async_remote_copy(
            src_ref=source, dst_ref=target, send_sem=send, recv_sem=recv,
            device_id=device, device_id_type=MESH,
        )

    def swap_out(step, source):
        return remote(source, mates.at[step], swap_send.at[step], swap_recv.at[step], partner(step))

    def swap_back(step):
        n = levels + step
        return remote(
            sent, shares.at[step], swap_send.at[n], swap_recv.at[n], partner(levels - 1 - step)
        )

    groups = [(gate_grads, gate_sums, gate_right, gate_left)]
    for step in range(levels):
        for out in (in_grads.at[levels - 1 - step], out_grads.at[step]):
            n = len(groups) - 1
            groups.append((out, sums.at[n], right.at[n], left.at[n]))

    def hop(g, k, h, way):
        _, total, up, down = groups[g]
        rows = up.shape[1]
        cols = pl.ds(h * half, half)
        into = (up, down)[way]
        at = (0 if way else chips - k) if k > 0 else 0
        if way:
            first = total.at[pl.ds((k - 1) * rows, rows), cols]
            send, recv, device = left_send, left_recv, lower
        else:
            first = total.at[pl.ds((chips - k) * rows, rows), cols]
            send, recv, device = right_send, right_recv, upper
        n = (g * (chips - 1) + k - 1) * 2 + h

        def copy(source):
            return remote(source, into.at[k - 1, :, cols], send.at[n], recv.at[n], device)

        later = into.at[k - 2, :, cols] if k > 1 else None
        return copy, first, later

    def depart(g):
        for k in range(1, chips):
            for h in range(2):
                for way, place in ((0, zi), (1, zo)):
                    copy, first, _ = hop(g, k, h, way)

                    @pl.when(place == 0)
                    def _(copy=copy, first=first):
                        copy(first).start()

    def forward(g, k, h):
        for way, place in ((0, zi), (1, zo)):
            copy, _, later = hop(g, k, h, way)

            @pl.when((place >= 1) & (place <= k - 1))
            def _(copy=copy, later=later):
                copy(later).start()

    def finish_sends(g):
        for k in range(1, chips):
            for h in range(2):
                for way, place in ((0, zi), (1, zo)):
                    copy, first, _ = hop(g, k, h, way)

                    @pl.when(place <= k - 1)
                    def _(copy=copy, first=first):
                        copy(first).wait_send()

    def event(g, k, h):
        out, total, up, down = groups[g]
        rows = up.shape[1]
        cols = pl.ds(h * half, half)
        for way, place in ((0, zi), (1, zo)):
            copy, first, _ = hop(g, k, h, way)

            @pl.when((place >= 1) & (place <= k))
            def _(way=way, copy=copy, first=first):
                copy(first).wait_recv()
                if k < chips - 1:
                    shard = zi - 1 + chips - k
                    if way:
                        shard = chips - 1 - (zo - 1 + chips - k)
                    at = pl.ds(pl.multiple_of(shard * rows, rows), rows)
                    into = (up, down)[way]
                    into[k - 1, :, cols] = (
                        into[k - 1, :, cols].astype(F32) + total[at, cols].astype(F32)
                    ).astype(BF16)

        if k < chips - 1:
            forward(g, k + 1, h)
            return
        at = pl.ds(pl.multiple_of(zi * rows, rows), rows)
        out[:, cols] = total[at, cols].astype(F32) * scale

        @pl.when(zi > 0)
        def _():
            out[:, cols] += up[chips - 2, :, cols].astype(F32) * scale

        @pl.when(zo > 0)
        def _():
            out[:, cols] += down[chips - 2, :, cols].astype(F32) * scale

    blocks = []

    def sibling_copy(b):
        g, offset, slot = blocks[b]
        total = groups[g][1]
        return remote(
            part.at[slot, 1 - core], total.at[pl.ds(offset, half)],
            sib_send.at[b], sib_recv.at[b], sibling,
        )

    def grad(g, offset, left_ref, right_ref):
        b = len(blocks)
        blocks.append((g, offset, b % 2))
        slot = b % 2
        if b >= 2:
            sibling_copy(b - 2).wait_send()
        rows = groups[g][2].shape[1]
        tile = min(256, width)

        @pl.loop(0, width // tile)
        def _(i):
            cols = pl.ds(pl.multiple_of(i * tile, tile), tile)
            result = dot_rows(left_ref[:, cols], right_ref[...]).astype(BF16)
            pieces = tile // rows
            if pieces <= 1:
                per = rows // tile
                shard = lax.div(i, per)
                at = lax.div(shard, 2) * rows + lax.rem(i, per) * tile
                part[slot, lax.rem(shard, 2), pl.ds(pl.multiple_of(at, tile), tile), :] = result
            else:
                for q in range(pieces):
                    at = i * (tile // 2) + q // 2 * rows
                    part[slot, q % 2, pl.ds(pl.multiple_of(at, rows), rows), :] = (
                        result[q * rows : (q + 1) * rows]
                    )

        sibling_copy(b).start()
        return b

    def chip_sum(b):
        g, offset, slot = blocks[b]
        total = groups[g][1]
        sibling_copy(b).wait_recv()
        tile = min(128, half)

        @pl.loop(0, half // tile)
        def _(i):
            at = pl.multiple_of(i * tile, tile)
            there = pl.ds(offset + at, tile)
            total[there, :] = (
                total[there, :].astype(F32) + part[slot, core, pl.ds(at, tile), :].astype(F32)
            ).astype(BF16)

    work = []
    tall = CHUNK

    def tiles(store):
        @pl.loop(0, tokens // tall)
        def _(i):
            store(pl.ds(pl.multiple_of(i * tall, tall), tall))

    def task(loads, run):
        work.append((loads, run))

    def top(weights, level):
        return weights.at[level, pl.ds(0, width)]

    def bot(weights, level):
        return weights.at[level, pl.ds(width, width)]

    queue = []
    pending = []

    def settle():
        while pending:
            b, group_done = pending.pop(0)
            chip_sum(b)
            if group_done:
                g = blocks[b][0]
                depart(g)
                for k in range(1, chips):
                    for h in range(2):
                        queue.append((g, k, h))

    def pump(count):
        for _ in range(count):
            if queue:
                event(*queue.pop(0))

    def drain(keep):
        pump(max(len(queue) - keep, 0))

    def grad_task(g, offset, left_ref, right_ref, last):
        fixed = [r for r in (left_ref, right_ref) if isinstance(r, tuple)]
        loads = [r[0] for r in fixed]

        def run(bufs):
            bufs = list(bufs)
            lhs = bufs.pop(0) if isinstance(left_ref, tuple) else left_ref
            rhs = bufs.pop(0) if isinstance(right_ref, tuple) else right_ref
            settle()
            pending.append((grad(g, offset, lhs, rhs), last))
            pump(1)

        task(loads, run)

    def hbm(ref):
        return (ref,)

    def share_task(step):
        down = levels - 1 - step
        loads = [bot(entering, down)]
        if step == 0:
            loads = [drive_grad] + loads

        def run(bufs):
            cot = bufs[0] if step == 0 else cots.at[step - 1]
            weight = bufs[-1]
            if step == 0:
                settle()
            if step > 0:
                swap_back(step - 1).wait_send()

            def store(at):
                sent[at, :] = dot_trans(cot[at, :], weight[...]).astype(BF16)

            tiles(store)
            swap_back(step).start()
            settle()
            pump(1)

        task(loads, run)

    def wait_task(fn, keep):
        def run(bufs):
            settle()
            drain(keep)
            fn()

        task([], run)

    def out_task(step):
        loads = [top(leaving, step), bot(leaving, step)]
        last = step == levels - 1
        if step == 0:
            loads.append(mixed)
        if last:
            loads.append(z[0])

        def run(bufs):
            held = bufs[2] if step == 0 else outs.at[step - 1]
            mate = mates.at[step]

            def store(at):
                total = dot(held[at, :], bufs[0][...]) + dot(mate[at, :], bufs[1][...])
                if last:
                    total = (bufs[-1][at, :].astype(F32) + total).astype(BF16)
                    layer_out[at, :] = dot(order[...], total).astype(BF16)
                else:
                    outs[step, at, :] = total.astype(BF16)

            tiles(store)
            if not last:
                swap_out(step + 1, outs.at[step]).start()
            settle()
            pump(1)

        task(loads, run)

    def back_task(step):
        down = levels - 1 - step
        last = step == levels - 1
        loads = [top(entering, down)]
        if step == 0:
            loads.append(drive_grad)
        if last:
            loads += [gate_pre, switch, e[levels]]

        def run(bufs):
            cot = bufs[1] if step == 0 else cots.at[step - 1]

            def store(at):
                total = dot_trans(cot[at, :], bufs[0][...]) + shares[step, at, :].astype(F32)
                if last:
                    total = total + dot_trans(bufs[-3][at, :], bufs[-2][...])
                    total = total + bufs[-1][at, :].astype(F32)
                    token_grads[at, :] = dot(order[...], total.astype(BF16)).astype(BF16)
                else:
                    cots[step, at, :] = total.astype(BF16)

            tiles(store)
            settle()
            pump(1)

        task(loads, run)

    grad_task(0, 0, hbm(z[0]), hbm(gate_pre), True)
    share_task(0)
    for step in range(levels):
        down = levels - 1 - step
        g = 1 + 2 * step
        cot = hbm(drive_grad) if step == 0 else cots.at[step - 1]
        held = hbm(mixed) if step == 0 else outs.at[step - 1]
        grad_task(g, 0, hbm(z[down]), cot, False)
        grad_task(g, half, hbm(zm[down]), cot, True)
        grad_task(g + 1, 0, held, hbm(e[step + 1]), False)
        wait_task(lambda step=step: swap_out(step, mixed).wait_recv(), 3)
        grad_task(g + 1, half, mates.at[step], hbm(e[step + 1]), True)
        out_task(step)
        wait_task(lambda step=step: swap_back(step).wait_recv(), 1 << 20)
        back_task(step)
        if step < levels - 1:
            share_task(step + 1)

    spans, count = [], 0
    for loads, _ in work:
        spans.append((count, count + len(loads)))
        count += len(loads)
    flat = [ref for loads, _ in work for ref in loads]
    owner = [t for t, (loads, _) in enumerate(work) for _ in loads]

    def load(n):
        rows = flat[n].shape[0]
        return pltpu.make_async_copy(
            flat[n], stage.at[n % SLOTS, pl.ds(0, rows)], load_sem.at[n % SLOTS]
        )

    ahead = 0
    while ahead < min(SLOTS, count):
        load(ahead).start()
        ahead += 1
    order[...] = swapped()

    barrier = pltpu.get_barrier_semaphore()

    def greet(device):
        pl.semaphore_signal(barrier, inc=1, device_id=device, device_id_type=MESH)

    for level in range(levels):
        greet(partner(level))
    greet(sibling)

    for device in (lax.rem(seq + 2, 2 * chips), lax.rem(seq + 2 * chips - 2, 2 * chips)):
        greet({"seq": device})
    pl.semaphore_wait(barrier, levels + 3)
    swap_out(0, mixed).start()
    for t, (loads, run) in enumerate(work):
        while ahead < count and (ahead < SLOTS or owner[ahead - SLOTS] < t):
            load(ahead).start()
            ahead += 1
        first, last = spans[t]
        for n in range(first, last):
            load(n).wait()
        run([stage.at[n % SLOTS, pl.ds(0, flat[n].shape[0])] for n in range(first, last)])
    settle()
    drain(0)
    for g in range(len(groups)):
        finish_sends(g)
    for b in (len(blocks) - 2, len(blocks) - 1):
        sibling_copy(b).wait_send()
    for step in range(levels):
        swap_out(step, mixed).wait_send()
    swap_back(levels - 1).wait_send()


def after_scan(z, z_mates, e, mixed, gate_pre, drive_grad, entering, leaving, switch, scale):
    levels = len(z)
    tokens, width = mixed.shape
    seq = lax.axis_size("seq")
    chips = seq // 2
    groups, blocks = 1 + 2 * levels, 1 + 4 * levels
    rows = 2 * width // seq
    hops = groups * (chips - 1) * 2
    hbm = pl.BlockSpec(memory_space=pl.ANY)
    dma = pltpu.SemaphoreType.DMA
    args = [*z, *z_mates, *e, mixed, gate_pre, drive_grad, entering, leaving, switch]
    square = width * width
    count = 2 * tokens * square * (4 * levels + 1 + 4 * levels + 1)
    results = pl.pallas_call(
        functools.partial(after_kernel, levels, chips, scale),
        in_specs=[hbm] * len(args),
        out_specs=[pl.BlockSpec(memory_space=pltpu.VMEM)] * 5,
        out_shape=[
            pltpu.VMEM((tokens, width), BF16),
            pltpu.VMEM((tokens, width), BF16),
            pltpu.VMEM((levels, rows, width), F32),
            pltpu.VMEM((levels, rows, width), F32),
            pltpu.VMEM((rows // 2, width), F32),
        ],
        scratch_shapes=[
            pltpu.VMEM((SLOTS, max(tokens, width), width), BF16),
            pltpu.VMEM((2, 2, width // 2, width), BF16),
            pltpu.VMEM((2 * levels, width, width), BF16),
            pltpu.VMEM((width // 2, width), BF16),
            pltpu.VMEM((2 * levels, chips - 1, rows, width), BF16),
            pltpu.VMEM((2 * levels, chips - 1, rows, width), BF16),
            pltpu.VMEM((chips - 1, rows // 2, width), BF16),
            pltpu.VMEM((chips - 1, rows // 2, width), BF16),
            pltpu.VMEM((levels, tokens, width), BF16),
            pltpu.VMEM((levels, tokens, width), BF16),
            pltpu.VMEM((levels - 1, tokens, width), BF16),
            pltpu.VMEM((levels - 1, tokens, width), BF16),
            pltpu.VMEM((tokens, width), BF16),
            pltpu.VMEM((CHUNK, CHUNK), BF16),
            dma((SLOTS,)), dma((blocks,)), dma((blocks,)),
            dma((hops,)), dma((hops,)), dma((hops,)), dma((hops,)),
            dma((2 * levels,)), dma((2 * levels,)),
        ],
        compiler_params=pltpu.CompilerParams(
            collective_id=0, has_side_effects=True, vmem_limit_bytes=52 << 20
        ),
        cost_estimate=pl.CostEstimate(
            flops=count, bytes_accessed=60 * tokens * width, transcendentals=0
        ),
        name="after_scan",
    )(*args)
    return pl.pallas_call(
        hand_over,
        in_specs=[pl.BlockSpec(memory_space=pltpu.VMEM)] * 5,
        out_specs=[hbm] * 5,
        out_shape=[jax.ShapeDtypeStruct(r.shape, r.dtype) for r in results],
        scratch_shapes=[dma((5,))],
        compiler_params=pltpu.CompilerParams(vmem_limit_bytes=1 << 20),
        name="hand_over",
    )(*results)


def hand_over(*refs):
    copies = [
        pltpu.make_async_copy(refs[n], refs[5 + n], refs[10].at[n]) for n in range(5)
    ]
    for copy in copies:
        copy.start()
    for copy in copies:
        copy.wait()


def shards(
    layer_source,
    entering,
    switch,
    leaving,
    channel_persistence,
    position_boosts,
    result_cotangent,
):
    scale = float(layer_source.shape[0] * lax.axis_size("seq")) ** (-0.5)
    z, z_mates, e, mixed, gate_pre_grad, drive_grad = before_scan(
        layer_source, result_cotangent, entering, leaving, switch,
        channel_persistence, position_boosts,
    )
    return after_scan(
        z, z_mates, e, mixed, gate_pre_grad, drive_grad, entering, leaving, switch, scale
    )


def solution(mesh):
    placed = (
        P("seq", "chan"),
        P(None, "chan", None),
        P("chan", None),
        P(None, "chan", None),
        P("chan"),
        P("seq"),
        P("seq", "chan"),
    )
    return jax.shard_map(
        shards,
        mesh=mesh,
        in_specs=placed,
        out_specs=(
            P("seq", "chan"),
            P("seq", "chan"),
            P(None, ("chan", "seq"), None),
            P(None, ("chan", "seq"), None),
            P(("chan", "seq"), None),
        ),
        check_vma=False,
    )
```

```python
import functools

import jax
import jax.numpy as jnp
from jax import lax
from jax.experimental import pallas as pl
from jax.experimental.pallas import tpu as pltpu
from jax.sharding import PartitionSpec as P

LANES = 128
MESH = pl.DeviceIdType.MESH
F32, BF16 = jnp.float32, jnp.bfloat16


def dot(left, right):
    return jnp.dot(left, right, preferred_element_type=jnp.float32)


def dot_rows(left, right):
    return lax.dot_general(
        left, right, (((0,), (0,)), ((), ())), preferred_element_type=jnp.float32
    )


def dot_trans(left, right):
    return lax.dot_general(
        left, right, (((1,), (1,)), ((), ())), preferred_element_type=jnp.float32
    )


SEGMENT = 16
CHUNK = SEGMENT * SEGMENT


def swapped():
    row = lax.broadcasted_iota(jnp.int32, (CHUNK, CHUNK), 0)
    col = lax.broadcasted_iota(jnp.int32, (CHUNK, CHUNK), 1)
    return (lax.rem(row, SEGMENT) * SEGMENT + lax.div(row, SEGMENT) == col).astype(BF16)


def before_kernel(levels, devices, *refs):
    it = iter(refs)
    source, cotangent, entering, leaving, switch, keep, position = (next(it) for _ in range(7))
    z_out = [next(it) for _ in range(levels)]
    m_out = [next(it) for _ in range(levels)]
    e_out = [next(it) for _ in range(levels)]
    mixed_out, gate_out, drive_out = (next(it) for _ in range(3))
    w_in, w_out, w_gate, zs, ms, es, shares, sent = (next(it) for _ in range(8))
    drive, out_cot, gate, mixed, gate_pre, drive_grad = (next(it) for _ in range(6))
    onward, homeward, ends, backs, carry, order, plain, boosts = (next(it) for _ in range(8))
    load_sem, chunk_sem, z_send, z_recv, s_send, s_recv, t_send, t_recv, store_sem = (
        next(it) for _ in range(9)
    )
    tokens, width = drive.shape
    chunks = tokens // CHUNK
    seq, chan = lax.axis_index("seq"), lax.axis_index("chan")

    def partner(level):
        d = 1 << level
        bit = lax.rem(lax.div(chan, d), 2)
        return {"chan": chan + d * (1 - 2 * bit)}

    def rows(c):
        return pl.ds(c * CHUNK, CHUNK)

    def load(n, source, target):
        return pltpu.make_async_copy(source, target, load_sem.at[n])

    def weight(weights, into, level, part, n):
        at = pl.ds(part * width, width)
        return load(n, weights.at[level, at], into.at[level, at])

    def load_z(c):
        return pltpu.make_async_copy(source.at[rows(c)], zs.at[0, rows(c)], chunk_sem.at[c])

    def load_e(c):
        return pltpu.make_async_copy(
            cotangent.at[rows(c)], es.at[levels - 1, rows(c)], chunk_sem.at[chunks + c]
        )

    load_w = {}
    wanted = []
    for step in range(levels):
        down = levels - 1 - step
        wanted += [("out", down, 1), ("in", step, 0), ("in", step, 1), ("out", down, 0)]
    for n, (which, level, part) in enumerate(wanted):
        load_w[which, level, part] = weight(
            *((entering, w_in) if which == "in" else (leaving, w_out)), level, part, n
        )
    load_gate = load(4 * levels, switch, w_gate)
    arrived = set()

    def need(*key):
        if key not in arrived:
            arrived.add(key)
            load_w[key].wait()

    for c in reversed(range(chunks)):
        load_e(c).start()
        if c == chunks - 1:
            load_w[wanted[0]].start()
    for c in range(chunks):
        load_z(c).start()
    load_gate.start()
    for key in wanted[1:]:
        load_w[key].start()

    onward[...] = jnp.zeros_like(onward)
    homeward[...] = jnp.zeros_like(homeward)
    barrier = pltpu.get_barrier_semaphore()
    for level in range(levels):
        pl.semaphore_signal(barrier, inc=1, device_id=partner(level), device_id_type=MESH)
    for k in range(1, devices):
        pl.semaphore_signal(
            barrier, inc=1, device_id={"seq": lax.rem(seq + k, devices)}, device_id_type=MESH
        )
    order[...] = swapped()
    for n in range(0, tokens, LANES):
        plain[n : n + LANES, :] = jnp.broadcast_to(
            position[:, n : n + LANES], (LANES, LANES)
        ).T
    for c in range(chunks):
        for i in range(SEGMENT):
            boosts[pl.ds(c * CHUNK + i * SEGMENT, SEGMENT), :] = plain[
                pl.ds(c * CHUNK + i, SEGMENT, stride=SEGMENT), :
            ]
    pl.semaphore_wait(barrier, levels + devices - 1)

    def remote(source, target, send, recv, device):
        return pltpu.make_async_remote_copy(
            src_ref=source, dst_ref=target, send_sem=send, recv_sem=recv,
            device_id=device, device_id_type=MESH,
        )

    def send_z(level, c):
        n = level * chunks + c
        block = source.at[rows(c)] if level == 0 else zs.at[level, rows(c)]
        return remote(block, ms.at[level, rows(c)], z_send.at[n], z_recv.at[n], partner(level))

    def send_share(level, c):
        n = level * chunks + c
        return remote(
            sent.at[level, rows(c)], shares.at[level, rows(c)],
            s_send.at[n], s_recv.at[n], partner(level),
        )

    held = width // LANES

    def pack(box, growth, end):
        for q in range(held):
            at = slice(q * LANES, (q + 1) * LANES)
            box[seq, q : q + 1, :] = carry[growth : growth + 1, at]
            box[seq, held + q : held + q + 1, :] = carry[end : end + 1, at]

    def totals_copy(box, k, back):
        n = k - 1 + back * (devices - 1)
        there = seq - k if back else seq + k
        return remote(box.at[seq], box.at[seq], t_send.at[n], t_recv.at[n], {"seq": there})

    def each_total(box, back, run):
        for k in range(1, devices):
            @pl.when(seq - k >= 0 if back else seq + k < devices)
            def _(k=k):
                run(totals_copy(box, k, back))

    def depart(box, back):
        each_total(box, back, lambda copy: copy.start())

    def arrive(box, back):
        for k in range(1, devices):
            source = seq + k if back else seq - k

            @pl.when(source < devices if back else source >= 0)
            def _(k=k, source=source):
                n = k - 1 + back * (devices - 1)
                remote(
                    box.at[source], box.at[source], t_send.at[n], t_recv.at[n],
                    {"seq": source},
                ).wait_recv()

    for c in range(chunks):
        send_z(0, c).start()
    def in_order(ref, level, c):
        ref[level, rows(c), :] = dot(order[...], ref[level, rows(c), :]).astype(BF16)

    def share(level, c):
        need("out", level, 1)
        sent[level, rows(c), :] = dot_trans(
            es[level, rows(c), :], w_out[level, pl.ds(width, width), :]
        ).astype(BF16)
        send_share(level, c).start()

    for c in reversed(range(chunks)):
        load_e(c).wait()
        in_order(es, levels - 1, c)
        share(levels - 1, c)
    load_gate.wait()
    for c in range(chunks):
        load_z(c).wait()
        in_order(zs, 0, c)
        gate[rows(c), :] = jax.nn.sigmoid(dot(zs[0, rows(c), :], w_gate[...]))

    piece = min(256, width)

    def tile(c, i, lane):
        return pl.ds(c * CHUNK + i * SEGMENT, SEGMENT), pl.ds(lane, LANES)

    def for_lanes(run):
        @pl.loop(0, width // piece)
        def _(n):
            run([pl.multiple_of(n * piece, piece) + q for q in range(0, piece, LANES)])

    def lane_row(lane):
        lam = keep[:, pl.ds(lane, LANES)]
        return lam, jnp.sqrt(1.0 - lam * lam)

    def wide(row):
        return jnp.broadcast_to(row, (SEGMENT, LANES))

    def ends_forward(c):
        @for_lanes
        def _(lanes):
            for lane in lanes:
                at = pl.ds(lane, LANES)
                lam, scale = (wide(v) for v in lane_row(lane))
                state = jnp.zeros((SEGMENT, LANES), F32)
                p = jnp.ones((SEGMENT, LANES), F32)
                for i in range(SEGMENT):
                    r, at = tile(c, i, lane)
                    a = boosts[r, :] * lam
                    state = a * state + scale * drive[r, at].astype(F32)
                    p = a * p
                span = pl.ds(c * SEGMENT, SEGMENT)
                run = carry[0:1, at]
                grown = carry[1:2, at]
                starts, growths = [], []
                for s in range(SEGMENT):
                    starts.append(run)
                    growths.append(grown)
                    run = p[s : s + 1] * run + state[s : s + 1]
                    grown = p[s : s + 1] * grown
                ends[0, span, at] = jnp.concatenate(starts, axis=0)
                ends[1, span, at] = jnp.concatenate(growths, axis=0)
                carry[0:1, at] = run
                carry[1:2, at] = grown

    def ends_backward(c):
        @for_lanes
        def _(lanes):
            for lane in lanes:
                at = pl.ds(lane, LANES)
                lam = wide(lane_row(lane)[0])
                back = jnp.zeros((SEGMENT, LANES), F32)
                p = jnp.ones((SEGMENT, LANES), F32)
                for i in reversed(range(SEGMENT)):
                    r, at = tile(c, i, lane)
                    a = boosts[r, :] * lam
                    back = a * (out_cot[r, at] * gate[r, at] + back)
                    p = a * p
                span = pl.ds(c * SEGMENT, SEGMENT)
                run = carry[2:3, at]
                grown = carry[3:4, at]
                starts, growths = [None] * SEGMENT, [None] * SEGMENT
                for s in reversed(range(SEGMENT)):
                    starts[s] = run
                    growths[s] = grown
                    run = p[s : s + 1] * run + back[s : s + 1]
                    grown = p[s : s + 1] * grown
                backs[0, span, at] = jnp.concatenate(starts, axis=0)
                backs[1, span, at] = jnp.concatenate(growths, axis=0)
                carry[2:3, at] = run
                carry[3:4, at] = grown

    carry[...] = jnp.zeros_like(carry)
    carry[1:2, :] = jnp.ones((1, width), F32)
    carry[3:4, :] = jnp.ones((1, width), F32)

    stores = []

    def store(ref, out):
        copy = pltpu.make_async_copy(ref, out, store_sem.at[len(stores)])
        copy.start()
        stores.append(copy)

    top, bot = pl.ds(0, width), pl.ds(width, width)
    store(zs.at[0], z_out[0])
    store(es.at[levels - 1], e_out[levels - 1])
    for step in range(levels):
        down = levels - 1 - step
        def ahead(c):
            send_z(step, c).wait_recv()
            if step == 0:
                in_order(ms, 0, c)
            need("in", step, 0)
            need("in", step, 1)
            summed = (
                dot(zs[step, rows(c), :], w_in[step, top, :])
                + dot(ms[step, rows(c), :], w_in[step, bot, :])
            ).astype(BF16)
            if step + 1 < levels:
                zs[step + 1, rows(c), :] = summed
                send_z(step + 1, c).start()
            else:
                drive[rows(c), :] = summed
                ends_forward(c)

        def astern(c):
            send_share(down, c).wait_recv()
            need("out", down, 0)
            total = dot_trans(es[down, rows(c), :], w_out[down, top, :])
            total = total + shares[down, rows(c), :].astype(F32)
            if down > 0:
                es[down - 1, rows(c), :] = total.astype(BF16)
                share(down - 1, c)
            else:
                out_cot[rows(c), :] = total
                ends_backward(c)

        for n in range(chunks):
            if step == 0:
                ahead(n)
            astern(chunks - 1 - n)
            if down == 0 and n == chunks - 1:
                pack(homeward, 3, 2)
                depart(homeward, 1)
            if step > 0:
                ahead(n)
        store(ms.at[step], m_out[step])
        if step + 1 < levels:
            store(zs.at[step + 1], z_out[step + 1])
            store(es.at[down - 1], e_out[down - 1])

    pack(onward, 1, 0)
    depart(onward, 0)
    arrive(homeward, 1)
    b = jnp.zeros((held, LANES), F32)
    for k in reversed(range(devices)):
        b = jnp.where(k > seq, homeward[k, :held] * b + homeward[k, held : 2 * held], b)
    arrive(onward, 0)
    h = jnp.zeros((held, LANES), F32)
    for k in range(devices):
        h = jnp.where(k < seq, onward[k, :held] * h + onward[k, held : 2 * held], h)
    for q in range(held):
        at = slice(q * LANES, (q + 1) * LANES)
        carry[0:1, at] = h[q : q + 1]
        carry[2:3, at] = b[q : q + 1]

    for c in range(chunks):
        span = pl.ds(c * SEGMENT, SEGMENT)

        @for_lanes
        def _(lanes):
            for lane in lanes:
                at = pl.ds(lane, LANES)
                lam, scale = (wide(v) for v in lane_row(lane))
                state = ends[0, span, at] + ends[1, span, at] * wide(carry[0:1, at])
                back = backs[0, span, at] + backs[1, span, at] * wide(carry[2:3, at])
                for i in range(SEGMENT):
                    r, at = tile(c, i, lane)
                    state = boosts[r, :] * lam * state + scale * drive[r, at].astype(F32)
                    sig = gate[r, at]
                    product = state * sig
                    mixed[r, at] = product.astype(BF16)
                    gate_pre[r, at] = (out_cot[r, at] * product * (1.0 - sig)).astype(BF16)
                for i in reversed(range(SEGMENT)):
                    r, at = tile(c, i, lane)
                    total = out_cot[r, at] * gate[r, at] + back
                    drive_grad[r, at] = (scale * total).astype(BF16)
                    back = boosts[r, :] * lam * total

        for ref, out in ((mixed, mixed_out), (gate_pre, gate_out), (drive_grad, drive_out)):
            store(ref.at[rows(c)], out.at[rows(c)])

    for copy in stores:
        copy.wait()
    for level in range(levels):
        for c in range(chunks):
            send_z(level, c).wait_send()
            send_share(level, c).wait_send()
    each_total(onward, 0, lambda copy: copy.wait_send())
    each_total(homeward, 1, lambda copy: copy.wait_send())


def before_scan(source, cotangent, entering, leaving, switch, keep, boosts):
    levels = entering.shape[0]
    tokens, width = source.shape
    devices = lax.axis_size("seq")
    chunks = tokens // CHUNK
    hbm = pl.BlockSpec(memory_space=pl.ANY)
    vmem = pl.BlockSpec(memory_space=pltpu.VMEM)
    dma = pltpu.SemaphoreType.DMA
    block = jax.ShapeDtypeStruct((tokens, width), BF16)
    count = 3 * levels + 3
    segments = tokens // SEGMENT
    result = pl.pallas_call(
        functools.partial(before_kernel, levels, devices),
        in_specs=[hbm] * 5 + [vmem] * 2,
        out_specs=[hbm] * count,
        out_shape=[block] * count,
        scratch_shapes=[
            pltpu.VMEM((levels, 2 * width, width), BF16),
            pltpu.VMEM((levels, 2 * width, width), BF16),
            pltpu.VMEM((width, width), BF16),
            *[pltpu.VMEM((levels, tokens, width), BF16)] * 5,
            pltpu.VMEM((tokens, width), BF16),
            pltpu.VMEM((tokens, width), F32),
            pltpu.VMEM((tokens, width), F32),
            *[pltpu.VMEM((tokens, width), BF16)] * 3,
            *[pltpu.VMEM((devices, max(8, 2 * width // LANES), LANES), F32)] * 2,
            pltpu.VMEM((2, segments, width), F32),
            pltpu.VMEM((2, segments, width), F32),
            pltpu.VMEM((8, width), F32),
            pltpu.VMEM((CHUNK, CHUNK), BF16),
            pltpu.VMEM((tokens, LANES), F32),
            pltpu.VMEM((tokens, LANES), F32),
            dma((4 * levels + 1,)), dma((2 * chunks,)),
            *[dma((levels * chunks,))] * 4,
            *[dma((2 * (devices - 1),))] * 2,
            dma((3 * levels + 3 * chunks,)),
        ],
        compiler_params=pltpu.CompilerParams(
            collective_id=1, has_side_effects=True, vmem_limit_bytes=60 << 20
        ),
        cost_estimate=pl.CostEstimate(
            flops=2 * tokens * width * width * (4 * levels + 1),
            bytes_accessed=60 * tokens * width, transcendentals=tokens * width,
        ),
        name="before_scan",
    )(source, cotangent, entering, leaving, switch, keep[None, :], boosts[None, :])
    return (
        result[:levels], result[levels : 2 * levels], result[2 * levels : 3 * levels],
        *result[3 * levels :],
    )


SLOTS = 4


def after_kernel(levels, chips, scale, *refs):
    it = iter(refs)
    z = [next(it) for _ in range(levels)]
    zm = [next(it) for _ in range(levels)]
    e = [None] + [next(it) for _ in range(levels)]
    mixed, gate_pre, drive_grad, entering, leaving, switch = (next(it) for _ in range(6))
    layer_out, token_grads, in_grads, out_grads, gate_grads = (next(it) for _ in range(5))
    stage, part, sums, gate_sums, right, left, gate_right, gate_left = (next(it) for _ in range(8))
    mates, shares, outs, cots, sent, order = (next(it) for _ in range(6))
    load_sem, sib_send, sib_recv, right_send, right_recv, left_send, left_recv = (
        next(it) for _ in range(7)
    )
    swap_send, swap_recv = (next(it) for _ in range(2))

    tokens, width = mixed.shape
    half = width // 2
    seq, chan = lax.axis_index("seq"), lax.axis_index("chan")
    zi, core = lax.div(seq, 2), lax.rem(seq, 2)
    zo = chips - 1 - zi
    sibling = {"seq": seq + 1 - 2 * core}
    upper, lower = {"seq": seq + 2}, {"seq": seq - 2}

    def partner(level):
        d = 1 << level
        bit = lax.rem(lax.div(chan, d), 2)
        return {"chan": chan + d * (1 - 2 * bit)}

    def remote(source, target, send, recv, device):
        return pltpu.make_async_remote_copy(
            src_ref=source, dst_ref=target, send_sem=send, recv_sem=recv,
            device_id=device, device_id_type=MESH,
        )

    def swap_out(step, source):
        return remote(source, mates.at[step], swap_send.at[step], swap_recv.at[step], partner(step))

    def swap_back(step):
        n = levels + step
        return remote(
            sent, shares.at[step], swap_send.at[n], swap_recv.at[n], partner(levels - 1 - step)
        )

    groups = [(gate_grads, gate_sums, gate_right, gate_left)]
    for step in range(levels):
        for out in (in_grads.at[levels - 1 - step], out_grads.at[step]):
            n = len(groups) - 1
            groups.append((out, sums.at[n], right.at[n], left.at[n]))

    def hop(g, k, h, way):
        _, total, up, down = groups[g]
        rows = up.shape[1]
        cols = pl.ds(h * half, half)
        into = (up, down)[way]
        at = (0 if way else chips - k) if k > 0 else 0
        if way:
            first = total.at[pl.ds((k - 1) * rows, rows), cols]
            send, recv, device = left_send, left_recv, lower
        else:
            first = total.at[pl.ds((chips - k) * rows, rows), cols]
            send, recv, device = right_send, right_recv, upper
        n = (g * (chips - 1) + k - 1) * 2 + h

        def copy(source):
            return remote(source, into.at[k - 1, :, cols], send.at[n], recv.at[n], device)

        later = into.at[k - 2, :, cols] if k > 1 else None
        return copy, first, later

    def depart(g):
        for k in range(1, chips):
            for h in range(2):
                for way, place in ((0, zi), (1, zo)):
                    copy, first, _ = hop(g, k, h, way)

                    @pl.when(place == 0)
                    def _(copy=copy, first=first):
                        copy(first).start()

    def forward(g, k, h):
        for way, place in ((0, zi), (1, zo)):
            copy, _, later = hop(g, k, h, way)

            @pl.when((place >= 1) & (place <= k - 1))
            def _(copy=copy, later=later):
                copy(later).start()

    def finish_sends(g):
        for k in range(1, chips):
            for h in range(2):
                for way, place in ((0, zi), (1, zo)):
                    copy, first, _ = hop(g, k, h, way)

                    @pl.when(place <= k - 1)
                    def _(copy=copy, first=first):
                        copy(first).wait_send()

    def event(g, k, h):
        out, total, up, down = groups[g]
        rows = up.shape[1]
        cols = pl.ds(h * half, half)
        for way, place in ((0, zi), (1, zo)):
            copy, first, _ = hop(g, k, h, way)

            @pl.when((place >= 1) & (place <= k))
            def _(way=way, copy=copy, first=first):
                copy(first).wait_recv()
                if k < chips - 1:
                    shard = zi - 1 + chips - k
                    if way:
                        shard = chips - 1 - (zo - 1 + chips - k)
                    at = pl.ds(pl.multiple_of(shard * rows, rows), rows)
                    into = (up, down)[way]
                    into[k - 1, :, cols] = (
                        into[k - 1, :, cols].astype(F32) + total[at, cols].astype(F32)
                    ).astype(BF16)

        if k < chips - 1:
            forward(g, k + 1, h)
            return
        at = pl.ds(pl.multiple_of(zi * rows, rows), rows)
        out[:, cols] = total[at, cols].astype(F32) * scale

        @pl.when(zi > 0)
        def _():
            out[:, cols] += up[chips - 2, :, cols].astype(F32) * scale

        @pl.when(zo > 0)
        def _():
            out[:, cols] += down[chips - 2, :, cols].astype(F32) * scale

    blocks = []

    def sibling_copy(b):
        g, offset, slot = blocks[b]
        total = groups[g][1]
        return remote(
            part.at[slot, 1 - core], total.at[pl.ds(offset, half)],
            sib_send.at[b], sib_recv.at[b], sibling,
        )

    def grad(g, offset, left_ref, right_ref):
        b = len(blocks)
        blocks.append((g, offset, b % 2))
        slot = b % 2
        if b == 2:
            for i in range(gate_tiles):
                gate_copy(i).wait_send()
        elif b > 2:
            sibling_copy(b - 2).wait_send()
        rows = groups[g][2].shape[1]
        tile = min(256, width)

        @pl.loop(0, width // tile)
        def _(i):
            cols = pl.ds(pl.multiple_of(i * tile, tile), tile)
            result = dot_rows(left_ref[:, cols], right_ref[...]).astype(BF16)
            pieces = tile // rows
            if pieces <= 1:
                per = rows // tile
                shard = lax.div(i, per)
                at = lax.div(shard, 2) * rows + lax.rem(i, per) * tile
                part[slot, lax.rem(shard, 2), pl.ds(pl.multiple_of(at, tile), tile), :] = result
            else:
                for q in range(pieces):
                    at = i * (tile // 2) + q // 2 * rows
                    part[slot, q % 2, pl.ds(pl.multiple_of(at, rows), rows), :] = (
                        result[q * rows : (q + 1) * rows]
                    )

        sibling_copy(b).start()
        return b

    def chip_sum(b):
        g, offset, slot = blocks[b]
        total = groups[g][1]
        sibling_copy(b).wait_recv()
        tile = min(128, half)

        @pl.loop(0, half // tile)
        def _(i):
            at = pl.multiple_of(i * tile, tile)
            there = pl.ds(offset + at, tile)
            total[there, :] = (
                total[there, :].astype(F32) + part[slot, core, pl.ds(at, tile), :].astype(F32)
            ).astype(BF16)

    work = []
    tall = CHUNK

    def tiles(store):
        @pl.loop(0, tokens // tall)
        def _(i):
            store(pl.ds(pl.multiple_of(i * tall, tall), tall))

    def task(loads, run):
        work.append((loads, run))

    def top(weights, level):
        return weights.at[level, pl.ds(0, width)]

    def bot(weights, level):
        return weights.at[level, pl.ds(width, width)]

    queue = []
    pending = []

    def settle():
        while pending:
            b, group_done = pending.pop(0)
            chip_sum(b)
            if group_done:
                g = blocks[b][0]
                depart(g)
                for k in range(1, chips):
                    for h in range(2):
                        queue.append((g, k, h))

    def pump(count):
        for _ in range(count):
            if queue:
                event(*queue.pop(0))

    def drain(keep):
        pump(max(len(queue) - keep, 0))

    gate_tile = min(256, width)
    gate_tiles = width // gate_tile
    gate_order = sorted(range(gate_tiles), key=lambda i: min(i, gate_tiles - 1 - i) * 2 + (i == 0))

    def gate_copy(i):
        at = pl.ds(i * (gate_tile // 2), gate_tile // 2)
        n = 1 + 4 * levels + i
        return remote(
            part.at[0, 1 - core, at], gate_sums.at[at], sib_send.at[n], sib_recv.at[n], sibling
        )

    def gate_tile_sum(i):
        gate_copy(i).wait_recv()
        at = pl.ds(i * (gate_tile // 2), gate_tile // 2)
        gate_sums[at, :] = (
            gate_sums[at, :].astype(F32) + part[0, core, at, :].astype(F32)
        ).astype(BF16)
        rows = gate_right.shape[1]
        per = gate_tile // (2 * rows)
        for q in range(per):
            for way, place in ((0, zi), (1, zo)):
                shard = i * per + (q if way else per - 1 - q)
                k = shard + 1 if way else chips - shard
                if k >= chips:
                    continue

                @pl.when(place == 0)
                def _(way=way, k=k):
                    for h in range(2):
                        copy, first, _ = hop(0, k, h, way)
                        copy(first).start()

    def gate_task():
        rows = gate_right.shape[1]

        def run(bufs):
            blocks.append((0, 0, 0))
            ahead = None
            for i in gate_order:
                result = dot_rows(
                    bufs[0][:, i * gate_tile : (i + 1) * gate_tile], bufs[1][...]
                ).astype(BF16)
                for q in range(gate_tile // rows):
                    at = i * (gate_tile // 2) + q // 2 * rows
                    part[0, q % 2, pl.ds(at, rows), :] = result[q * rows : (q + 1) * rows]
                gate_copy(i).start()
                if ahead is not None:
                    gate_tile_sum(ahead)
                ahead = i
            gate_tile_sum(ahead)
            for k in range(1, chips):
                for h in range(2):
                    queue.append((0, k, h))

        task([z[0], gate_pre], run)

    def grad_task(g, offset, left_ref, right_ref, last):
        fixed = [r for r in (left_ref, right_ref) if isinstance(r, tuple)]
        loads = [r[0] for r in fixed]

        def run(bufs):
            bufs = list(bufs)
            lhs = bufs.pop(0) if isinstance(left_ref, tuple) else left_ref
            rhs = bufs.pop(0) if isinstance(right_ref, tuple) else right_ref
            settle()
            pending.append((grad(g, offset, lhs, rhs), last))
            pump(1)

        task(loads, run)

    def hbm(ref):
        return (ref,)

    def share_task(step):
        down = levels - 1 - step
        loads = [bot(entering, down)]
        if step == 0:
            loads = [drive_grad] + loads

        def run(bufs):
            cot = bufs[0] if step == 0 else cots.at[step - 1]
            weight = bufs[-1]
            if step == 0:
                settle()
            if step > 0:
                swap_back(step - 1).wait_send()

            def store(at):
                sent[at, :] = dot_trans(cot[at, :], weight[...]).astype(BF16)

            tiles(store)
            swap_back(step).start()
            settle()
            pump(1)

        task(loads, run)

    def wait_task(fn, keep):
        def run(bufs):
            settle()
            drain(keep)
            fn()

        task([], run)

    def out_task(step):
        loads = [top(leaving, step), bot(leaving, step)]
        last = step == levels - 1
        if step == 0:
            loads.append(mixed)
        if last:
            loads.append(z[0])

        def run(bufs):
            held = bufs[2] if step == 0 else outs.at[step - 1]
            mate = mates.at[step]

            def store(at):
                total = dot(held[at, :], bufs[0][...]) + dot(mate[at, :], bufs[1][...])
                if last:
                    total = (bufs[-1][at, :].astype(F32) + total).astype(BF16)
                    layer_out[at, :] = dot(order[...], total).astype(BF16)
                else:
                    outs[step, at, :] = total.astype(BF16)

            tiles(store)
            if not last:
                swap_out(step + 1, outs.at[step]).start()
            settle()
            pump(1)

        task(loads, run)

    def back_task(step):
        down = levels - 1 - step
        last = step == levels - 1
        loads = [top(entering, down)]
        if step == 0:
            loads.append(drive_grad)
        if last:
            loads += [gate_pre, switch, e[levels]]

        def run(bufs):
            cot = bufs[1] if step == 0 else cots.at[step - 1]

            def store(at):
                total = dot_trans(cot[at, :], bufs[0][...]) + shares[step, at, :].astype(F32)
                if last:
                    total = total + dot_trans(bufs[-3][at, :], bufs[-2][...])
                    total = total + bufs[-1][at, :].astype(F32)
                    token_grads[at, :] = dot(order[...], total.astype(BF16)).astype(BF16)
                else:
                    cots[step, at, :] = total.astype(BF16)

            tiles(store)
            settle()
            pump(1)

        task(loads, run)

    gate_task()
    share_task(0)
    for step in range(levels):
        down = levels - 1 - step
        g = 1 + 2 * step
        cot = hbm(drive_grad) if step == 0 else cots.at[step - 1]
        held = hbm(mixed) if step == 0 else outs.at[step - 1]
        grad_task(g, 0, hbm(z[down]), cot, False)
        grad_task(g, half, hbm(zm[down]), cot, True)
        grad_task(g + 1, 0, held, hbm(e[step + 1]), False)
        wait_task(lambda step=step: swap_out(step, mixed).wait_recv(), 3)
        grad_task(g + 1, half, mates.at[step], hbm(e[step + 1]), True)
        out_task(step)
        wait_task(lambda step=step: swap_back(step).wait_recv(), 1 << 20)
        back_task(step)
        if step < levels - 1:
            share_task(step + 1)

    spans, count = [], 0
    for loads, _ in work:
        spans.append((count, count + len(loads)))
        count += len(loads)
    flat = [ref for loads, _ in work for ref in loads]
    owner = [t for t, (loads, _) in enumerate(work) for _ in loads]

    def load(n):
        rows = flat[n].shape[0]
        return pltpu.make_async_copy(
            flat[n], stage.at[n % SLOTS, pl.ds(0, rows)], load_sem.at[n % SLOTS]
        )

    ahead = 0
    while ahead < min(SLOTS, count):
        load(ahead).start()
        ahead += 1
    order[...] = swapped()

    barrier = pltpu.get_barrier_semaphore()

    def greet(device):
        pl.semaphore_signal(barrier, inc=1, device_id=device, device_id_type=MESH)

    for level in range(levels):
        greet(partner(level))
    greet(sibling)

    for device in (lax.rem(seq + 2, 2 * chips), lax.rem(seq + 2 * chips - 2, 2 * chips)):
        greet({"seq": device})
    pl.semaphore_wait(barrier, levels + 3)
    swap_out(0, mixed).start()
    for t, (loads, run) in enumerate(work):
        while ahead < count and (ahead < SLOTS or owner[ahead - SLOTS] < t):
            load(ahead).start()
            ahead += 1
        first, last = spans[t]
        for n in range(first, last):
            load(n).wait()
        run([stage.at[n % SLOTS, pl.ds(0, flat[n].shape[0])] for n in range(first, last)])
    settle()
    last = len(groups) - 1
    drain(2 * (chips - 1))
    for g in range(last):
        finish_sends(g)
    drain(0)
    finish_sends(last)
    for b in (len(blocks) - 2, len(blocks) - 1):
        sibling_copy(b).wait_send()
    for step in range(levels):
        swap_out(step, mixed).wait_send()
    swap_back(levels - 1).wait_send()


def after_scan(z, z_mates, e, mixed, gate_pre, drive_grad, entering, leaving, switch, scale):
    levels = len(z)
    tokens, width = mixed.shape
    seq = lax.axis_size("seq")
    chips = seq // 2
    groups, blocks = 1 + 2 * levels, 1 + 4 * levels + max(width // 256, 1)
    rows = 2 * width // seq
    hops = groups * (chips - 1) * 2
    hbm = pl.BlockSpec(memory_space=pl.ANY)
    dma = pltpu.SemaphoreType.DMA
    args = [*z, *z_mates, *e, mixed, gate_pre, drive_grad, entering, leaving, switch]
    square = width * width
    count = 2 * tokens * square * (4 * levels + 1 + 4 * levels + 1)
    results = pl.pallas_call(
        functools.partial(after_kernel, levels, chips, scale),
        in_specs=[hbm] * len(args),
        out_specs=[pl.BlockSpec(memory_space=pltpu.VMEM)] * 5,
        out_shape=[
            pltpu.VMEM((tokens, width), BF16),
            pltpu.VMEM((tokens, width), BF16),
            pltpu.VMEM((levels, rows, width), F32),
            pltpu.VMEM((levels, rows, width), F32),
            pltpu.VMEM((rows // 2, width), F32),
        ],
        scratch_shapes=[
            pltpu.VMEM((SLOTS, max(tokens, width), width), BF16),
            pltpu.VMEM((2, 2, width // 2, width), BF16),
            pltpu.VMEM((2 * levels, width, width), BF16),
            pltpu.VMEM((width // 2, width), BF16),
            pltpu.VMEM((2 * levels, chips - 1, rows, width), BF16),
            pltpu.VMEM((2 * levels, chips - 1, rows, width), BF16),
            pltpu.VMEM((chips - 1, rows // 2, width), BF16),
            pltpu.VMEM((chips - 1, rows // 2, width), BF16),
            pltpu.VMEM((levels, tokens, width), BF16),
            pltpu.VMEM((levels, tokens, width), BF16),
            pltpu.VMEM((levels - 1, tokens, width), BF16),
            pltpu.VMEM((levels - 1, tokens, width), BF16),
            pltpu.VMEM((tokens, width), BF16),
            pltpu.VMEM((CHUNK, CHUNK), BF16),
            dma((SLOTS,)), dma((blocks,)), dma((blocks,)),
            dma((hops,)), dma((hops,)), dma((hops,)), dma((hops,)),
            dma((2 * levels,)), dma((2 * levels,)),
        ],
        compiler_params=pltpu.CompilerParams(
            collective_id=0, has_side_effects=True, vmem_limit_bytes=52 << 20
        ),
        cost_estimate=pl.CostEstimate(
            flops=count, bytes_accessed=60 * tokens * width, transcendentals=0
        ),
        name="after_scan",
    )(*args)
    return pl.pallas_call(
        hand_over,
        in_specs=[pl.BlockSpec(memory_space=pltpu.VMEM)] * 5,
        out_specs=[hbm] * 5,
        out_shape=[jax.ShapeDtypeStruct(r.shape, r.dtype) for r in results],
        scratch_shapes=[dma((5,))],
        compiler_params=pltpu.CompilerParams(vmem_limit_bytes=1 << 20),
        name="hand_over",
    )(*results)


def hand_over(*refs):
    copies = [
        pltpu.make_async_copy(refs[n], refs[5 + n], refs[10].at[n]) for n in range(5)
    ]
    for copy in copies:
        copy.start()
    for copy in copies:
        copy.wait()


def shards(
    layer_source,
    entering,
    switch,
    leaving,
    channel_persistence,
    position_boosts,
    result_cotangent,
):
    scale = float(layer_source.shape[0] * lax.axis_size("seq")) ** (-0.5)
    z, z_mates, e, mixed, gate_pre_grad, drive_grad = before_scan(
        layer_source, result_cotangent, entering, leaving, switch,
        channel_persistence, position_boosts,
    )
    return after_scan(
        z, z_mates, e, mixed, gate_pre_grad, drive_grad, entering, leaving, switch, scale
    )


def solution(mesh):
    placed = (
        P("seq", "chan"),
        P(None, "chan", None),
        P("chan", None),
        P(None, "chan", None),
        P("chan"),
        P("seq"),
        P("seq", "chan"),
    )
    return jax.shard_map(
        shards,
        mesh=mesh,
        in_specs=placed,
        out_specs=(
            P("seq", "chan"),
            P("seq", "chan"),
            P(None, ("chan", "seq"), None),
            P(None, ("chan", "seq"), None),
            P(("chan", "seq"), None),
        ),
        check_vma=False,
    )
```

```python
import functools

import jax
import jax.numpy as jnp
from jax import lax
from jax.experimental import pallas as pl
from jax.experimental.pallas import tpu as pltpu
from jax.sharding import PartitionSpec as P

LANES = 128
MESH = pl.DeviceIdType.MESH
F32, BF16 = jnp.float32, jnp.bfloat16


def dot(left, right):
    return jnp.dot(left, right, preferred_element_type=jnp.float32)


def dot_rows(left, right):
    return lax.dot_general(
        left, right, (((0,), (0,)), ((), ())), preferred_element_type=jnp.float32
    )


def dot_trans(left, right):
    return lax.dot_general(
        left, right, (((1,), (1,)), ((), ())), preferred_element_type=jnp.float32
    )


SEGMENT = 16
CHUNK = SEGMENT * SEGMENT


def swapped():
    row = lax.broadcasted_iota(jnp.int32, (CHUNK, CHUNK), 0)
    col = lax.broadcasted_iota(jnp.int32, (CHUNK, CHUNK), 1)
    return (lax.rem(row, SEGMENT) * SEGMENT + lax.div(row, SEGMENT) == col).astype(BF16)


def before_kernel(levels, devices, *refs):
    it = iter(refs)
    source, cotangent, entering, leaving, switch, keep, position = (next(it) for _ in range(7))
    z_out = [next(it) for _ in range(levels)]
    m_out = [next(it) for _ in range(levels)]
    e_out = [next(it) for _ in range(levels)]
    mixed_out, gate_out, drive_out = (next(it) for _ in range(3))
    w_in, w_out, w_gate, zs, ms, es, shares, sent = (next(it) for _ in range(8))
    drive, out_cot, gate, mixed, gate_pre, drive_grad = (next(it) for _ in range(6))
    onward, homeward, ends, backs, carry, order, plain, boosts = (next(it) for _ in range(8))
    load_sem, chunk_sem, z_send, z_recv, s_send, s_recv, t_send, t_recv, store_sem = (
        next(it) for _ in range(9)
    )
    tokens, width = drive.shape
    chunks = tokens // CHUNK
    seq, chan = lax.axis_index("seq"), lax.axis_index("chan")

    def partner(level):
        d = 1 << level
        bit = lax.rem(lax.div(chan, d), 2)
        return {"chan": chan + d * (1 - 2 * bit)}

    def rows(c):
        return pl.ds(c * CHUNK, CHUNK)

    def load(n, source, target):
        return pltpu.make_async_copy(source, target, load_sem.at[n])

    def weight(weights, into, level, part, n):
        at = pl.ds(part * width, width)
        return load(n, weights.at[level, at], into.at[level, at])

    def load_z(c):
        return pltpu.make_async_copy(source.at[rows(c)], zs.at[0, rows(c)], chunk_sem.at[c])

    def load_e(c):
        return pltpu.make_async_copy(
            cotangent.at[rows(c)], es.at[levels - 1, rows(c)], chunk_sem.at[chunks + c]
        )

    load_w = {}
    wanted = []
    for step in range(levels):
        down = levels - 1 - step
        wanted += [("out", down, 1), ("in", step, 0), ("in", step, 1), ("out", down, 0)]
    for n, (which, level, part) in enumerate(wanted):
        load_w[which, level, part] = weight(
            *((entering, w_in) if which == "in" else (leaving, w_out)), level, part, n
        )
    load_gate = load(4 * levels, switch, w_gate)
    arrived = set()

    def need(*key):
        if key not in arrived:
            arrived.add(key)
            load_w[key].wait()

    for c in reversed(range(chunks)):
        load_e(c).start()
        if c == chunks - 1:
            load_w[wanted[0]].start()
    for c in range(chunks):
        load_z(c).start()
    load_gate.start()
    for key in wanted[1:]:
        load_w[key].start()

    onward[...] = jnp.zeros_like(onward)
    homeward[...] = jnp.zeros_like(homeward)
    barrier = pltpu.get_barrier_semaphore()
    for level in range(levels):
        pl.semaphore_signal(barrier, inc=1, device_id=partner(level), device_id_type=MESH)
    for k in range(1, devices):
        pl.semaphore_signal(
            barrier, inc=1, device_id={"seq": lax.rem(seq + k, devices)}, device_id_type=MESH
        )
    order[...] = swapped()
    pl.semaphore_wait(barrier, levels + devices - 1)

    def remote(source, target, send, recv, device):
        return pltpu.make_async_remote_copy(
            src_ref=source, dst_ref=target, send_sem=send, recv_sem=recv,
            device_id=device, device_id_type=MESH,
        )

    def send_z(level, c):
        n = level * chunks + c
        block = source.at[rows(c)] if level == 0 else zs.at[level, rows(c)]
        return remote(block, ms.at[level, rows(c)], z_send.at[n], z_recv.at[n], partner(level))

    def send_share(level, c):
        n = level * chunks + c
        return remote(
            sent.at[level, rows(c)], shares.at[level, rows(c)],
            s_send.at[n], s_recv.at[n], partner(level),
        )

    held = width // LANES

    def pack(box, growth, end):
        for q in range(held):
            at = slice(q * LANES, (q + 1) * LANES)
            box[seq, q : q + 1, :] = carry[growth : growth + 1, at]
            box[seq, held + q : held + q + 1, :] = carry[end : end + 1, at]

    def totals_copy(box, k, back):
        n = k - 1 + back * (devices - 1)
        there = seq - k if back else seq + k
        return remote(box.at[seq], box.at[seq], t_send.at[n], t_recv.at[n], {"seq": there})

    def each_total(box, back, run):
        for k in range(1, devices):
            @pl.when(seq - k >= 0 if back else seq + k < devices)
            def _(k=k):
                run(totals_copy(box, k, back))

    def depart(box, back):
        each_total(box, back, lambda copy: copy.start())

    def arrive(box, back):
        for k in range(1, devices):
            source = seq + k if back else seq - k

            @pl.when(source < devices if back else source >= 0)
            def _(k=k, source=source):
                n = k - 1 + back * (devices - 1)
                remote(
                    box.at[source], box.at[source], t_send.at[n], t_recv.at[n],
                    {"seq": source},
                ).wait_recv()

    for c in range(chunks):
        send_z(0, c).start()
    def in_order(ref, level, c):
        ref[level, rows(c), :] = dot(order[...], ref[level, rows(c), :]).astype(BF16)

    def share(level, c):
        need("out", level, 1)
        sent[level, rows(c), :] = dot_trans(
            es[level, rows(c), :], w_out[level, pl.ds(width, width), :]
        ).astype(BF16)
        send_share(level, c).start()

    for c in reversed(range(chunks)):
        load_e(c).wait()
        in_order(es, levels - 1, c)
        share(levels - 1, c)
    for n in range(0, tokens, LANES):
        plain[n : n + LANES, :] = jnp.broadcast_to(
            position[:, n : n + LANES], (LANES, LANES)
        ).T
    for c in range(chunks):
        for i in range(SEGMENT):
            boosts[pl.ds(c * CHUNK + i * SEGMENT, SEGMENT), :] = plain[
                pl.ds(c * CHUNK + i, SEGMENT, stride=SEGMENT), :
            ]
    load_gate.wait()
    for c in range(chunks):
        load_z(c).wait()
        in_order(zs, 0, c)
        gate[rows(c), :] = jax.nn.sigmoid(dot(zs[0, rows(c), :], w_gate[...]))

    piece = min(256, width)

    def tile(c, i, lane):
        return pl.ds(c * CHUNK + i * SEGMENT, SEGMENT), pl.ds(lane, LANES)

    def for_lanes(run):
        @pl.loop(0, width // piece)
        def _(n):
            run([pl.multiple_of(n * piece, piece) + q for q in range(0, piece, LANES)])

    def lane_row(lane):
        lam = keep[:, pl.ds(lane, LANES)]
        return lam, jnp.sqrt(1.0 - lam * lam)

    def wide(row):
        return jnp.broadcast_to(row, (SEGMENT, LANES))

    def ends_forward(c):
        @for_lanes
        def _(lanes):
            for lane in lanes:
                at = pl.ds(lane, LANES)
                lam, scale = (wide(v) for v in lane_row(lane))
                state = jnp.zeros((SEGMENT, LANES), F32)
                p = jnp.ones((SEGMENT, LANES), F32)
                for i in range(SEGMENT):
                    r, at = tile(c, i, lane)
                    a = boosts[r, :] * lam
                    state = a * state + scale * drive[r, at].astype(F32)
                    p = a * p
                span = pl.ds(c * SEGMENT, SEGMENT)
                run = carry[0:1, at]
                grown = carry[1:2, at]
                starts, growths = [], []
                for s in range(SEGMENT):
                    starts.append(run)
                    growths.append(grown)
                    run = p[s : s + 1] * run + state[s : s + 1]
                    grown = p[s : s + 1] * grown
                ends[0, span, at] = jnp.concatenate(starts, axis=0)
                ends[1, span, at] = jnp.concatenate(growths, axis=0)
                carry[0:1, at] = run
                carry[1:2, at] = grown

    def ends_backward(c):
        @for_lanes
        def _(lanes):
            for lane in lanes:
                at = pl.ds(lane, LANES)
                lam = wide(lane_row(lane)[0])
                back = jnp.zeros((SEGMENT, LANES), F32)
                p = jnp.ones((SEGMENT, LANES), F32)
                for i in reversed(range(SEGMENT)):
                    r, at = tile(c, i, lane)
                    a = boosts[r, :] * lam
                    back = a * (out_cot[r, at] * gate[r, at] + back)
                    p = a * p
                span = pl.ds(c * SEGMENT, SEGMENT)
                run = carry[2:3, at]
                grown = carry[3:4, at]
                starts, growths = [None] * SEGMENT, [None] * SEGMENT
                for s in reversed(range(SEGMENT)):
                    starts[s] = run
                    growths[s] = grown
                    run = p[s : s + 1] * run + back[s : s + 1]
                    grown = p[s : s + 1] * grown
                backs[0, span, at] = jnp.concatenate(starts, axis=0)
                backs[1, span, at] = jnp.concatenate(growths, axis=0)
                carry[2:3, at] = run
                carry[3:4, at] = grown

    carry[...] = jnp.zeros_like(carry)
    carry[1:2, :] = jnp.ones((1, width), F32)
    carry[3:4, :] = jnp.ones((1, width), F32)

    stores = []

    def store(ref, out):
        copy = pltpu.make_async_copy(ref, out, store_sem.at[len(stores)])
        copy.start()
        stores.append(copy)

    top, bot = pl.ds(0, width), pl.ds(width, width)
    store(zs.at[0], z_out[0])
    store(es.at[levels - 1], e_out[levels - 1])
    for step in range(levels):
        down = levels - 1 - step
        def ahead(c):
            send_z(step, c).wait_recv()
            if step == 0:
                in_order(ms, 0, c)
            need("in", step, 0)
            need("in", step, 1)
            summed = (
                dot(zs[step, rows(c), :], w_in[step, top, :])
                + dot(ms[step, rows(c), :], w_in[step, bot, :])
            ).astype(BF16)
            if step + 1 < levels:
                zs[step + 1, rows(c), :] = summed
                send_z(step + 1, c).start()
            else:
                drive[rows(c), :] = summed
                ends_forward(c)

        def astern(c):
            send_share(down, c).wait_recv()
            need("out", down, 0)
            total = dot_trans(es[down, rows(c), :], w_out[down, top, :])
            total = total + shares[down, rows(c), :].astype(F32)
            if down > 0:
                es[down - 1, rows(c), :] = total.astype(BF16)
                share(down - 1, c)
            else:
                out_cot[rows(c), :] = total
                ends_backward(c)

        for n in range(chunks):
            if step == 0:
                ahead(n)
            astern(chunks - 1 - n)
            if down == 0 and n == chunks - 1:
                pack(homeward, 3, 2)
                depart(homeward, 1)
            if step > 0:
                ahead(n)
        store(ms.at[step], m_out[step])
        if step + 1 < levels:
            store(zs.at[step + 1], z_out[step + 1])
            store(es.at[down - 1], e_out[down - 1])

    pack(onward, 1, 0)
    depart(onward, 0)
    arrive(homeward, 1)
    b = jnp.zeros((held, LANES), F32)
    for k in reversed(range(devices)):
        b = jnp.where(k > seq, homeward[k, :held] * b + homeward[k, held : 2 * held], b)
    arrive(onward, 0)
    h = jnp.zeros((held, LANES), F32)
    for k in range(devices):
        h = jnp.where(k < seq, onward[k, :held] * h + onward[k, held : 2 * held], h)
    for q in range(held):
        at = slice(q * LANES, (q + 1) * LANES)
        carry[0:1, at] = h[q : q + 1]
        carry[2:3, at] = b[q : q + 1]

    for c in range(chunks):
        span = pl.ds(c * SEGMENT, SEGMENT)

        @for_lanes
        def _(lanes):
            for lane in lanes:
                at = pl.ds(lane, LANES)
                lam, scale = (wide(v) for v in lane_row(lane))
                state = ends[0, span, at] + ends[1, span, at] * wide(carry[0:1, at])
                back = backs[0, span, at] + backs[1, span, at] * wide(carry[2:3, at])
                for i in range(SEGMENT):
                    r, at = tile(c, i, lane)
                    state = boosts[r, :] * lam * state + scale * drive[r, at].astype(F32)
                    sig = gate[r, at]
                    product = state * sig
                    mixed[r, at] = product.astype(BF16)
                    gate_pre[r, at] = (out_cot[r, at] * product * (1.0 - sig)).astype(BF16)
                for i in reversed(range(SEGMENT)):
                    r, at = tile(c, i, lane)
                    total = out_cot[r, at] * gate[r, at] + back
                    drive_grad[r, at] = (scale * total).astype(BF16)
                    back = boosts[r, :] * lam * total

        for ref, out in ((mixed, mixed_out), (gate_pre, gate_out), (drive_grad, drive_out)):
            store(ref.at[rows(c)], out.at[rows(c)])

    for copy in stores:
        copy.wait()
    for level in range(levels):
        for c in range(chunks):
            send_z(level, c).wait_send()
            send_share(level, c).wait_send()
    each_total(onward, 0, lambda copy: copy.wait_send())
    each_total(homeward, 1, lambda copy: copy.wait_send())


def before_scan(source, cotangent, entering, leaving, switch, keep, boosts):
    levels = entering.shape[0]
    tokens, width = source.shape
    devices = lax.axis_size("seq")
    chunks = tokens // CHUNK
    hbm = pl.BlockSpec(memory_space=pl.ANY)
    vmem = pl.BlockSpec(memory_space=pltpu.VMEM)
    dma = pltpu.SemaphoreType.DMA
    block = jax.ShapeDtypeStruct((tokens, width), BF16)
    count = 3 * levels + 3
    segments = tokens // SEGMENT
    result = pl.pallas_call(
        functools.partial(before_kernel, levels, devices),
        in_specs=[hbm] * 5 + [vmem] * 2,
        out_specs=[hbm] * count,
        out_shape=[block] * count,
        scratch_shapes=[
            pltpu.VMEM((levels, 2 * width, width), BF16),
            pltpu.VMEM((levels, 2 * width, width), BF16),
            pltpu.VMEM((width, width), BF16),
            *[pltpu.VMEM((levels, tokens, width), BF16)] * 5,
            pltpu.VMEM((tokens, width), BF16),
            pltpu.VMEM((tokens, width), F32),
            pltpu.VMEM((tokens, width), F32),
            *[pltpu.VMEM((tokens, width), BF16)] * 3,
            *[pltpu.VMEM((devices, max(8, 2 * width // LANES), LANES), F32)] * 2,
            pltpu.VMEM((2, segments, width), F32),
            pltpu.VMEM((2, segments, width), F32),
            pltpu.VMEM((8, width), F32),
            pltpu.VMEM((CHUNK, CHUNK), BF16),
            pltpu.VMEM((tokens, LANES), F32),
            pltpu.VMEM((tokens, LANES), F32),
            dma((4 * levels + 1,)), dma((2 * chunks,)),
            *[dma((levels * chunks,))] * 4,
            *[dma((2 * (devices - 1),))] * 2,
            dma((3 * levels + 3 * chunks,)),
        ],
        compiler_params=pltpu.CompilerParams(
            collective_id=1, has_side_effects=True, vmem_limit_bytes=60 << 20
        ),
        cost_estimate=pl.CostEstimate(
            flops=2 * tokens * width * width * (4 * levels + 1),
            bytes_accessed=60 * tokens * width, transcendentals=tokens * width,
        ),
        name="before_scan",
    )(source, cotangent, entering, leaving, switch, keep[None, :], boosts[None, :])
    return (
        result[:levels], result[levels : 2 * levels], result[2 * levels : 3 * levels],
        *result[3 * levels :],
    )


SLOTS = 4
PIECES = 4


def after_kernel(levels, chips, scale, *refs):
    it = iter(refs)
    z = [next(it) for _ in range(levels)]
    zm = [next(it) for _ in range(levels)]
    e = [None] + [next(it) for _ in range(levels)]
    mixed, gate_pre, drive_grad, entering, leaving, switch = (next(it) for _ in range(6))
    layer_out, token_grads, in_grads, out_grads, gate_grads = (next(it) for _ in range(5))
    stage, part, sums, gate_sums, right, left, gate_right, gate_left = (next(it) for _ in range(8))
    mates, shares, outs, cots, sent, order = (next(it) for _ in range(6))
    load_sem, sib_send, sib_recv, right_send, right_recv, left_send, left_recv = (
        next(it) for _ in range(7)
    )
    swap_send, swap_recv = (next(it) for _ in range(2))

    tokens, width = mixed.shape
    half = width // 2
    pieces = min(PIECES, width // LANES)
    piece = width // pieces
    seq, chan = lax.axis_index("seq"), lax.axis_index("chan")
    zi, core = lax.div(seq, 2), lax.rem(seq, 2)
    zo = chips - 1 - zi
    sibling = {"seq": seq + 1 - 2 * core}
    upper, lower = {"seq": seq + 2}, {"seq": seq - 2}

    def partner(level):
        d = 1 << level
        bit = lax.rem(lax.div(chan, d), 2)
        return {"chan": chan + d * (1 - 2 * bit)}

    def remote(source, target, send, recv, device):
        return pltpu.make_async_remote_copy(
            src_ref=source, dst_ref=target, send_sem=send, recv_sem=recv,
            device_id=device, device_id_type=MESH,
        )

    def swap_out(step, source):
        return remote(source, mates.at[step], swap_send.at[step], swap_recv.at[step], partner(step))

    def swap_back(step):
        n = levels + step
        return remote(
            sent, shares.at[step], swap_send.at[n], swap_recv.at[n], partner(levels - 1 - step)
        )

    groups = [(gate_grads, gate_sums, gate_right, gate_left)]
    for step in range(levels):
        for out in (in_grads.at[levels - 1 - step], out_grads.at[step]):
            n = len(groups) - 1
            groups.append((out, sums.at[n], right.at[n], left.at[n]))

    def hop(g, k, h, way):
        _, total, up, down = groups[g]
        rows = up.shape[1]
        cols = pl.ds(h * piece, piece)
        into = (up, down)[way]
        at = (0 if way else chips - k) if k > 0 else 0
        if way:
            first = total.at[pl.ds((k - 1) * rows, rows), cols]
            send, recv, device = left_send, left_recv, lower
        else:
            first = total.at[pl.ds((chips - k) * rows, rows), cols]
            send, recv, device = right_send, right_recv, upper
        n = (g * (chips - 1) + k - 1) * pieces + h

        def copy(source):
            return remote(source, into.at[k - 1, :, cols], send.at[n], recv.at[n], device)

        later = into.at[k - 2, :, cols] if k > 1 else None
        return copy, first, later

    def depart(g):
        for k in range(1, chips):
            for h in range(pieces):
                for way, place in ((0, zi), (1, zo)):
                    copy, first, _ = hop(g, k, h, way)

                    @pl.when(place == 0)
                    def _(copy=copy, first=first):
                        copy(first).start()

    def forward(g, k, h):
        for way, place in ((0, zi), (1, zo)):
            copy, _, later = hop(g, k, h, way)

            @pl.when((place >= 1) & (place <= k - 1))
            def _(copy=copy, later=later):
                copy(later).start()

    def finish_sends(g):
        for k in range(1, chips):
            for h in range(pieces):
                for way, place in ((0, zi), (1, zo)):
                    copy, first, _ = hop(g, k, h, way)

                    @pl.when(place <= k - 1)
                    def _(copy=copy, first=first):
                        copy(first).wait_send()

    def event(g, k, h):
        out, total, up, down = groups[g]
        rows = up.shape[1]
        cols = pl.ds(h * piece, piece)
        for way, place in ((0, zi), (1, zo)):
            copy, first, _ = hop(g, k, h, way)

            @pl.when((place >= 1) & (place <= k))
            def _(way=way, copy=copy, first=first):
                copy(first).wait_recv()
                if k < chips - 1:
                    shard = zi - 1 + chips - k
                    if way:
                        shard = chips - 1 - (zo - 1 + chips - k)
                    at = pl.ds(pl.multiple_of(shard * rows, rows), rows)
                    into = (up, down)[way]
                    into[k - 1, :, cols] = (
                        into[k - 1, :, cols].astype(F32) + total[at, cols].astype(F32)
                    ).astype(BF16)

        if k < chips - 1:
            forward(g, k + 1, h)
            return
        at = pl.ds(pl.multiple_of(zi * rows, rows), rows)
        out[:, cols] = total[at, cols].astype(F32) * scale

        @pl.when(zi > 0)
        def _():
            out[:, cols] += up[chips - 2, :, cols].astype(F32) * scale

        @pl.when(zo > 0)
        def _():
            out[:, cols] += down[chips - 2, :, cols].astype(F32) * scale

    blocks = []

    def sibling_copy(b):
        g, offset, slot = blocks[b]
        total = groups[g][1]
        return remote(
            part.at[slot, 1 - core], total.at[pl.ds(offset, half)],
            sib_send.at[b], sib_recv.at[b], sibling,
        )

    def grad(g, offset, left_ref, right_ref):
        b = len(blocks)
        blocks.append((g, offset, b % 2))
        slot = b % 2
        if b == 2:
            for i in range(gate_tiles):
                gate_copy(i).wait_send()
        elif b > 2:
            sibling_copy(b - 2).wait_send()
        rows = groups[g][2].shape[1]
        tile = min(256, width)

        @pl.loop(0, width // tile)
        def _(i):
            cols = pl.ds(pl.multiple_of(i * tile, tile), tile)
            result = dot_rows(left_ref[:, cols], right_ref[...]).astype(BF16)
            parts = tile // rows
            if parts <= 1:
                per = rows // tile
                shard = lax.div(i, per)
                at = lax.div(shard, 2) * rows + lax.rem(i, per) * tile
                part[slot, lax.rem(shard, 2), pl.ds(pl.multiple_of(at, tile), tile), :] = result
            else:
                for q in range(parts):
                    at = i * (tile // 2) + q // 2 * rows
                    part[slot, q % 2, pl.ds(pl.multiple_of(at, rows), rows), :] = (
                        result[q * rows : (q + 1) * rows]
                    )

        sibling_copy(b).start()
        return b

    def chip_sum(b):
        g, offset, slot = blocks[b]
        total = groups[g][1]
        sibling_copy(b).wait_recv()
        tile = min(128, half)

        @pl.loop(0, half // tile)
        def _(i):
            at = pl.multiple_of(i * tile, tile)
            there = pl.ds(offset + at, tile)
            total[there, :] = (
                total[there, :].astype(F32) + part[slot, core, pl.ds(at, tile), :].astype(F32)
            ).astype(BF16)

    work = []
    tall = CHUNK

    def tiles(store):
        @pl.loop(0, tokens // tall)
        def _(i):
            store(pl.ds(pl.multiple_of(i * tall, tall), tall))

    def task(loads, run):
        work.append((loads, run))

    def top(weights, level):
        return weights.at[level, pl.ds(0, width)]

    def bot(weights, level):
        return weights.at[level, pl.ds(width, width)]

    queue = []
    pending = []

    def settle():
        while pending:
            b, group_done = pending.pop(0)
            chip_sum(b)
            if group_done:
                g = blocks[b][0]
                depart(g)
                for k in range(1, chips):
                    for h in range(pieces):
                        queue.append((g, k, h))

    def pump(count):
        for _ in range(count):
            if queue:
                event(*queue.pop(0))

    def drain(keep):
        pump(max(len(queue) - keep, 0))

    gate_tile = min(256, width)
    gate_tiles = width // gate_tile
    gate_order = sorted(range(gate_tiles), key=lambda i: min(i, gate_tiles - 1 - i) * 2 + (i == 0))

    def gate_copy(i):
        at = pl.ds(i * (gate_tile // 2), gate_tile // 2)
        n = 1 + 4 * levels + i
        return remote(
            part.at[0, 1 - core, at], gate_sums.at[at], sib_send.at[n], sib_recv.at[n], sibling
        )

    def gate_tile_sum(i):
        gate_copy(i).wait_recv()
        at = pl.ds(i * (gate_tile // 2), gate_tile // 2)
        gate_sums[at, :] = (
            gate_sums[at, :].astype(F32) + part[0, core, at, :].astype(F32)
        ).astype(BF16)
        rows = gate_right.shape[1]
        per = gate_tile // (2 * rows)
        for q in range(per):
            for way, place in ((0, zi), (1, zo)):
                shard = i * per + (q if way else per - 1 - q)
                k = shard + 1 if way else chips - shard
                if k >= chips:
                    continue

                @pl.when(place == 0)
                def _(way=way, k=k):
                    for h in range(pieces):
                        copy, first, _ = hop(0, k, h, way)
                        copy(first).start()

    def gate_task():
        rows = gate_right.shape[1]

        def run(bufs):
            blocks.append((0, 0, 0))
            ahead = None
            for i in gate_order:
                result = dot_rows(
                    bufs[0][:, i * gate_tile : (i + 1) * gate_tile], bufs[1][...]
                ).astype(BF16)
                for q in range(gate_tile // rows):
                    at = i * (gate_tile // 2) + q // 2 * rows
                    part[0, q % 2, pl.ds(at, rows), :] = result[q * rows : (q + 1) * rows]
                gate_copy(i).start()
                if ahead is not None:
                    gate_tile_sum(ahead)
                ahead = i
            gate_tile_sum(ahead)
            for k in range(1, chips):
                for h in range(pieces):
                    queue.append((0, k, h))

        task([z[0], gate_pre], run)

    def grad_task(g, offset, left_ref, right_ref, last):
        fixed = [r for r in (left_ref, right_ref) if isinstance(r, tuple)]
        loads = [r[0] for r in fixed]

        def run(bufs):
            bufs = list(bufs)
            lhs = bufs.pop(0) if isinstance(left_ref, tuple) else left_ref
            rhs = bufs.pop(0) if isinstance(right_ref, tuple) else right_ref
            settle()
            pending.append((grad(g, offset, lhs, rhs), last))
            pump(1)

        task(loads, run)

    def hbm(ref):
        return (ref,)

    def share_task(step):
        down = levels - 1 - step
        loads = [bot(entering, down)]
        if step == 0:
            loads = [drive_grad] + loads

        def run(bufs):
            cot = bufs[0] if step == 0 else cots.at[step - 1]
            weight = bufs[-1]
            if step == 0:
                settle()
            if step > 0:
                swap_back(step - 1).wait_send()

            def store(at):
                sent[at, :] = dot_trans(cot[at, :], weight[...]).astype(BF16)

            tiles(store)
            swap_back(step).start()
            settle()
            pump(1)

        task(loads, run)

    def wait_task(fn, keep):
        def run(bufs):
            settle()
            drain(keep)
            fn()

        task([], run)

    def out_task(step):
        loads = [top(leaving, step), bot(leaving, step)]
        last = step == levels - 1
        if step == 0:
            loads.append(mixed)
        if last:
            loads.append(z[0])

        def run(bufs):
            held = bufs[2] if step == 0 else outs.at[step - 1]
            mate = mates.at[step]

            def store(at):
                total = dot(held[at, :], bufs[0][...]) + dot(mate[at, :], bufs[1][...])
                if last:
                    total = (bufs[-1][at, :].astype(F32) + total).astype(BF16)
                    layer_out[at, :] = dot(order[...], total).astype(BF16)
                else:
                    outs[step, at, :] = total.astype(BF16)

            tiles(store)
            if not last:
                swap_out(step + 1, outs.at[step]).start()
            settle()
            pump(1)

        task(loads, run)

    def back_task(step):
        down = levels - 1 - step
        last = step == levels - 1
        loads = [top(entering, down)]
        if step == 0:
            loads.append(drive_grad)
        if last:
            loads += [gate_pre, switch, e[levels]]

        def run(bufs):
            cot = bufs[1] if step == 0 else cots.at[step - 1]

            def store(at):
                total = dot_trans(cot[at, :], bufs[0][...]) + shares[step, at, :].astype(F32)
                if last:
                    total = total + dot_trans(bufs[-3][at, :], bufs[-2][...])
                    total = total + bufs[-1][at, :].astype(F32)
                    token_grads[at, :] = dot(order[...], total.astype(BF16)).astype(BF16)
                else:
                    cots[step, at, :] = total.astype(BF16)

            tiles(store)
            settle()
            pump(1)

        task(loads, run)

    gate_task()
    share_task(0)
    for step in range(levels):
        down = levels - 1 - step
        g = 1 + 2 * step
        cot = hbm(drive_grad) if step == 0 else cots.at[step - 1]
        held = hbm(mixed) if step == 0 else outs.at[step - 1]
        grad_task(g, 0, hbm(z[down]), cot, False)
        grad_task(g, half, hbm(zm[down]), cot, True)
        grad_task(g + 1, 0, held, hbm(e[step + 1]), False)
        wait_task(lambda step=step: swap_out(step, mixed).wait_recv(), 3)
        grad_task(g + 1, half, mates.at[step], hbm(e[step + 1]), True)
        out_task(step)
        wait_task(lambda step=step: swap_back(step).wait_recv(), 1 << 20)
        back_task(step)
        if step < levels - 1:
            share_task(step + 1)

    spans, count = [], 0
    for loads, _ in work:
        spans.append((count, count + len(loads)))
        count += len(loads)
    flat = [ref for loads, _ in work for ref in loads]
    owner = [t for t, (loads, _) in enumerate(work) for _ in loads]

    def load(n):
        rows = flat[n].shape[0]
        return pltpu.make_async_copy(
            flat[n], stage.at[n % SLOTS, pl.ds(0, rows)], load_sem.at[n % SLOTS]
        )

    ahead = 0
    while ahead < min(SLOTS, count):
        load(ahead).start()
        ahead += 1
    order[...] = swapped()

    barrier = pltpu.get_barrier_semaphore()

    def greet(device):
        pl.semaphore_signal(barrier, inc=1, device_id=device, device_id_type=MESH)

    for level in range(levels):
        greet(partner(level))
    greet(sibling)

    for device in (lax.rem(seq + 2, 2 * chips), lax.rem(seq + 2 * chips - 2, 2 * chips)):
        greet({"seq": device})
    pl.semaphore_wait(barrier, levels + 3)
    swap_out(0, mixed).start()
    for t, (loads, run) in enumerate(work):
        while ahead < count and (ahead < SLOTS or owner[ahead - SLOTS] < t):
            load(ahead).start()
            ahead += 1
        first, last = spans[t]
        for n in range(first, last):
            load(n).wait()
        run([stage.at[n % SLOTS, pl.ds(0, flat[n].shape[0])] for n in range(first, last)])
    settle()
    last = len(groups) - 1
    drain(pieces * (chips - 1))
    for g in range(last):
        finish_sends(g)
    drain(0)
    finish_sends(last)
    for b in (len(blocks) - 2, len(blocks) - 1):
        sibling_copy(b).wait_send()
    for step in range(levels):
        swap_out(step, mixed).wait_send()
    swap_back(levels - 1).wait_send()


def after_scan(z, z_mates, e, mixed, gate_pre, drive_grad, entering, leaving, switch, scale):
    levels = len(z)
    tokens, width = mixed.shape
    seq = lax.axis_size("seq")
    chips = seq // 2
    groups, blocks = 1 + 2 * levels, 1 + 4 * levels + max(width // 256, 1)
    rows = 2 * width // seq
    hops = groups * (chips - 1) * min(PIECES, width // LANES)
    hbm = pl.BlockSpec(memory_space=pl.ANY)
    dma = pltpu.SemaphoreType.DMA
    args = [*z, *z_mates, *e, mixed, gate_pre, drive_grad, entering, leaving, switch]
    square = width * width
    count = 2 * tokens * square * (4 * levels + 1 + 4 * levels + 1)
    results = pl.pallas_call(
        functools.partial(after_kernel, levels, chips, scale),
        in_specs=[hbm] * len(args),
        out_specs=[pl.BlockSpec(memory_space=pltpu.VMEM)] * 5,
        out_shape=[
            pltpu.VMEM((tokens, width), BF16),
            pltpu.VMEM((tokens, width), BF16),
            pltpu.VMEM((levels, rows, width), F32),
            pltpu.VMEM((levels, rows, width), F32),
            pltpu.VMEM((rows // 2, width), F32),
        ],
        scratch_shapes=[
            pltpu.VMEM((SLOTS, max(tokens, width), width), BF16),
            pltpu.VMEM((2, 2, width // 2, width), BF16),
            pltpu.VMEM((2 * levels, width, width), BF16),
            pltpu.VMEM((width // 2, width), BF16),
            pltpu.VMEM((2 * levels, chips - 1, rows, width), BF16),
            pltpu.VMEM((2 * levels, chips - 1, rows, width), BF16),
            pltpu.VMEM((chips - 1, rows // 2, width), BF16),
            pltpu.VMEM((chips - 1, rows // 2, width), BF16),
            pltpu.VMEM((levels, tokens, width), BF16),
            pltpu.VMEM((levels, tokens, width), BF16),
            pltpu.VMEM((levels - 1, tokens, width), BF16),
            pltpu.VMEM((levels - 1, tokens, width), BF16),
            pltpu.VMEM((tokens, width), BF16),
            pltpu.VMEM((CHUNK, CHUNK), BF16),
            dma((SLOTS,)), dma((blocks,)), dma((blocks,)),
            dma((hops,)), dma((hops,)), dma((hops,)), dma((hops,)),
            dma((2 * levels,)), dma((2 * levels,)),
        ],
        compiler_params=pltpu.CompilerParams(
            collective_id=0, has_side_effects=True, vmem_limit_bytes=52 << 20
        ),
        cost_estimate=pl.CostEstimate(
            flops=count, bytes_accessed=60 * tokens * width, transcendentals=0
        ),
        name="after_scan",
    )(*args)
    return pl.pallas_call(
        hand_over,
        in_specs=[pl.BlockSpec(memory_space=pltpu.VMEM)] * 5,
        out_specs=[hbm] * 5,
        out_shape=[jax.ShapeDtypeStruct(r.shape, r.dtype) for r in results],
        scratch_shapes=[dma((5,))],
        compiler_params=pltpu.CompilerParams(vmem_limit_bytes=1 << 20),
        name="hand_over",
    )(*results)


def hand_over(*refs):
    copies = [
        pltpu.make_async_copy(refs[n], refs[5 + n], refs[10].at[n]) for n in range(5)
    ]
    for copy in copies:
        copy.start()
    for copy in copies:
        copy.wait()


def shards(
    layer_source,
    entering,
    switch,
    leaving,
    channel_persistence,
    position_boosts,
    result_cotangent,
):
    scale = float(layer_source.shape[0] * lax.axis_size("seq")) ** (-0.5)
    z, z_mates, e, mixed, gate_pre_grad, drive_grad = before_scan(
        layer_source, result_cotangent, entering, leaving, switch,
        channel_persistence, position_boosts,
    )
    return after_scan(
        z, z_mates, e, mixed, gate_pre_grad, drive_grad, entering, leaving, switch, scale
    )


def solution(mesh):
    placed = (
        P("seq", "chan"),
        P(None, "chan", None),
        P("chan", None),
        P(None, "chan", None),
        P("chan"),
        P("seq"),
        P("seq", "chan"),
    )
    return jax.shard_map(
        shards,
        mesh=mesh,
        in_specs=placed,
        out_specs=(
            P("seq", "chan"),
            P("seq", "chan"),
            P(None, ("chan", "seq"), None),
            P(None, ("chan", "seq"), None),
            P(("chan", "seq"), None),
        ),
        check_vma=False,
    )
```

```python
import functools

import jax
import jax.numpy as jnp
from jax import lax
from jax.experimental import pallas as pl
from jax.experimental.pallas import tpu as pltpu
from jax.sharding import PartitionSpec as P

LANES = 128
MESH = pl.DeviceIdType.MESH
F32, BF16 = jnp.float32, jnp.bfloat16


def dot(left, right):
    return jnp.dot(left, right, preferred_element_type=jnp.float32)


def dot_rows(left, right):
    return lax.dot_general(
        left, right, (((0,), (0,)), ((), ())), preferred_element_type=jnp.float32
    )


def dot_trans(left, right):
    return lax.dot_general(
        left, right, (((1,), (1,)), ((), ())), preferred_element_type=jnp.float32
    )


SEGMENT = 16
CHUNK = SEGMENT * SEGMENT


def swapped():
    row = lax.broadcasted_iota(jnp.int32, (CHUNK, CHUNK), 0)
    col = lax.broadcasted_iota(jnp.int32, (CHUNK, CHUNK), 1)
    return (lax.rem(row, SEGMENT) * SEGMENT + lax.div(row, SEGMENT) == col).astype(BF16)


def before_kernel(levels, devices, *refs):
    it = iter(refs)
    source, cotangent, entering, leaving, switch, keep, position = (next(it) for _ in range(7))
    z_out = [next(it) for _ in range(levels)]
    m_out = [next(it) for _ in range(levels)]
    e_out = [next(it) for _ in range(levels)]
    mixed_out, gate_out, drive_out = (next(it) for _ in range(3))
    w_in, w_out, w_gate, zs, ms, es, shares, sent = (next(it) for _ in range(8))
    drive, out_cot, gate, mixed, gate_pre, drive_grad = (next(it) for _ in range(6))
    onward, homeward, ends, backs, carry, order, plain, boosts = (next(it) for _ in range(8))
    load_sem, chunk_sem, z_send, z_recv, s_send, s_recv, t_send, t_recv, store_sem = (
        next(it) for _ in range(9)
    )
    tokens, width = drive.shape
    chunks = tokens // CHUNK
    seq, chan = lax.axis_index("seq"), lax.axis_index("chan")

    def partner(level):
        d = 1 << level
        bit = lax.rem(lax.div(chan, d), 2)
        return {"chan": chan + d * (1 - 2 * bit)}

    def rows(c):
        return pl.ds(c * CHUNK, CHUNK)

    def load(n, source, target):
        return pltpu.make_async_copy(source, target, load_sem.at[n])

    def weight(weights, into, level, part, n):
        at = pl.ds(part * width, width)
        return load(n, weights.at[level, at], into.at[level, at])

    def load_z(c):
        return pltpu.make_async_copy(source.at[rows(c)], zs.at[0, rows(c)], chunk_sem.at[c])

    def load_e(c):
        return pltpu.make_async_copy(
            cotangent.at[rows(c)], es.at[levels - 1, rows(c)], chunk_sem.at[chunks + c]
        )

    load_w = {}
    wanted = []
    for step in range(levels):
        down = levels - 1 - step
        wanted += [("out", down, 1), ("in", step, 0), ("in", step, 1), ("out", down, 0)]
    for n, (which, level, part) in enumerate(wanted):
        load_w[which, level, part] = weight(
            *((entering, w_in) if which == "in" else (leaving, w_out)), level, part, n
        )
    load_gate = load(4 * levels, switch, w_gate)
    arrived = set()

    def need(*key):
        if key not in arrived:
            arrived.add(key)
            load_w[key].wait()

    for c in reversed(range(chunks)):
        load_e(c).start()
        if c == chunks - 1:
            load_w[wanted[0]].start()
    for c in range(chunks):
        load_z(c).start()
    load_gate.start()
    for key in wanted[1:]:
        load_w[key].start()

    onward[...] = jnp.zeros_like(onward)
    homeward[...] = jnp.zeros_like(homeward)
    barrier = pltpu.get_barrier_semaphore()
    for level in range(levels):
        pl.semaphore_signal(barrier, inc=1, device_id=partner(level), device_id_type=MESH)
    for k in range(1, devices):
        pl.semaphore_signal(
            barrier, inc=1, device_id={"seq": lax.rem(seq + k, devices)}, device_id_type=MESH
        )
    order[...] = swapped()

    def remote(source, target, send, recv, device):
        return pltpu.make_async_remote_copy(
            src_ref=source, dst_ref=target, send_sem=send, recv_sem=recv,
            device_id=device, device_id_type=MESH,
        )

    def send_z(level, c):
        n = level * chunks + c
        block = source.at[rows(c)] if level == 0 else zs.at[level, rows(c)]
        return remote(block, ms.at[level, rows(c)], z_send.at[n], z_recv.at[n], partner(level))

    def send_share(level, c):
        n = level * chunks + c
        return remote(
            sent.at[level, rows(c)], shares.at[level, rows(c)],
            s_send.at[n], s_recv.at[n], partner(level),
        )

    held = width // LANES

    def pack(box, growth, end):
        for q in range(held):
            at = slice(q * LANES, (q + 1) * LANES)
            box[seq, q : q + 1, :] = carry[growth : growth + 1, at]
            box[seq, held + q : held + q + 1, :] = carry[end : end + 1, at]

    def totals_copy(box, k, back):
        n = k - 1 + back * (devices - 1)
        there = seq - k if back else seq + k
        return remote(box.at[seq], box.at[seq], t_send.at[n], t_recv.at[n], {"seq": there})

    def each_total(box, back, run):
        for k in range(1, devices):
            @pl.when(seq - k >= 0 if back else seq + k < devices)
            def _(k=k):
                run(totals_copy(box, k, back))

    def depart(box, back):
        each_total(box, back, lambda copy: copy.start())

    def arrive(box, back):
        for k in range(1, devices):
            source = seq + k if back else seq - k

            @pl.when(source < devices if back else source >= 0)
            def _(k=k, source=source):
                n = k - 1 + back * (devices - 1)
                remote(
                    box.at[source], box.at[source], t_send.at[n], t_recv.at[n],
                    {"seq": source},
                ).wait_recv()

    def in_order(ref, level, c):
        ref[level, rows(c), :] = dot(order[...], ref[level, rows(c), :]).astype(BF16)

    def share(level, c):
        need("out", level, 1)
        sent[level, rows(c), :] = dot_trans(
            es[level, rows(c), :], w_out[level, pl.ds(width, width), :]
        ).astype(BF16)
        if level == levels - 1 and c == chunks - 1:
            pl.semaphore_wait(barrier, levels + devices - 1)
            for n in range(chunks):
                send_z(0, n).start()
        send_share(level, c).start()

    for c in reversed(range(chunks)):
        load_e(c).wait()
        in_order(es, levels - 1, c)
        share(levels - 1, c)
    for n in range(0, tokens, LANES):
        plain[n : n + LANES, :] = jnp.broadcast_to(
            position[:, n : n + LANES], (LANES, LANES)
        ).T
    for c in range(chunks):
        for i in range(SEGMENT):
            boosts[pl.ds(c * CHUNK + i * SEGMENT, SEGMENT), :] = plain[
                pl.ds(c * CHUNK + i, SEGMENT, stride=SEGMENT), :
            ]
    load_gate.wait()
    for c in range(chunks):
        load_z(c).wait()
        in_order(zs, 0, c)
        gate[rows(c), :] = jax.nn.sigmoid(dot(zs[0, rows(c), :], w_gate[...]))

    piece = min(256, width)

    def tile(c, i, lane):
        return pl.ds(c * CHUNK + i * SEGMENT, SEGMENT), pl.ds(lane, LANES)

    def for_lanes(run):
        @pl.loop(0, width // piece)
        def _(n):
            run([pl.multiple_of(n * piece, piece) + q for q in range(0, piece, LANES)])

    def lane_row(lane):
        lam = keep[:, pl.ds(lane, LANES)]
        return lam, jnp.sqrt(1.0 - lam * lam)

    def wide(row):
        return jnp.broadcast_to(row, (SEGMENT, LANES))

    def ends_forward(c):
        @for_lanes
        def _(lanes):
            for lane in lanes:
                at = pl.ds(lane, LANES)
                lam, scale = (wide(v) for v in lane_row(lane))
                state = jnp.zeros((SEGMENT, LANES), F32)
                p = jnp.ones((SEGMENT, LANES), F32)
                for i in range(SEGMENT):
                    r, at = tile(c, i, lane)
                    a = boosts[r, :] * lam
                    state = a * state + scale * drive[r, at].astype(F32)
                    p = a * p
                span = pl.ds(c * SEGMENT, SEGMENT)
                run = carry[0:1, at]
                grown = carry[1:2, at]
                starts, growths = [], []
                for s in range(SEGMENT):
                    starts.append(run)
                    growths.append(grown)
                    run = p[s : s + 1] * run + state[s : s + 1]
                    grown = p[s : s + 1] * grown
                ends[0, span, at] = jnp.concatenate(starts, axis=0)
                ends[1, span, at] = jnp.concatenate(growths, axis=0)
                carry[0:1, at] = run
                carry[1:2, at] = grown

    def ends_backward(c):
        @for_lanes
        def _(lanes):
            for lane in lanes:
                at = pl.ds(lane, LANES)
                lam = wide(lane_row(lane)[0])
                back = jnp.zeros((SEGMENT, LANES), F32)
                p = jnp.ones((SEGMENT, LANES), F32)
                for i in reversed(range(SEGMENT)):
                    r, at = tile(c, i, lane)
                    a = boosts[r, :] * lam
                    back = a * (out_cot[r, at] * gate[r, at] + back)
                    p = a * p
                span = pl.ds(c * SEGMENT, SEGMENT)
                run = carry[2:3, at]
                grown = carry[3:4, at]
                starts, growths = [None] * SEGMENT, [None] * SEGMENT
                for s in reversed(range(SEGMENT)):
                    starts[s] = run
                    growths[s] = grown
                    run = p[s : s + 1] * run + back[s : s + 1]
                    grown = p[s : s + 1] * grown
                backs[0, span, at] = jnp.concatenate(starts, axis=0)
                backs[1, span, at] = jnp.concatenate(growths, axis=0)
                carry[2:3, at] = run
                carry[3:4, at] = grown

    carry[...] = jnp.zeros_like(carry)
    carry[1:2, :] = jnp.ones((1, width), F32)
    carry[3:4, :] = jnp.ones((1, width), F32)

    stores = []

    def store(ref, out):
        copy = pltpu.make_async_copy(ref, out, store_sem.at[len(stores)])
        copy.start()
        stores.append(copy)

    top, bot = pl.ds(0, width), pl.ds(width, width)
    store(zs.at[0], z_out[0])
    store(es.at[levels - 1], e_out[levels - 1])
    for step in range(levels):
        down = levels - 1 - step
        def ahead(c):
            send_z(step, c).wait_recv()
            if step == 0:
                in_order(ms, 0, c)
            need("in", step, 0)
            need("in", step, 1)
            summed = (
                dot(zs[step, rows(c), :], w_in[step, top, :])
                + dot(ms[step, rows(c), :], w_in[step, bot, :])
            ).astype(BF16)
            if step + 1 < levels:
                zs[step + 1, rows(c), :] = summed
                send_z(step + 1, c).start()
            else:
                drive[rows(c), :] = summed
                ends_forward(c)

        def astern(c):
            send_share(down, c).wait_recv()
            need("out", down, 0)
            total = dot_trans(es[down, rows(c), :], w_out[down, top, :])
            total = total + shares[down, rows(c), :].astype(F32)
            if down > 0:
                es[down - 1, rows(c), :] = total.astype(BF16)
                share(down - 1, c)
            else:
                out_cot[rows(c), :] = total
                ends_backward(c)

        for n in range(chunks):
            if step == 0:
                ahead(n)
            astern(chunks - 1 - n)
            if down == 0 and n == chunks - 1:
                pack(homeward, 3, 2)
                depart(homeward, 1)
            if step > 0:
                ahead(n)
        store(ms.at[step], m_out[step])
        if step + 1 < levels:
            store(zs.at[step + 1], z_out[step + 1])
            store(es.at[down - 1], e_out[down - 1])

    pack(onward, 1, 0)
    depart(onward, 0)
    arrive(homeward, 1)
    b = jnp.zeros((held, LANES), F32)
    for k in reversed(range(devices)):
        b = jnp.where(k > seq, homeward[k, :held] * b + homeward[k, held : 2 * held], b)
    arrive(onward, 0)
    h = jnp.zeros((held, LANES), F32)
    for k in range(devices):
        h = jnp.where(k < seq, onward[k, :held] * h + onward[k, held : 2 * held], h)
    for q in range(held):
        at = slice(q * LANES, (q + 1) * LANES)
        carry[0:1, at] = h[q : q + 1]
        carry[2:3, at] = b[q : q + 1]

    for c in range(chunks):
        span = pl.ds(c * SEGMENT, SEGMENT)

        @for_lanes
        def _(lanes):
            for lane in lanes:
                at = pl.ds(lane, LANES)
                lam, scale = (wide(v) for v in lane_row(lane))
                state = ends[0, span, at] + ends[1, span, at] * wide(carry[0:1, at])
                back = backs[0, span, at] + backs[1, span, at] * wide(carry[2:3, at])
                for i in range(SEGMENT):
                    r, at = tile(c, i, lane)
                    state = boosts[r, :] * lam * state + scale * drive[r, at].astype(F32)
                    sig = gate[r, at]
                    product = state * sig
                    mixed[r, at] = product.astype(BF16)
                    gate_pre[r, at] = (out_cot[r, at] * product * (1.0 - sig)).astype(BF16)
                for i in reversed(range(SEGMENT)):
                    r, at = tile(c, i, lane)
                    total = out_cot[r, at] * gate[r, at] + back
                    drive_grad[r, at] = (scale * total).astype(BF16)
                    back = boosts[r, :] * lam * total

        for ref, out in ((mixed, mixed_out), (gate_pre, gate_out), (drive_grad, drive_out)):
            store(ref.at[rows(c)], out.at[rows(c)])

    for copy in stores:
        copy.wait()
    for level in range(levels):
        for c in range(chunks):
            send_z(level, c).wait_send()
            send_share(level, c).wait_send()
    each_total(onward, 0, lambda copy: copy.wait_send())
    each_total(homeward, 1, lambda copy: copy.wait_send())


def before_scan(source, cotangent, entering, leaving, switch, keep, boosts):
    levels = entering.shape[0]
    tokens, width = source.shape
    devices = lax.axis_size("seq")
    chunks = tokens // CHUNK
    hbm = pl.BlockSpec(memory_space=pl.ANY)
    vmem = pl.BlockSpec(memory_space=pltpu.VMEM)
    dma = pltpu.SemaphoreType.DMA
    block = jax.ShapeDtypeStruct((tokens, width), BF16)
    count = 3 * levels + 3
    segments = tokens // SEGMENT
    result = pl.pallas_call(
        functools.partial(before_kernel, levels, devices),
        in_specs=[hbm] * 5 + [vmem] * 2,
        out_specs=[hbm] * count,
        out_shape=[block] * count,
        scratch_shapes=[
            pltpu.VMEM((levels, 2 * width, width), BF16),
            pltpu.VMEM((levels, 2 * width, width), BF16),
            pltpu.VMEM((width, width), BF16),
            *[pltpu.VMEM((levels, tokens, width), BF16)] * 5,
            pltpu.VMEM((tokens, width), BF16),
            pltpu.VMEM((tokens, width), F32),
            pltpu.VMEM((tokens, width), F32),
            *[pltpu.VMEM((tokens, width), BF16)] * 3,
            *[pltpu.VMEM((devices, max(8, 2 * width // LANES), LANES), F32)] * 2,
            pltpu.VMEM((2, segments, width), F32),
            pltpu.VMEM((2, segments, width), F32),
            pltpu.VMEM((8, width), F32),
            pltpu.VMEM((CHUNK, CHUNK), BF16),
            pltpu.VMEM((tokens, LANES), F32),
            pltpu.VMEM((tokens, LANES), F32),
            dma((4 * levels + 1,)), dma((2 * chunks,)),
            *[dma((levels * chunks,))] * 4,
            *[dma((2 * (devices - 1),))] * 2,
            dma((3 * levels + 3 * chunks,)),
        ],
        compiler_params=pltpu.CompilerParams(
            collective_id=1, has_side_effects=True, vmem_limit_bytes=60 << 20
        ),
        cost_estimate=pl.CostEstimate(
            flops=2 * tokens * width * width * (4 * levels + 1),
            bytes_accessed=60 * tokens * width, transcendentals=tokens * width,
        ),
        name="before_scan",
    )(source, cotangent, entering, leaving, switch, keep[None, :], boosts[None, :])
    return (
        result[:levels], result[levels : 2 * levels], result[2 * levels : 3 * levels],
        *result[3 * levels :],
    )


SLOTS = 4
PIECES = 4


def after_kernel(levels, chips, scale, *refs):
    it = iter(refs)
    z = [next(it) for _ in range(levels)]
    zm = [next(it) for _ in range(levels)]
    e = [None] + [next(it) for _ in range(levels)]
    mixed, gate_pre, drive_grad, entering, leaving, switch = (next(it) for _ in range(6))
    layer_out, token_grads, in_grads, out_grads, gate_grads = (next(it) for _ in range(5))
    stage, part, sums, gate_sums, right, left, gate_right, gate_left = (next(it) for _ in range(8))
    mates, shares, outs, cots, sent, order = (next(it) for _ in range(6))
    load_sem, sib_send, sib_recv, right_send, right_recv, left_send, left_recv = (
        next(it) for _ in range(7)
    )
    swap_send, swap_recv = (next(it) for _ in range(2))

    tokens, width = mixed.shape
    half = width // 2
    pieces = min(PIECES, width // LANES)
    piece = width // pieces
    seq, chan = lax.axis_index("seq"), lax.axis_index("chan")
    zi, core = lax.div(seq, 2), lax.rem(seq, 2)
    zo = chips - 1 - zi
    sibling = {"seq": seq + 1 - 2 * core}
    upper, lower = {"seq": seq + 2}, {"seq": seq - 2}

    def partner(level):
        d = 1 << level
        bit = lax.rem(lax.div(chan, d), 2)
        return {"chan": chan + d * (1 - 2 * bit)}

    def remote(source, target, send, recv, device):
        return pltpu.make_async_remote_copy(
            src_ref=source, dst_ref=target, send_sem=send, recv_sem=recv,
            device_id=device, device_id_type=MESH,
        )

    def swap_out(step, source):
        return remote(source, mates.at[step], swap_send.at[step], swap_recv.at[step], partner(step))

    def swap_back(step):
        n = levels + step
        return remote(
            sent, shares.at[step], swap_send.at[n], swap_recv.at[n], partner(levels - 1 - step)
        )

    groups = [(gate_grads, gate_sums, gate_right, gate_left)]
    for step in range(levels):
        for out in (in_grads.at[levels - 1 - step], out_grads.at[step]):
            n = len(groups) - 1
            groups.append((out, sums.at[n], right.at[n], left.at[n]))

    def hop(g, k, h, way):
        _, total, up, down = groups[g]
        rows = up.shape[1]
        cols = pl.ds(h * piece, piece)
        into = (up, down)[way]
        at = (0 if way else chips - k) if k > 0 else 0
        if way:
            first = total.at[pl.ds((k - 1) * rows, rows), cols]
            send, recv, device = left_send, left_recv, lower
        else:
            first = total.at[pl.ds((chips - k) * rows, rows), cols]
            send, recv, device = right_send, right_recv, upper
        n = (g * (chips - 1) + k - 1) * pieces + h

        def copy(source):
            return remote(source, into.at[k - 1, :, cols], send.at[n], recv.at[n], device)

        later = into.at[k - 2, :, cols] if k > 1 else None
        return copy, first, later

    def depart(g):
        for k in range(1, chips):
            for h in range(pieces):
                for way, place in ((0, zi), (1, zo)):
                    copy, first, _ = hop(g, k, h, way)

                    @pl.when(place == 0)
                    def _(copy=copy, first=first):
                        copy(first).start()

    def forward(g, k, h):
        for way, place in ((0, zi), (1, zo)):
            copy, _, later = hop(g, k, h, way)

            @pl.when((place >= 1) & (place <= k - 1))
            def _(copy=copy, later=later):
                copy(later).start()

    def finish_sends(g):
        for k in range(1, chips):
            for h in range(pieces):
                for way, place in ((0, zi), (1, zo)):
                    copy, first, _ = hop(g, k, h, way)

                    @pl.when(place <= k - 1)
                    def _(copy=copy, first=first):
                        copy(first).wait_send()

    def event(g, k, h):
        out, total, up, down = groups[g]
        rows = up.shape[1]
        cols = pl.ds(h * piece, piece)
        for way, place in ((0, zi), (1, zo)):
            copy, first, _ = hop(g, k, h, way)

            @pl.when((place >= 1) & (place <= k))
            def _(way=way, copy=copy, first=first):
                copy(first).wait_recv()
                if k < chips - 1:
                    shard = zi - 1 + chips - k
                    if way:
                        shard = chips - 1 - (zo - 1 + chips - k)
                    at = pl.ds(pl.multiple_of(shard * rows, rows), rows)
                    into = (up, down)[way]
                    into[k - 1, :, cols] = (
                        into[k - 1, :, cols].astype(F32) + total[at, cols].astype(F32)
                    ).astype(BF16)

        if k < chips - 1:
            forward(g, k + 1, h)
            return
        at = pl.ds(pl.multiple_of(zi * rows, rows), rows)
        out[:, cols] = total[at, cols].astype(F32) * scale

        @pl.when(zi > 0)
        def _():
            out[:, cols] += up[chips - 2, :, cols].astype(F32) * scale

        @pl.when(zo > 0)
        def _():
            out[:, cols] += down[chips - 2, :, cols].astype(F32) * scale

    blocks = []

    def sibling_copy(b):
        g, offset, slot = blocks[b]
        total = groups[g][1]
        return remote(
            part.at[slot, 1 - core], total.at[pl.ds(offset, half)],
            sib_send.at[b], sib_recv.at[b], sibling,
        )

    def grad(g, offset, left_ref, right_ref):
        b = len(blocks)
        blocks.append((g, offset, b % 2))
        slot = b % 2
        if b == 2:
            for i in range(gate_tiles):
                gate_copy(i).wait_send()
        elif b > 2:
            sibling_copy(b - 2).wait_send()
        rows = groups[g][2].shape[1]
        tile = min(256, width)

        @pl.loop(0, width // tile)
        def _(i):
            cols = pl.ds(pl.multiple_of(i * tile, tile), tile)
            result = dot_rows(left_ref[:, cols], right_ref[...]).astype(BF16)
            parts = tile // rows
            if parts <= 1:
                per = rows // tile
                shard = lax.div(i, per)
                at = lax.div(shard, 2) * rows + lax.rem(i, per) * tile
                part[slot, lax.rem(shard, 2), pl.ds(pl.multiple_of(at, tile), tile), :] = result
            else:
                for q in range(parts):
                    at = i * (tile // 2) + q // 2 * rows
                    part[slot, q % 2, pl.ds(pl.multiple_of(at, rows), rows), :] = (
                        result[q * rows : (q + 1) * rows]
                    )

        sibling_copy(b).start()
        return b

    def chip_sum(b):
        g, offset, slot = blocks[b]
        total = groups[g][1]
        sibling_copy(b).wait_recv()
        tile = min(128, half)

        @pl.loop(0, half // tile)
        def _(i):
            at = pl.multiple_of(i * tile, tile)
            there = pl.ds(offset + at, tile)
            total[there, :] = (
                total[there, :].astype(F32) + part[slot, core, pl.ds(at, tile), :].astype(F32)
            ).astype(BF16)

    work = []
    tall = CHUNK

    def tiles(store):
        @pl.loop(0, tokens // tall)
        def _(i):
            store(pl.ds(pl.multiple_of(i * tall, tall), tall))

    def task(loads, run):
        work.append((loads, run))

    def top(weights, level):
        return weights.at[level, pl.ds(0, width)]

    def bot(weights, level):
        return weights.at[level, pl.ds(width, width)]

    queue = []
    pending = []

    def settle():
        while pending:
            b, group_done = pending.pop(0)
            chip_sum(b)
            if group_done:
                g = blocks[b][0]
                depart(g)
                for k in range(1, chips):
                    for h in range(pieces):
                        queue.append((g, k, h))

    def pump(count):
        for _ in range(count):
            if queue:
                event(*queue.pop(0))

    def drain(keep):
        pump(max(len(queue) - keep, 0))

    gate_tile = min(256, width)
    gate_tiles = width // gate_tile
    gate_order = sorted(range(gate_tiles), key=lambda i: min(i, gate_tiles - 1 - i) * 2 + (i == 0))

    def gate_copy(i):
        at = pl.ds(i * (gate_tile // 2), gate_tile // 2)
        n = 1 + 4 * levels + i
        return remote(
            part.at[0, 1 - core, at], gate_sums.at[at], sib_send.at[n], sib_recv.at[n], sibling
        )

    def gate_tile_sum(i):
        gate_copy(i).wait_recv()
        at = pl.ds(i * (gate_tile // 2), gate_tile // 2)
        gate_sums[at, :] = (
            gate_sums[at, :].astype(F32) + part[0, core, at, :].astype(F32)
        ).astype(BF16)
        rows = gate_right.shape[1]
        per = gate_tile // (2 * rows)
        for q in range(per):
            for way, place in ((0, zi), (1, zo)):
                shard = i * per + (q if way else per - 1 - q)
                k = shard + 1 if way else chips - shard
                if k >= chips:
                    continue

                @pl.when(place == 0)
                def _(way=way, k=k):
                    for h in range(pieces):
                        copy, first, _ = hop(0, k, h, way)
                        copy(first).start()

    def gate_task():
        rows = gate_right.shape[1]

        def run(bufs):
            blocks.append((0, 0, 0))
            ahead = None
            for i in gate_order:
                result = dot_rows(
                    bufs[0][:, i * gate_tile : (i + 1) * gate_tile], bufs[1][...]
                ).astype(BF16)
                for q in range(gate_tile // rows):
                    at = i * (gate_tile // 2) + q // 2 * rows
                    part[0, q % 2, pl.ds(at, rows), :] = result[q * rows : (q + 1) * rows]
                gate_copy(i).start()
                if ahead is not None:
                    gate_tile_sum(ahead)
                ahead = i
            gate_tile_sum(ahead)
            for k in range(1, chips):
                for h in range(pieces):
                    queue.append((0, k, h))

        task([z[0], gate_pre], run)

    def grad_task(g, offset, left_ref, right_ref, last):
        fixed = [r for r in (left_ref, right_ref) if isinstance(r, tuple)]
        loads = [r[0] for r in fixed]

        def run(bufs):
            bufs = list(bufs)
            lhs = bufs.pop(0) if isinstance(left_ref, tuple) else left_ref
            rhs = bufs.pop(0) if isinstance(right_ref, tuple) else right_ref
            settle()
            pending.append((grad(g, offset, lhs, rhs), last))
            pump(1)

        task(loads, run)

    def hbm(ref):
        return (ref,)

    def share_task(step):
        down = levels - 1 - step
        loads = [bot(entering, down)]
        if step == 0:
            loads = [drive_grad] + loads

        def run(bufs):
            cot = bufs[0] if step == 0 else cots.at[step - 1]
            weight = bufs[-1]
            if step == 0:
                settle()
            if step > 0:
                swap_back(step - 1).wait_send()

            def store(at):
                sent[at, :] = dot_trans(cot[at, :], weight[...]).astype(BF16)

            tiles(store)
            swap_back(step).start()
            settle()
            pump(1)

        task(loads, run)

    def wait_task(fn, keep):
        def run(bufs):
            settle()
            drain(keep)
            fn()

        task([], run)

    def out_task(step):
        loads = [top(leaving, step), bot(leaving, step)]
        last = step == levels - 1
        if step == 0:
            loads.append(mixed)
        if last:
            loads.append(z[0])

        def run(bufs):
            held = bufs[2] if step == 0 else outs.at[step - 1]
            mate = mates.at[step]

            def store(at):
                total = dot(held[at, :], bufs[0][...]) + dot(mate[at, :], bufs[1][...])
                if last:
                    total = (bufs[-1][at, :].astype(F32) + total).astype(BF16)
                    layer_out[at, :] = dot(order[...], total).astype(BF16)
                else:
                    outs[step, at, :] = total.astype(BF16)

            tiles(store)
            if not last:
                swap_out(step + 1, outs.at[step]).start()
            settle()
            pump(1)

        task(loads, run)

    def back_task(step):
        down = levels - 1 - step
        last = step == levels - 1
        loads = [top(entering, down)]
        if step == 0:
            loads.append(drive_grad)
        if last:
            loads += [gate_pre, switch, e[levels]]

        def run(bufs):
            cot = bufs[1] if step == 0 else cots.at[step - 1]

            def store(at):
                total = dot_trans(cot[at, :], bufs[0][...]) + shares[step, at, :].astype(F32)
                if last:
                    total = total + dot_trans(bufs[-3][at, :], bufs[-2][...])
                    total = total + bufs[-1][at, :].astype(F32)
                    token_grads[at, :] = dot(order[...], total.astype(BF16)).astype(BF16)
                else:
                    cots[step, at, :] = total.astype(BF16)

            tiles(store)
            settle()
            pump(1)

        task(loads, run)

    gate_task()
    share_task(0)
    for step in range(levels):
        down = levels - 1 - step
        g = 1 + 2 * step
        cot = hbm(drive_grad) if step == 0 else cots.at[step - 1]
        held = hbm(mixed) if step == 0 else outs.at[step - 1]
        grad_task(g, 0, hbm(z[down]), cot, False)
        grad_task(g, half, hbm(zm[down]), cot, True)
        grad_task(g + 1, 0, held, hbm(e[step + 1]), False)
        wait_task(lambda step=step: swap_out(step, mixed).wait_recv(), 3)
        grad_task(g + 1, half, mates.at[step], hbm(e[step + 1]), True)
        out_task(step)
        wait_task(lambda step=step: swap_back(step).wait_recv(), 1 << 20)
        back_task(step)
        if step < levels - 1:
            share_task(step + 1)

    spans, count = [], 0
    for loads, _ in work:
        spans.append((count, count + len(loads)))
        count += len(loads)
    flat = [ref for loads, _ in work for ref in loads]
    owner = [t for t, (loads, _) in enumerate(work) for _ in loads]

    def load(n):
        rows = flat[n].shape[0]
        return pltpu.make_async_copy(
            flat[n], stage.at[n % SLOTS, pl.ds(0, rows)], load_sem.at[n % SLOTS]
        )

    ahead = 0
    while ahead < min(SLOTS, count):
        load(ahead).start()
        ahead += 1
    order[...] = swapped()

    barrier = pltpu.get_barrier_semaphore()

    def greet(device):
        pl.semaphore_signal(barrier, inc=1, device_id=device, device_id_type=MESH)

    for level in range(levels):
        greet(partner(level))
    greet(sibling)

    for device in (lax.rem(seq + 2, 2 * chips), lax.rem(seq + 2 * chips - 2, 2 * chips)):
        greet({"seq": device})
    pl.semaphore_wait(barrier, levels + 3)
    swap_out(0, mixed).start()
    for t, (loads, run) in enumerate(work):
        while ahead < count and (ahead < SLOTS or owner[ahead - SLOTS] < t):
            load(ahead).start()
            ahead += 1
        first, last = spans[t]
        for n in range(first, last):
            load(n).wait()
        run([stage.at[n % SLOTS, pl.ds(0, flat[n].shape[0])] for n in range(first, last)])
    settle()
    last = len(groups) - 1
    drain(pieces * (chips - 1))
    for g in range(last):
        finish_sends(g)
    drain(0)
    finish_sends(last)
    for b in (len(blocks) - 2, len(blocks) - 1):
        sibling_copy(b).wait_send()
    for step in range(levels):
        swap_out(step, mixed).wait_send()
    swap_back(levels - 1).wait_send()


def after_scan(z, z_mates, e, mixed, gate_pre, drive_grad, entering, leaving, switch, scale):
    levels = len(z)
    tokens, width = mixed.shape
    seq = lax.axis_size("seq")
    chips = seq // 2
    groups, blocks = 1 + 2 * levels, 1 + 4 * levels + max(width // 256, 1)
    rows = 2 * width // seq
    hops = groups * (chips - 1) * min(PIECES, width // LANES)
    hbm = pl.BlockSpec(memory_space=pl.ANY)
    dma = pltpu.SemaphoreType.DMA
    args = [*z, *z_mates, *e, mixed, gate_pre, drive_grad, entering, leaving, switch]
    square = width * width
    count = 2 * tokens * square * (4 * levels + 1 + 4 * levels + 1)
    results = pl.pallas_call(
        functools.partial(after_kernel, levels, chips, scale),
        in_specs=[hbm] * len(args),
        out_specs=[pl.BlockSpec(memory_space=pltpu.VMEM)] * 5,
        out_shape=[
            pltpu.VMEM((tokens, width), BF16),
            pltpu.VMEM((tokens, width), BF16),
            pltpu.VMEM((levels, rows, width), F32),
            pltpu.VMEM((levels, rows, width), F32),
            pltpu.VMEM((rows // 2, width), F32),
        ],
        scratch_shapes=[
            pltpu.VMEM((SLOTS, max(tokens, width), width), BF16),
            pltpu.VMEM((2, 2, width // 2, width), BF16),
            pltpu.VMEM((2 * levels, width, width), BF16),
            pltpu.VMEM((width // 2, width), BF16),
            pltpu.VMEM((2 * levels, chips - 1, rows, width), BF16),
            pltpu.VMEM((2 * levels, chips - 1, rows, width), BF16),
            pltpu.VMEM((chips - 1, rows // 2, width), BF16),
            pltpu.VMEM((chips - 1, rows // 2, width), BF16),
            pltpu.VMEM((levels, tokens, width), BF16),
            pltpu.VMEM((levels, tokens, width), BF16),
            pltpu.VMEM((levels - 1, tokens, width), BF16),
            pltpu.VMEM((levels - 1, tokens, width), BF16),
            pltpu.VMEM((tokens, width), BF16),
            pltpu.VMEM((CHUNK, CHUNK), BF16),
            dma((SLOTS,)), dma((blocks,)), dma((blocks,)),
            dma((hops,)), dma((hops,)), dma((hops,)), dma((hops,)),
            dma((2 * levels,)), dma((2 * levels,)),
        ],
        compiler_params=pltpu.CompilerParams(
            collective_id=0, has_side_effects=True, vmem_limit_bytes=52 << 20
        ),
        cost_estimate=pl.CostEstimate(
            flops=count, bytes_accessed=60 * tokens * width, transcendentals=0
        ),
        name="after_scan",
    )(*args)
    return pl.pallas_call(
        hand_over,
        in_specs=[pl.BlockSpec(memory_space=pltpu.VMEM)] * 5,
        out_specs=[hbm] * 5,
        out_shape=[jax.ShapeDtypeStruct(r.shape, r.dtype) for r in results],
        scratch_shapes=[dma((5,))],
        compiler_params=pltpu.CompilerParams(vmem_limit_bytes=1 << 20),
        name="hand_over",
    )(*results)


def hand_over(*refs):
    copies = [
        pltpu.make_async_copy(refs[n], refs[5 + n], refs[10].at[n]) for n in range(5)
    ]
    for copy in copies:
        copy.start()
    for copy in copies:
        copy.wait()


def shards(
    layer_source,
    entering,
    switch,
    leaving,
    channel_persistence,
    position_boosts,
    result_cotangent,
):
    scale = float(layer_source.shape[0] * lax.axis_size("seq")) ** (-0.5)
    z, z_mates, e, mixed, gate_pre_grad, drive_grad = before_scan(
        layer_source, result_cotangent, entering, leaving, switch,
        channel_persistence, position_boosts,
    )
    return after_scan(
        z, z_mates, e, mixed, gate_pre_grad, drive_grad, entering, leaving, switch, scale
    )


def solution(mesh):
    placed = (
        P("seq", "chan"),
        P(None, "chan", None),
        P("chan", None),
        P(None, "chan", None),
        P("chan"),
        P("seq"),
        P("seq", "chan"),
    )
    return jax.shard_map(
        shards,
        mesh=mesh,
        in_specs=placed,
        out_specs=(
            P("seq", "chan"),
            P("seq", "chan"),
            P(None, ("chan", "seq"), None),
            P(None, ("chan", "seq"), None),
            P(("chan", "seq"), None),
        ),
        check_vma=False,
    )
```
